512 devices in a mesh: slab: 64 (over x, z, y_lo), cross: 8 (over y_hi, core).
Axes of the slice: x: 4, y: 8 (y_hi: 4, y_lo: 2; y = y_hi * 2 + y_lo), z: 8, core: 2. Of those that a mesh axis runs over, the one named last changes fastest.
Arguments:
- adjoint_source: float32 [384, 48, 384], P('slab', 'cross'), may hold values from -24 to 24
- potential: float32 [384, 48, 384], P('slab', 'cross'), may hold values from -6 to 6
- element_matrix: float32 [64, 64], replicated
- region_labels: int32 [128, 16, 128], P('slab', 'cross'), may hold values from 0 to 3
- conductivity: float32 [4], replicated, may hold values from 0.3 to 3
- restriction_map: int32 [384, 48, 384], P('slab', 'cross'), may hold values from 0 to 7
Outputs:
- solution: float32 [384, 48, 384], P('slab', 'cross')
- residual: float32 [384, 48, 384], P('slab', 'cross')
The draws below stay inside these ranges and needn't reach their ends.
All inputs are finite; a program needn't handle non-finite values.
Results may differ from the reference program's by a relative error of at most 0.0025.
Values sent between devices are 32-bit elements; how exact they have to be, the bound alone decides.
No kernel may reach another device: no remote copies, remote signals or barrier semaphores. Data moves between devices by JAX's collectives and lax.ppermute only.
A program may use at most 128 MiB of HBM per device.

```python
import math
import jax
import jax.numpy as jnp
from jax import lax

EX = 2
EY = 2
EZ = 128
ELEM_NODES = 64
REGIONS = 4
ZB = 64
LABELS = 8
ITERS = 2
SWEEPS = 4
NC = 512
MX = 128
MY = 16
GX = 384
GY = 48
GZ = 384
N_SLAB = 64
N_CROSS = 8


def draw_element_matrix(key, part):
    key = jax.random.fold_in(key, 7)
    first, second = jax.random.split(key)
    diagonal = jax.random.uniform(second, (ELEM_NODES,), jnp.float32, 3.0, 5.0)
    raw = jax.random.uniform(first, (ELEM_NODES, ELEM_NODES), jnp.float32, -0.045, 0.045)
    mirrored = 0.5 * (raw + raw.T)
    unit = jnp.eye(ELEM_NODES, dtype=jnp.float32)
    return mirrored * (1.0 - unit) + jnp.diag(diagonal)


def set_ends(result, stream_key, least, high):
    dims = result.shape
    place = [jax.random.randint(jax.random.fold_in(stream_key, axis), (), 0, dims[axis]) for axis in range(len(dims))]
    result = result.at[tuple(place)].set(least)
    longest = dims.index(max(dims))
    place[longest] = (place[longest] + 1) % dims[longest]
    return result.at[tuple(place)].set(high)


def shard_levels(stream_key, extent, cuts, least, high):
    def one(dim, shards_of):
        heights = jax.random.uniform(jax.random.fold_in(jax.random.fold_in(stream_key, 6), dim), (shards_of,), jnp.float32, least / len(cuts), high / len(cuts))
        return jnp.repeat(jnp.exp(heights), extent[dim] // shards_of).reshape((-1,) + (1,) * (len(extent) - dim - 1))

    gain = one(*cuts[0])
    for cut in cuts[1:]:
        gain = gain * one(*cut)
    return gain


def gaussian(key, shape, scale, bound, cuts=(), held_as=jnp.bfloat16):
    drawn = scale * jax.random.normal(key, shape, jnp.float32)
    if cuts:
        drawn = drawn * shard_levels(key, shape, cuts, -0.22, 0.18)
    return jnp.clip(drawn, -bound, bound).astype(held_as)


def setup_inputs(seed: int = 0) -> dict:
    arg_keys = jax.random.split(jax.random.key(seed), 7)
    adjoint_source = gaussian(arg_keys[0], (GX, GY, GZ), 4.0, 24.0, ((0, 64), (1, 8)), jnp.float32)
    potential = gaussian(arg_keys[1], (GX, GY, GZ), 1.0, 6.0, ((0, 64), (1, 8)), jnp.float32)
    element_matrix = draw_element_matrix(jax.random.fold_in(arg_keys[6], 71), 0)
    region_labels = set_ends(jax.random.randint(arg_keys[3], (MX, MY, EZ), 0, REGIONS), jax.random.fold_in(arg_keys[3], 1), 0, REGIONS - 1).astype(jnp.int32)
    conductivity = jnp.clip(jnp.exp(jax.random.uniform(arg_keys[4], (REGIONS,), jnp.float32, math.log(0.3), math.log(3.0))), 0.3, 3.0)
    restriction_map = set_ends(jax.random.randint(arg_keys[5], (GX, GY, GZ), 0, LABELS), jax.random.fold_in(arg_keys[5], 1), 0, LABELS - 1).astype(jnp.int32)
    return dict(adjoint_source=adjoint_source, potential=potential, element_matrix=element_matrix, region_labels=region_labels, conductivity=conductivity, restriction_map=restriction_map)


DAMPING = 0.8
COUPLING = 0.2
SHARE = 0.1

def unfold(field, axis):
    moved = jnp.moveaxis(field, axis, -1)
    count = (moved.shape[-1] - 1) // 3
    triples = moved[..., :3 * count].reshape(moved.shape[:-1] + (count, 3))
    parts = jnp.stack([triples[..., 0], triples[..., 1], triples[..., 2], moved[..., 3::3]], 0)
    return jnp.moveaxis(parts, -1, axis + 1)

def fold(stacked, axis):
    moved = jnp.moveaxis(stacked, axis + 1, -1)
    count = moved.shape[-1]
    merged = jnp.stack([moved[0], moved[1], moved[2]], -1).reshape(moved.shape[1:-1] + (3 * count,))
    widths = [(0, 0)] * (merged.ndim - 1) + [(0, 1)]
    merged = jnp.pad(merged, widths)
    merged = merged.at[..., 3::3].add(moved[3])
    return jnp.moveaxis(merged, -1, axis)

def to_elements(padded):
    blocks = unfold(unfold(unfold(padded, 0), 2), 4)
    return blocks.reshape((64,) + blocks.shape[3:])

def from_elements(values):
    blocks = values.reshape((4, 4, 4) + values.shape[1:])
    return fold(fold(fold(blocks, 4), 2), 0)

def element_apply(padded, stiffness, sigma):
    local = to_elements(padded)
    product = jnp.einsum('pq,qxyz->pxyz', stiffness, local, precision=lax.Precision.HIGHEST)
    return from_elements(product * sigma)

def conductance(labels, table):
    regions = jnp.arange(table.shape[0], dtype=jnp.int32)
    return lax.optimization_barrier(jnp.sum(jnp.where(labels[..., None] == regions, table, jnp.float32(0.0)), -1))

def ionic_term(potential):
    tangent = jnp.tanh(potential)
    return 1.0 + 2.0 * (1.0 - tangent * tangent)

def neighbours(values):
    widths = [(1, 1)] + [(0, 0)] * (values.ndim - 1)
    padded = jnp.pad(values, widths)
    slab_sum = padded[2:] + padded[:-2]
    widths = [(0, 0)] * (values.ndim - 1) + [(1, 1)]
    padded = jnp.pad(values, widths)
    return slab_sum + (padded[..., 2:] + padded[..., :-2])

def sweep_coarse(coarse_rhs, coarse_diag):
    scale = jnp.sqrt(coarse_diag)
    guess = DAMPING * coarse_rhs / coarse_diag
    for sweep in range(SWEEPS - 1):
        product = coarse_diag * guess - COUPLING * scale * neighbours(scale * guess)
        guess = guess + DAMPING * (coarse_rhs - product) / coarse_diag
    return guess + lax.optimization_barrier(jnp.sum(coarse_rhs, 0)) / lax.optimization_barrier(jnp.sum(coarse_diag, 0))

def reference(adjoint_source, potential, element_matrix, region_labels, conductivity, restriction_map):
    size_x, size_y, size_z = adjoint_source.shape
    sigma = conductance(region_labels, conductivity)
    ionic = ionic_term(potential)

    def operate(field):
        padded = jnp.pad(field, ((0, 1), (0, 1), (0, 1)))
        return element_apply(padded, element_matrix, sigma)[:size_x, :size_y, :size_z] + ionic * field
    corner = jnp.diagonal(element_matrix)[:, None, None, None] * sigma
    diagonal = from_elements(corner)[:size_x, :size_y, :size_z] + ionic
    slab_id = jnp.arange(size_x, dtype=jnp.int32) // (3 * EX)
    cross_id = jnp.arange(size_y, dtype=jnp.int32) // (3 * EY)
    block_id = jnp.arange(size_z, dtype=jnp.int32) // (size_z // ZB)
    owner = ((slab_id[:, None, None] * N_CROSS + cross_id[None, :, None]) * ZB + block_id[None, None, :]) * LABELS + restriction_map
    owner = owner.astype(jnp.int32)
    segments = N_SLAB * N_CROSS * NC

    def restrict(field):
        return jax.ops.segment_sum(field.ravel(), owner.ravel(), num_segments=segments).reshape(N_SLAB, N_CROSS, NC)
    coarse_diag = SHARE * restrict(diagonal)

    def precondition(field):
        smooth = sweep_coarse(restrict(field), coarse_diag)
        return field / diagonal + smooth.ravel()[owner]
    solution = jnp.zeros_like(adjoint_source)
    residual = adjoint_source
    search = precondition(residual)
    direction = search
    rz_now = jnp.sum(residual * search)
    for step in range(ITERS):
        image = operate(direction)
        alpha = rz_now / jnp.sum(direction * image)
        solution = solution + alpha * direction
        residual = residual - alpha * image
        if step + 1 < ITERS:
            search = precondition(residual)
            rz_next = jnp.sum(residual * search)
            direction = search + rz_next / rz_now * direction
            rz_now = rz_next
    return (solution, residual)
```

```python
import jax
import jax.numpy as jnp
from jax import lax
from jax.sharding import PartitionSpec as P

ZB = 64
LABELS = 8
ITERS = 2
SWEEPS = 4
NC = 512


DAMPING = 0.8
COUPLING = 0.2
SHARE = 0.1


def shifted(value, axis, steps):
    count = lax.axis_size(axis)
    leading, last = (max(0, -steps), min(count, count - steps))
    return lax.ppermute(value, axis, [(source, source + steps) for source in range(leading, last)])


def unfold(field, axis):
    moved = jnp.moveaxis(field, axis, -1)
    count = (moved.shape[-1] - 1) // 3
    triples = moved[..., : 3 * count].reshape(moved.shape[:-1] + (count, 3))
    parts = jnp.stack([triples[..., 0], triples[..., 1], triples[..., 2], moved[..., 3::3]], 0)
    return jnp.moveaxis(parts, -1, axis + 1)


def fold(stacked, axis):
    moved = jnp.moveaxis(stacked, axis + 1, -1)
    count = moved.shape[-1]
    merged = jnp.stack([moved[0], moved[1], moved[2]], -1).reshape(moved.shape[1:-1] + (3 * count,))
    widths = [(0, 0)] * (merged.ndim - 1) + [(0, 1)]
    merged = jnp.pad(merged, widths)
    merged = merged.at[..., 3::3].add(moved[3])
    return jnp.moveaxis(merged, -1, axis)


def to_elements(padded):
    blocks = unfold(unfold(unfold(padded, 0), 2), 4)
    return blocks.reshape((64,) + blocks.shape[3:])


def from_elements(values):
    blocks = values.reshape((4, 4, 4) + values.shape[1:])
    return fold(fold(fold(blocks, 4), 2), 0)


def element_apply(padded, stiffness, sigma):
    local = to_elements(padded)
    product = jnp.einsum("pq,qxyz->pxyz", stiffness, local, precision=lax.Precision.HIGHEST)
    return from_elements(product * sigma)


def conductance(labels, table):
    regions = jnp.arange(table.shape[0], dtype=jnp.int32)
    return jnp.sum(jnp.where(labels[..., None] == regions, table, jnp.float32(0.0)), -1)


def ionic_term(potential):
    tangent = jnp.tanh(potential)
    return 1.0 + 2.0 * (1.0 - tangent * tangent)


def sweep_coarse(coarse_rhs, coarse_diag):
    scale = jnp.sqrt(coarse_diag)
    guess = DAMPING * coarse_rhs / coarse_diag
    for sweep in range(SWEEPS - 1):
        widths = [(1, 1)] + [(0, 0)] * (guess.ndim - 1)
        weighted = scale * guess
        padded = jnp.pad(weighted, widths)
        beside_all = padded[2:] + padded[:-2]
        widths = [(0, 0)] * (guess.ndim - 1) + [(1, 1)]
        padded = jnp.pad(weighted, widths)
        beside_all = beside_all + (padded[..., 2:] + padded[..., :-2])
        product = coarse_diag * guess - COUPLING * scale * beside_all
        guess = guess + DAMPING * (coarse_rhs - product) / coarse_diag
    return guess + jnp.sum(coarse_rhs, 0) / jnp.sum(coarse_diag, 0)


def body(adjoint_source, potential, element_matrix, region_labels, conductivity, restriction_map):
    rows_x, rows_y, depth = adjoint_source.shape
    sigma = conductance(region_labels, conductivity)
    ionic = ionic_term(potential)
    corner_values = jnp.diagonal(element_matrix)[:, None, None, None]

    def assemble(full):
        trimmed = full[:, :, :depth]
        arriving = shifted(trimmed[:, rows_y:], "cross", 1)
        trimmed = trimmed[:, :rows_y].at[:, 0:1].add(arriving)
        coming = shifted(trimmed[rows_x:], "slab", 1)
        return trimmed[:rows_x].at[0:1].add(coming)

    diagonal = assemble(from_elements(corner_values * sigma)) + ionic
    label_range = jnp.arange(LABELS, dtype=jnp.int32)
    member = (restriction_map[None] == label_range[:, None, None, None]).astype(jnp.float32)
    span = depth // ZB

    def restrict(field):
        sums = jnp.sum((member * field).reshape(LABELS, rows_x * rows_y, ZB, span), axis=(1, 3))
        return sums.T.reshape(NC)

    def prolong(coarse):
        table = jnp.repeat(coarse.reshape(ZB, LABELS).T, span, axis=1)
        return jnp.sum(member * table[:, None, None, :], 0)

    coarse_diag = SHARE * restrict(diagonal)
    n_slab = lax.axis_size("slab")
    n_cross = lax.axis_size("cross")
    position = lax.axis_index("slab")

    def share_slab(values):
        tile = jnp.pad(values, (0, 1024 - values.shape[0])).reshape(1, 8, 128)
        copies = jnp.broadcast_to(tile, (n_slab, 8, 128))
        return lax.all_to_all(copies, "slab", 0, 0, tiled=True).reshape(n_slab, 1024)

    def coarse_solve(rhs_all):
        smooth_all = sweep_coarse(rhs_all, diag_all)
        return lax.dynamic_slice_in_dim(smooth_all, position, 1, 0)[0]

    def operate(direction):
        upper = shifted(direction[0:1], "slab", -1)
        grown = jnp.concatenate([direction, upper], 0)
        side = shifted(grown[:, 0:1], "cross", -1)
        grown = jnp.concatenate([grown, side], 1)
        return (
            assemble(element_apply(jnp.pad(grown, ((0, 0), (0, 0), (0, 1))), element_matrix, sigma))
            + ionic * direction
        )

    first = share_slab(jnp.concatenate([restrict(adjoint_source), coarse_diag]))
    rhs_all, diag_all = first[:, :NC], first[:, NC:]
    search0 = adjoint_source / diagonal + prolong(coarse_solve(rhs_all))
    image0 = operate(search0)
    dots = jnp.stack([jnp.sum(adjoint_source * search0), jnp.sum(search0 * image0)])
    second = share_slab(jnp.concatenate([restrict(image0), dots]))
    rz0, pq0 = lax.psum(jnp.sum(second[:, NC : NC + 2], 0), "cross")
    alpha0 = rz0 / pq0
    residual1 = adjoint_source - alpha0 * image0
    search1 = residual1 / diagonal + prolong(coarse_solve(rhs_all - alpha0 * second[:, :NC]))
    image1 = operate(search1)
    dots = jnp.stack(
        [
            jnp.sum(residual1 * search1),
            jnp.sum(search1 * image1),
            jnp.sum(search1 * image0) + jnp.sum(search0 * image1),
        ]
    )
    line = jnp.pad(dots, (0, 125)).reshape(1, 128)
    total = line
    for step in range(1, n_cross):
        pairs = [(source, (source + step) % n_cross) for source in range(n_cross)]
        total = total + lax.ppermute(line, "cross", pairs)
    copies = jnp.broadcast_to(total[None], (n_slab, 1, 128))
    total = jnp.sum(lax.all_to_all(copies, "slab", 0, 0, tiled=True), (0, 1))
    rz1, own, mixed = total[0], total[1], total[2]
    beta = rz1 / rz0
    alpha1 = rz1 / (own + beta * mixed + beta * beta * pq0)
    answer = alpha0 * search0 + alpha1 * (search1 + beta * search0)
    residual2 = residual1 - alpha1 * (image1 + beta * image0)
    return (answer, residual2)


def solution(mesh):
    return jax.shard_map(
        body,
        mesh=mesh,
        in_specs=(
            P("slab", "cross", None),
            P("slab", "cross", None),
            P(),
            P("slab", "cross", None),
            P(),
            P("slab", "cross", None),
        ),
        out_specs=(P("slab", "cross", None), P("slab", "cross", None)),
        check_vma=False,
    )
```

```python
import functools

import jax
import jax.numpy as jnp
from jax import lax
from jax.experimental import pallas as pl
from jax.experimental.pallas import tpu as pltpu
from jax.sharding import PartitionSpec as P

LABELS = 8
DAMPING = 0.8
COUPLING = 0.2
SHARE = 0.1
REACH = 3
INNER = 8


F32 = jnp.float32
BF16 = jnp.bfloat16
SPAN = (-1, 0, 1)


def lanes(shape):
    return lax.broadcasted_iota(jnp.int32, shape, len(shape) - 1)


def call(kernel, out_shapes, scratch, *operands, smem=()):
    specs = [
        pl.BlockSpec(memory_space=pltpu.SMEM if index in smem else pltpu.VMEM) for index in range(len(operands))
    ]
    return pl.pallas_call(
        kernel,
        out_shape=[jax.ShapeDtypeStruct(shape, F32) for shape in out_shapes],
        in_specs=specs,
        out_specs=[pl.BlockSpec(memory_space=pltpu.VMEM)] * len(out_shapes),
        scratch_shapes=[pltpu.VMEM(shape, F32) for shape in scratch],
        compiler_params=pltpu.CompilerParams(vmem_limit_bytes=24 << 20),
    )(*operands)


def restrict(field, labels):
    rows = []
    for label in range(LABELS):
        kept = jnp.sum(jnp.where(labels == float(label), field, 0.0), axis=0)
        rows.append(jnp.sum(kept, axis=0, keepdims=True))
    sums = jnp.concatenate(rows, 0)
    even = lanes((8, 128)) % 2 == 0
    return sums + jnp.where(even, pltpu.roll(sums, 127, 1), pltpu.roll(sums, 1, 1))


def prolong(coarse, labels):
    field = jnp.zeros_like(labels)
    for label in range(LABELS):
        field = jnp.where(labels == float(label), coarse[label : label + 1, :][None], field)
    return field


def assemble(product_of, total_ref):
    total_ref[...] = jnp.zeros_like(total_ref)
    start = lanes((16, 128)) == 0
    for i in SPAN:
        low_a, high_a = {-1: (3, 4), 0: (0, 4), 1: (0, 3)}[i]
        for j in SPAN:
            product = product_of((i + 1) * 3 + j + 1)
            last = pltpu.roll(product[48:64], 1, 1)
            pieces = [
                product[0:16] + jnp.where(start, 0.0, last),
                product[16:32],
                product[32:48],
            ]
            for c in range(3):
                for b in range(4):
                    y = 3 * j + b
                    if 0 <= y < 6:
                        x = 3 * i + low_a
                        rows = pieces[c][4 * b + low_a : 4 * b + high_a]
                        total_ref[c * 6 + y, x : x + high_a - low_a, :] += rows


def unpack_kernel(source_ref, potential_ref, map_ref, r_ref, ionic_ref, label_ref, coarse_ref, rows_ref, turned_ref):
    rows_ref[...] = jnp.zeros_like(rows_ref)
    for y in range(6):
        for x in range(6):
            row = y * 6 + x
            rows_ref[row : row + 1, :] = source_ref[x, y : y + 1, :]
            rows_ref[36 + row : 37 + row, :] = potential_ref[x, y : y + 1, :]
            rows_ref[72 + row : 73 + row, :] = map_ref[x, y : y + 1, :].astype(F32)
    for piece in range(3):
        turned_ref[128 * piece : 128 * piece + 128, :] = rows_ref[:, 128 * piece : 128 * piece + 128].T
    r_ref[...] = jnp.zeros_like(r_ref)
    ionic_ref[...] = jnp.zeros_like(ionic_ref)
    label_ref[...] = jnp.full_like(label_ref, -1.0)
    for c in range(3):
        split = turned_ref[pl.ds(c, 128, stride=3), :].T
        for y in range(6):
            r_ref[c * 6 + y, 0:6, :] = split[6 * y : 6 * y + 6]
            tangent = jnp.tanh(split[36 + 6 * y : 42 + 6 * y])
            ionic_ref[c * 6 + y, 0:6, :] = 1.0 + 2.0 * (1.0 - tangent * tangent)
            label_ref[c * 6 + y, 0:6, :] = split[72 + 6 * y : 78 + 6 * y]
    coarse_ref[...] = restrict(r_ref[...], label_ref[...])


def diagonal_kernel(own_ref, beside_ref, below_ref, table_ref, matrix_ref, ionic_ref, label_ref, coarse_ref,
                    sigma_ref, diagonal_ref, message_ref, total_ref):
    def conductance(region):
        value = jnp.zeros(region.shape, F32)
        for index in range(4):
            value = jnp.where(region == index + 1, table_ref[index], value)
        return value

    sigma_ref[0:3, :] = conductance(below_ref[...])
    for i in range(2):
        sigma_ref[3 + 3 * i : 4 + 3 * i, :] = conductance(beside_ref[i : i + 1, :])
        sigma_ref[4 + 3 * i : 6 + 3 * i, :] = conductance(own_ref[i] + 1)
    square = (64, 64)
    eye = lax.broadcasted_iota(jnp.int32, square, 0) == lax.broadcasted_iota(jnp.int32, square, 1)
    corner = jnp.sum(jnp.where(eye, matrix_ref[...], 0.0), axis=1, keepdims=True)
    assemble(lambda e: corner * sigma_ref[e : e + 1, :], total_ref)
    labels = label_ref[...]
    diagonal = jnp.where(labels < 0.0, 1.0, total_ref[...] + ionic_ref[...])
    diagonal_ref[...] = diagonal
    coarse_diag = SHARE * restrict(diagonal, labels)
    even = lanes((8, 128)) % 2 == 0
    message = jnp.where(even, coarse_ref[...], coarse_diag)
    message_ref[...] = jnp.broadcast_to(message[None], message_ref.shape)


def along(values):
    lane = lanes(values.shape)
    row = lax.broadcasted_iota(jnp.int32, values.shape, 1)
    after = pltpu.roll(values, 7, 1)
    carried = jnp.where(lane < 126, pltpu.roll(after, 126, 2), 0.0)
    after = jnp.where(row == 7, carried, after)
    before = pltpu.roll(values, 1, 1)
    carried = jnp.where(lane >= 2, pltpu.roll(before, 2, 2), 0.0)
    return after + jnp.where(row == 0, carried, before)


def smooth(start, valid):
    level = start
    for sweep in range(REACH):
        beside = level[2:] + level[:-2] + along(level[1:-1])
        here = slice(sweep + 1, 2 * REACH - sweep)
        level = start[here] + (1.0 - DAMPING) * level[1:-1] + (DAMPING * COUPLING) * beside
        level = level * valid[here]
    return level[0]


def around(place_ref, count):
    rows, valid = [], []
    for step in range(-REACH, REACH + 1):
        row = place_ref[0] + step
        inside = jnp.logical_and(row >= 0, row < count)
        rows.append(jnp.clip(row, 0, count - 1))
        valid.append(jnp.where(inside, jnp.ones((1, 8, 128), F32), 0.0))
    return rows, jnp.concatenate(valid, 0)


def even_part(tiles):
    even = lanes(tiles.shape) % 2 == 0
    return jnp.where(even, tiles, pltpu.roll(tiles, 1, tiles.ndim - 1))


def odd_part(tiles):
    even = lanes(tiles.shape) % 2 == 0
    return jnp.where(even, pltpu.roll(tiles, 127, tiles.ndim - 1), tiles)


def send_cross(field_ref, up_ref, down_ref):
    for c in range(3):
        up_ref[3 * c : 3 * c + 3] = field_ref[6 * c + 3 : 6 * c + 6]
        down_ref[c : c + 1] = field_ref[6 * c : 6 * c + 1]


def first_solve_kernel(place_ref, gathered_ref, r_ref, diagonal_ref, label_ref, z_ref, up_ref, down_ref, scale_ref):
    count = gathered_ref.shape[0]
    rows, valid = around(place_ref, count)
    near = jnp.concatenate([gathered_ref[pl.ds(row, 1)] for row in rows], 0)
    sums = jnp.sum(gathered_ref[...], axis=0)
    inverse = valid / jnp.sqrt(odd_part(near))
    share = 1.0 / odd_part(sums)
    scale_ref[0 : 2 * REACH + 1] = inverse
    scale_ref[2 * REACH + 1] = share
    level = smooth(DAMPING * even_part(near) * inverse, valid)
    coarse = level * inverse[REACH] + even_part(sums) * share
    z_ref[...] = r_ref[...] / diagonal_ref[...] + prolong(coarse, label_ref[...])
    send_cross(z_ref, up_ref, down_ref)


def next_solve_kernel(place_ref, gathered_ref, q_ref, diagonal_ref, label_ref, scale_ref, w_ref, up_ref, down_ref):
    rows, valid = around(place_ref, gathered_ref.shape[0])
    near = jnp.concatenate([gathered_ref[pl.ds(row, 1)] for row in rows], 0)
    sums = jnp.sum(gathered_ref[...], axis=0)
    inverse = scale_ref[0 : 2 * REACH + 1]
    level = smooth(DAMPING * near * inverse, valid)
    coarse = level * inverse[REACH] + sums * scale_ref[2 * REACH + 1]
    w_ref[...] = q_ref[...] / diagonal_ref[...] + prolong(coarse, label_ref[...])
    send_cross(w_ref, up_ref, down_ref)


def send_slab_kernel(field_ref, above_ref, under_ref, up_ref, down_ref):
    up_ref[90:96, :] = jnp.zeros((6, 128), F32)
    down_ref[30:32, :] = jnp.zeros((2, 128), F32)
    for c in range(3):
        for y in range(10):
            if y < 3:
                tile = above_ref[3 * c + y]
            elif y < 9:
                tile = field_ref[6 * c + y - 3]
            else:
                tile = under_ref[c]
            n = c * 10 + y
            up_ref[3 * n : 3 * n + 3, :] = tile[3:6]
            down_ref[n : n + 1, :] = tile[0:1]


def operate(field_ref, above_ref, under_ref, low_ref, high_ref, sigma_ref, matrix_ref, ionic_ref,
            grid_ref, local_ref, product_ref, total_ref):
    for c in range(3):
        for y in range(10):
            n = c * 10 + y
            if y < 3:
                tile = above_ref[3 * c + y]
            elif y < 9:
                tile = field_ref[6 * c + y - 3]
            else:
                tile = under_ref[c]
            grid_ref[n, 3:9, :] = tile[0:6]
            grid_ref[n, 0:3, :] = low_ref[3 * n : 3 * n + 3, :]
            grid_ref[n, 9:10, :] = high_ref[n : n + 1, :]
    end = lanes((10, 128)) == 127
    for y in range(10):
        grid_ref[30 + y, 0:10, :] = jnp.where(end, 0.0, pltpu.roll(grid_ref[y, 0:10, :], 127, 1))
    for i in SPAN:
        for j in SPAN:
            left = ((i + 1) * 3 + j + 1) * 128
            for c in range(4):
                for b in range(4):
                    row = 16 * c + 4 * b
                    n = c * 10 + 3 * (j + 1) + b
                    local_ref[row : row + 4, left : left + 128] = grid_ref[n, 3 * i + 3 : 3 * i + 7, :]
    matrix = matrix_ref[...]
    matrix_high = matrix.astype(BF16)
    matrix_low = (matrix - matrix_high.astype(F32)).astype(BF16)
    local = local_ref[...]
    high = local.astype(BF16)
    low = (local - high.astype(F32)).astype(BF16)
    dot = functools.partial(jnp.dot, preferred_element_type=F32)
    product_ref[...] = dot(matrix_high, high) + (dot(matrix_high, low) + dot(matrix_low, high))
    assemble(lambda e: product_ref[:, 128 * e : 128 * e + 128] * sigma_ref[e : e + 1, :], total_ref)
    return total_ref[...] + ionic_ref[...] * field_ref[...]


def first_image_kernel(z_ref, above_ref, under_ref, low_ref, high_ref, sigma_ref, matrix_ref, ionic_ref, label_ref,
                       q_ref, message_ref, *scratch):
    image = operate(z_ref, above_ref, under_ref, low_ref, high_ref, sigma_ref, matrix_ref, ionic_ref, *scratch)
    q_ref[...] = image
    message_ref[...] = jnp.broadcast_to(restrict(image, label_ref[...])[None], message_ref.shape)


def next_image_kernel(w_ref, above_ref, under_ref, low_ref, high_ref, sigma_ref, matrix_ref, ionic_ref,
                      r_ref, z_ref, q_ref, t_ref, message_ref, *scratch):
    image = operate(w_ref, above_ref, under_ref, low_ref, high_ref, sigma_ref, matrix_ref, ionic_ref, *scratch)
    t_ref[...] = image
    r, z, q, w = r_ref[...], z_ref[...], q_ref[...], w_ref[...]
    rows = []
    for left, right in ((r, z), (z, q), (r, w), (q, w), (z, image), (w, image)):
        rows.append(jnp.sum(jnp.sum(left * right, axis=0), axis=0, keepdims=True))
    rows.append(jnp.zeros((2, 128), F32))
    message_ref[...] = jnp.broadcast_to(jnp.concatenate(rows, 0)[None], message_ref.shape)


def finish_kernel(dots_ref, r_ref, z_ref, q_ref, w_ref, t_ref, solution_ref, residual_ref, rows_ref, turned_ref):
    dots = jnp.sum(jnp.sum(dots_ref[...], axis=0), axis=1, keepdims=True)
    rz, zq, rw, qw, zt, wt = [dots[index : index + 1] for index in range(6)]
    alpha = rz / zq
    rz_next = alpha * (alpha * qw - rw)
    beta = rz_next / rz
    more = 1.0 + beta
    second = rz_next / (more * more * zq - more * alpha * (zt + qw) + alpha * alpha * wt)
    from_z = alpha + second * more
    from_w = second * alpha
    rows_ref[...] = jnp.zeros_like(rows_ref)
    for c in range(3):
        for y in range(6):
            n = 6 * c + y
            answer = from_z * z_ref[n] - from_w * w_ref[n]
            left = r_ref[n] - from_z * q_ref[n] + from_w * t_ref[n]
            rows_ref[6 * y : 6 * y + 6, :] = answer[0:6]
            rows_ref[36 + 6 * y : 42 + 6 * y, :] = left[0:6]
        turned_ref[pl.ds(c, 128, stride=3), :] = rows_ref[...].T
    for piece in range(3):
        back = turned_ref[128 * piece : 128 * piece + 128, :].T
        for y in range(6):
            for x in range(6):
                row = y * 6 + x
                solution_ref[x, y : y + 1, 128 * piece : 128 * piece + 128] = back[row : row + 1]
                residual_ref[x, y : y + 1, 128 * piece : 128 * piece + 128] = back[36 + row : 37 + row]


def body(adjoint_source, potential, element_matrix, region_labels, conductivity, restriction_map):
    n_slab = lax.axis_size("slab")
    n_cross = lax.axis_size("cross")
    outer = n_slab // INNER
    place = lax.axis_index("slab").astype(jnp.int32).reshape(1)
    inner_groups = [[block * INNER + k for k in range(INNER)] for block in range(outer)]
    outer_groups = [[block * INNER + k for block in range(outer)] for k in range(INNER)]

    def shifted(value, axis, step):
        count = lax.axis_size(axis)
        pairs = [(source, source + step) for source in range(count) if 0 <= source + step < count]
        return lax.ppermute(value, axis, pairs)

    def gather(copies):
        block = lax.all_to_all(copies, "slab", 0, 0, axis_index_groups=inner_groups, tiled=True)
        copies = jnp.broadcast_to(block[None], (outer,) + block.shape)
        everything = lax.all_to_all(copies, "slab", 0, 0, axis_index_groups=outer_groups, tiled=True)
        return everything.reshape(n_slab, 8, 128)

    def add_up(copies):
        total = lax.all_to_all(copies, "slab", 0, 0, axis_index_groups=inner_groups, tiled=True).sum(0)
        copies = jnp.broadcast_to(total[None], (outer, 8, 128))
        total = lax.all_to_all(copies, "slab", 0, 0, axis_index_groups=outer_groups, tiled=True).sum(0)
        copies = jnp.broadcast_to(total[None], (n_cross, 8, 128))
        return lax.all_to_all(copies, "cross", 0, 0, tiled=True)

    field, above, under = (18, 8, 128), (9, 8, 128), (3, 8, 128)
    space = [(40, 16, 128), (64, 1152), (64, 1152), field]
    beside = shifted(region_labels[:, 1] + 1, "cross", 1)
    below = shifted(jnp.concatenate([beside[1:2], region_labels[1] + 1], 0), "slab", 1)
    r, ionic, labels, coarse = call(
        unpack_kernel, [field] * 3 + [(8, 128)], [(128, 384), (384, 128)], adjoint_source, potential, restriction_map
    )
    sigma, diagonal, message = call(
        diagonal_kernel, [(9, 128), field, (INNER, 8, 128)], [field],
        region_labels, beside, below, conductivity, element_matrix, ionic, labels, coarse, smem=(3,),
    )

    def with_halo(value, up, down):
        over = shifted(up, "cross", 1)
        low = shifted(down, "cross", -1)
        up, down = call(send_slab_kernel, [(96, 128), (32, 128)], [], value, over, low)
        return (value, over, low, shifted(up, "slab", 1), shifted(down, "slab", -1), sigma, element_matrix, ionic)

    z, up, down, scale = call(
        first_solve_kernel, [field, above, under, (8, 8, 128)], [], place, gather(message), r, diagonal, labels, smem=(0,)
    )
    q, message = call(first_image_kernel, [field, (INNER, 8, 128)], space, *with_halo(z, up, down), labels)
    w, up, down = call(
        next_solve_kernel, [field, above, under], [], place, gather(message), q, diagonal, labels, scale, smem=(0,)
    )
    t, message = call(next_image_kernel, [field, (INNER, 8, 128)], space, *with_halo(w, up, down), r, z, q)
    return tuple(
        call(finish_kernel, [(6, 6, 384)] * 2, [(128, 128), (384, 128)], add_up(message), r, z, q, w, t)
    )


def solution(mesh):
    return jax.shard_map(
        body,
        mesh=mesh,
        in_specs=(
            P("slab", "cross", None),
            P("slab", "cross", None),
            P(),
            P("slab", "cross", None),
            P(),
            P("slab", "cross", None),
        ),
        out_specs=(P("slab", "cross", None), P("slab", "cross", None)),
        check_vma=False,
    )
```

```python
import functools

import jax
import jax.numpy as jnp
from jax import lax
from jax.experimental import pallas as pl
from jax.experimental.pallas import tpu as pltpu
from jax.sharding import PartitionSpec as P

LABELS = 8
DAMPING = 0.8
COUPLING = 0.2
SHARE = 0.1
REACH = 3


F32 = jnp.float32
BF16 = jnp.bfloat16
SPAN = (-1, 0, 1)


def lanes(shape):
    return lax.broadcasted_iota(jnp.int32, shape, len(shape) - 1)


def call(kernel, out_shapes, scratch, *operands, smem=(), away=()):
    specs = [
        pl.BlockSpec(memory_space=pltpu.SMEM if index in smem else pl.ANY if index in away else pltpu.VMEM)
        for index in range(len(operands))
    ]
    return pl.pallas_call(
        kernel,
        out_shape=[jax.ShapeDtypeStruct(shape, F32) for shape in out_shapes],
        in_specs=specs,
        out_specs=[pl.BlockSpec(memory_space=pltpu.VMEM)] * len(out_shapes),
        scratch_shapes=[pltpu.VMEM(shape, F32) if isinstance(shape, tuple) else shape for shape in scratch],
        compiler_params=pltpu.CompilerParams(vmem_limit_bytes=24 << 20),
    )(*operands)


def restrict(field, labels):
    rows = []
    for label in range(LABELS):
        kept = jnp.sum(jnp.where(labels == float(label), field, 0.0), axis=0)
        rows.append(jnp.sum(kept, axis=0, keepdims=True))
    sums = jnp.concatenate(rows, 0)
    even = lanes((8, 128)) % 2 == 0
    return sums + jnp.where(even, pltpu.roll(sums, 127, 1), pltpu.roll(sums, 1, 1))


def prolong(coarse, labels):
    field = jnp.zeros_like(labels)
    for label in range(LABELS):
        field = jnp.where(labels == float(label), coarse[label : label + 1, :][None], field)
    return field


def assemble(product_of, total_ref):
    total_ref[...] = jnp.zeros_like(total_ref)
    start = lanes((16, 128)) == 0
    for i in SPAN:
        low_a, high_a = {-1: (3, 4), 0: (0, 4), 1: (0, 3)}[i]
        for j in SPAN:
            product = product_of((i + 1) * 3 + j + 1)
            last = pltpu.roll(product[48:64], 1, 1)
            pieces = [
                product[0:16] + jnp.where(start, 0.0, last),
                product[16:32],
                product[32:48],
            ]
            for c in range(3):
                for b in range(4):
                    y = 3 * j + b
                    if 0 <= y < 6:
                        x = 3 * i + low_a
                        rows = pieces[c][4 * b + low_a : 4 * b + high_a]
                        total_ref[c * 6 + y, x : x + high_a - low_a, :] += rows


def unpack_kernel(source_hbm, potential_hbm, map_hbm, r_ref, ionic_ref, label_ref, coarse_ref,
                  rows_ref, turned_ref, source_ref, potential_ref, map_ref, sems):
    copies = [
        pltpu.make_async_copy(away, here, sems.at[index])
        for index, (away, here) in enumerate(
            ((source_hbm, source_ref), (potential_hbm, potential_ref), (map_hbm, map_ref))
        )
    ]
    for copy in copies:
        copy.start()
    rows_ref[...] = jnp.zeros_like(rows_ref)
    for copy in copies:
        copy.wait()
    for y in range(6):
        for x in range(6):
            row = y * 6 + x
            rows_ref[row : row + 1, :] = source_ref[x, y : y + 1, :]
            rows_ref[36 + row : 37 + row, :] = potential_ref[x, y : y + 1, :]
            rows_ref[72 + row : 73 + row, :] = map_ref[x, y : y + 1, :].astype(F32)
    for piece in range(3):
        turned_ref[128 * piece : 128 * piece + 128, :] = rows_ref[:, 128 * piece : 128 * piece + 128].T
    r_ref[...] = jnp.zeros_like(r_ref)
    ionic_ref[...] = jnp.zeros_like(ionic_ref)
    label_ref[...] = jnp.full_like(label_ref, -1.0)
    for c in range(3):
        split = turned_ref[pl.ds(c, 128, stride=3), :].T
        for y in range(6):
            r_ref[c * 6 + y, 0:6, :] = split[6 * y : 6 * y + 6]
            tangent = jnp.tanh(split[36 + 6 * y : 42 + 6 * y])
            ionic_ref[c * 6 + y, 0:6, :] = 1.0 + 2.0 * (1.0 - tangent * tangent)
            label_ref[c * 6 + y, 0:6, :] = split[72 + 6 * y : 78 + 6 * y]
    coarse_ref[...] = restrict(r_ref[...], label_ref[...])


def diagonal_kernel(own_ref, beside_ref, below_ref, table_ref, matrix_ref, ionic_ref, label_ref, coarse_ref,
                    sigma_ref, diagonal_ref, message_ref, total_ref):
    def conductance(region):
        value = jnp.zeros(region.shape, F32)
        for index in range(4):
            value = jnp.where(region == index + 1, table_ref[index], value)
        return value

    sigma_ref[0:3, :] = conductance(below_ref[...])
    for i in range(2):
        sigma_ref[3 + 3 * i : 4 + 3 * i, :] = conductance(beside_ref[i : i + 1, :])
        sigma_ref[4 + 3 * i : 6 + 3 * i, :] = conductance(own_ref[i] + 1)
    square = (64, 64)
    eye = lax.broadcasted_iota(jnp.int32, square, 0) == lax.broadcasted_iota(jnp.int32, square, 1)
    corner = jnp.sum(jnp.where(eye, matrix_ref[...], 0.0), axis=1, keepdims=True)
    assemble(lambda e: corner * sigma_ref[e : e + 1, :], total_ref)
    labels = label_ref[...]
    diagonal = jnp.where(labels < 0.0, 1.0, total_ref[...] + ionic_ref[...])
    diagonal_ref[...] = diagonal
    coarse_diag = SHARE * restrict(diagonal, labels)
    even = lanes((8, 128)) % 2 == 0
    message = jnp.where(even, coarse_ref[...], coarse_diag)
    message_ref[...] = jnp.broadcast_to(message[None], message_ref.shape)


def along(values):
    lane = lanes(values.shape)
    row = lax.broadcasted_iota(jnp.int32, values.shape, 1)
    after = pltpu.roll(values, 7, 1)
    carried = jnp.where(lane < 126, pltpu.roll(after, 126, 2), 0.0)
    after = jnp.where(row == 7, carried, after)
    before = pltpu.roll(values, 1, 1)
    carried = jnp.where(lane >= 2, pltpu.roll(before, 2, 2), 0.0)
    return after + jnp.where(row == 0, carried, before)


def smooth(start, valid):
    level = start
    for sweep in range(REACH):
        beside = level[2:] + level[:-2] + along(level[1:-1])
        here = slice(sweep + 1, 2 * REACH - sweep)
        level = start[here] + (1.0 - DAMPING) * level[1:-1] + (DAMPING * COUPLING) * beside
        level = level * valid[here]
    return level[0]


def around(place_ref, count):
    rows, valid = [], []
    for step in range(-REACH, REACH + 1):
        row = place_ref[0] + step
        inside = jnp.logical_and(row >= 0, row < count)
        rows.append(jnp.clip(row, 0, count - 1))
        valid.append(jnp.where(inside, jnp.ones((1, 8, 128), F32), 0.0))
    return rows, jnp.concatenate(valid, 0)


def even_part(tiles):
    even = lanes(tiles.shape) % 2 == 0
    return jnp.where(even, tiles, pltpu.roll(tiles, 1, tiles.ndim - 1))


def odd_part(tiles):
    even = lanes(tiles.shape) % 2 == 0
    return jnp.where(even, pltpu.roll(tiles, 127, tiles.ndim - 1), tiles)


def send_cross(field_ref, up_ref, down_ref):
    for c in range(3):
        up_ref[3 * c : 3 * c + 3] = field_ref[6 * c + 3 : 6 * c + 6]
        down_ref[c : c + 1] = field_ref[6 * c : 6 * c + 1]


def first_solve_kernel(place_ref, gathered_ref, r_ref, diagonal_ref, label_ref, z_ref, up_ref, down_ref, scale_ref):
    count = gathered_ref.shape[0]
    rows, valid = around(place_ref, count)
    near = jnp.concatenate([gathered_ref[pl.ds(row, 1)] for row in rows], 0)
    sums = jnp.sum(gathered_ref[...], axis=0)
    inverse = valid / jnp.sqrt(odd_part(near))
    share = 1.0 / odd_part(sums)
    scale_ref[0 : 2 * REACH + 1] = inverse
    scale_ref[2 * REACH + 1] = share
    level = smooth(DAMPING * even_part(near) * inverse, valid)
    coarse = level * inverse[REACH] + even_part(sums) * share
    z_ref[...] = r_ref[...] / diagonal_ref[...] + prolong(coarse, label_ref[...])
    send_cross(z_ref, up_ref, down_ref)


def next_solve_kernel(place_ref, gathered_ref, q_ref, diagonal_ref, label_ref, scale_ref, w_ref, up_ref, down_ref):
    rows, valid = around(place_ref, gathered_ref.shape[0])
    near = jnp.concatenate([gathered_ref[pl.ds(row, 1)] for row in rows], 0)
    sums = jnp.sum(gathered_ref[...], axis=0)
    inverse = scale_ref[0 : 2 * REACH + 1]
    level = smooth(DAMPING * near * inverse, valid)
    coarse = level * inverse[REACH] + sums * scale_ref[2 * REACH + 1]
    w_ref[...] = q_ref[...] / diagonal_ref[...] + prolong(coarse, label_ref[...])
    send_cross(w_ref, up_ref, down_ref)


def send_slab_kernel(field_ref, above_ref, under_ref, up_ref, down_ref):
    up_ref[90:96, :] = jnp.zeros((6, 128), F32)
    down_ref[30:32, :] = jnp.zeros((2, 128), F32)
    for c in range(3):
        for y in range(10):
            if y < 3:
                tile = above_ref[3 * c + y]
            elif y < 9:
                tile = field_ref[6 * c + y - 3]
            else:
                tile = under_ref[c]
            n = c * 10 + y
            up_ref[3 * n : 3 * n + 3, :] = tile[3:6]
            down_ref[n : n + 1, :] = tile[0:1]


def operate(field_ref, above_ref, under_ref, low_ref, high_ref, sigma_ref, matrix_ref, ionic_ref,
            grid_ref, local_ref, product_ref, total_ref):
    for c in range(3):
        for y in range(10):
            n = c * 10 + y
            if y < 3:
                tile = above_ref[3 * c + y]
            elif y < 9:
                tile = field_ref[6 * c + y - 3]
            else:
                tile = under_ref[c]
            grid_ref[n, 3:9, :] = tile[0:6]
            grid_ref[n, 0:3, :] = low_ref[3 * n : 3 * n + 3, :]
            grid_ref[n, 9:10, :] = high_ref[n : n + 1, :]
    end = lanes((10, 128)) == 127
    for y in range(10):
        grid_ref[30 + y, 0:10, :] = jnp.where(end, 0.0, pltpu.roll(grid_ref[y, 0:10, :], 127, 1))
    for i in SPAN:
        for j in SPAN:
            left = ((i + 1) * 3 + j + 1) * 128
            for c in range(4):
                for b in range(4):
                    row = 16 * c + 4 * b
                    n = c * 10 + 3 * (j + 1) + b
                    local_ref[row : row + 4, left : left + 128] = grid_ref[n, 3 * i + 3 : 3 * i + 7, :]
    matrix = matrix_ref[...]
    matrix_high = matrix.astype(BF16)
    matrix_low = (matrix - matrix_high.astype(F32)).astype(BF16)
    local = local_ref[...]
    high = local.astype(BF16)
    low = (local - high.astype(F32)).astype(BF16)
    dot = functools.partial(jnp.dot, preferred_element_type=F32)
    product_ref[...] = dot(matrix_high, high) + (dot(matrix_high, low) + dot(matrix_low, high))
    assemble(lambda e: product_ref[:, 128 * e : 128 * e + 128] * sigma_ref[e : e + 1, :], total_ref)
    return total_ref[...] + ionic_ref[...] * field_ref[...]


def first_image_kernel(z_ref, above_ref, under_ref, low_ref, high_ref, sigma_ref, matrix_ref, ionic_ref, label_ref,
                       q_ref, message_ref, *scratch):
    image = operate(z_ref, above_ref, under_ref, low_ref, high_ref, sigma_ref, matrix_ref, ionic_ref, *scratch)
    q_ref[...] = image
    message_ref[...] = jnp.broadcast_to(restrict(image, label_ref[...])[None], message_ref.shape)


def next_image_kernel(w_ref, above_ref, under_ref, low_ref, high_ref, sigma_ref, matrix_ref, ionic_ref,
                      r_ref, z_ref, q_ref, t_ref, tile_ref, *scratch):
    image = operate(w_ref, above_ref, under_ref, low_ref, high_ref, sigma_ref, matrix_ref, ionic_ref, *scratch)
    t_ref[...] = image
    r, z, q, w = r_ref[...], z_ref[...], q_ref[...], w_ref[...]
    rows = []
    for left, right in ((r, z), (z, q), (r, w), (q, w), (z, image), (w, image)):
        rows.append(jnp.sum(jnp.sum(left * right, axis=0), axis=0, keepdims=True))
    rows.append(jnp.zeros((2, 128), F32))
    tile_ref[...] = jnp.concatenate(rows, 0)


def finish_kernel(dots_ref, r_ref, z_ref, q_ref, w_ref, t_ref, solution_ref, residual_ref, rows_ref, turned_ref):
    dots = jnp.sum(jnp.sum(dots_ref[...], axis=0), axis=1, keepdims=True)
    rz, zq, rw, qw, zt, wt = [dots[index : index + 1] for index in range(6)]
    alpha = rz / zq
    rz_next = alpha * (alpha * qw - rw)
    beta = rz_next / rz
    more = 1.0 + beta
    second = rz_next / (more * more * zq - more * alpha * (zt + qw) + alpha * alpha * wt)
    from_z = alpha + second * more
    from_w = second * alpha
    rows_ref[...] = jnp.zeros_like(rows_ref)
    for c in range(3):
        for y in range(6):
            n = 6 * c + y
            answer = from_z * z_ref[n] - from_w * w_ref[n]
            left = r_ref[n] - from_z * q_ref[n] + from_w * t_ref[n]
            rows_ref[6 * y : 6 * y + 6, :] = answer[0:6]
            rows_ref[36 + 6 * y : 42 + 6 * y, :] = left[0:6]
        turned_ref[pl.ds(c, 128, stride=3), :] = rows_ref[...].T
    for piece in range(3):
        back = turned_ref[128 * piece : 128 * piece + 128, :].T
        for y in range(6):
            for x in range(6):
                row = y * 6 + x
                solution_ref[x, y : y + 1, 128 * piece : 128 * piece + 128] = back[row : row + 1]
                residual_ref[x, y : y + 1, 128 * piece : 128 * piece + 128] = back[36 + row : 37 + row]


def body(adjoint_source, potential, element_matrix, region_labels, conductivity, restriction_map):
    n_slab = lax.axis_size("slab")
    n_cross = lax.axis_size("cross")
    place = lax.axis_index("slab").astype(jnp.int32).reshape(1)
    def shifted(value, axis, step):
        count = lax.axis_size(axis)
        pairs = [(source, source + step) for source in range(count) if 0 <= source + step < count]
        return lax.ppermute(value, axis, pairs)

    def gather(copies):
        return lax.all_to_all(copies, "slab", 0, 0, tiled=True)

    def add_up(tile):
        step = 1
        while step < n_cross:
            tile = tile + lax.ppermute(tile, "cross", [(source, source ^ step) for source in range(n_cross)])
            step *= 2
        return gather(jnp.broadcast_to(tile[None], (n_slab, 8, 128)))

    field, above, under = (18, 8, 128), (9, 8, 128), (3, 8, 128)
    space = [(40, 16, 128), (64, 1152), (64, 1152), field]
    beside = shifted(region_labels[:, 1] + 1, "cross", 1)
    below = shifted(jnp.concatenate([beside[1:2], region_labels[1] + 1], 0), "slab", 1)
    r, ionic, labels, coarse = call(
        unpack_kernel, [field] * 3 + [(8, 128)],
        [(128, 384), (384, 128), (6, 6, 384), (6, 6, 384), pltpu.VMEM((6, 6, 384), jnp.int32), pltpu.SemaphoreType.DMA((3,))],
        adjoint_source, potential, restriction_map, away=(0, 1, 2),
    )
    sigma, diagonal, message = call(
        diagonal_kernel, [(9, 128), field, (n_slab, 8, 128)], [field],
        region_labels, beside, below, conductivity, element_matrix, ionic, labels, coarse, smem=(3,),
    )

    def with_halo(value, up, down):
        over = shifted(up, "cross", 1)
        low = shifted(down, "cross", -1)
        up, down = call(send_slab_kernel, [(96, 128), (32, 128)], [], value, over, low)
        return (value, over, low, shifted(up, "slab", 1), shifted(down, "slab", -1), sigma, element_matrix, ionic)

    z, up, down, scale = call(
        first_solve_kernel, [field, above, under, (8, 8, 128)], [], place, gather(message), r, diagonal, labels, smem=(0,)
    )
    q, message = call(first_image_kernel, [field, (n_slab, 8, 128)], space, *with_halo(z, up, down), labels)
    w, up, down = call(
        next_solve_kernel, [field, above, under], [], place, gather(message), q, diagonal, labels, scale, smem=(0,)
    )
    t, tile = call(next_image_kernel, [field, (8, 128)], space, *with_halo(w, up, down), r, z, q)
    return tuple(
        call(finish_kernel, [(6, 6, 384)] * 2, [(128, 128), (384, 128)], add_up(tile), r, z, q, w, t)
    )


def solution(mesh):
    return jax.shard_map(
        body,
        mesh=mesh,
        in_specs=(
            P("slab", "cross", None),
            P("slab", "cross", None),
            P(),
            P("slab", "cross", None),
            P(),
            P("slab", "cross", None),
        ),
        out_specs=(P("slab", "cross", None), P("slab", "cross", None)),
        check_vma=False,
    )
```

```python
import functools

import jax
import jax.numpy as jnp
from jax import lax
from jax.experimental import pallas as pl
from jax.experimental.pallas import tpu as pltpu
from jax.sharding import PartitionSpec as P

LABELS = 8
DAMPING = 0.8
COUPLING = 0.2
SHARE = 0.1
REACH = 3
NEAR = REACH + 1


F32 = jnp.float32
BF16 = jnp.bfloat16
SPAN = (-1, 0, 1)


def lanes(shape):
    return lax.broadcasted_iota(jnp.int32, shape, len(shape) - 1)


def call(kernel, out_shapes, scratch, *operands, smem=(), away=()):
    specs = [
        pl.BlockSpec(memory_space=pltpu.SMEM if index in smem else pltpu.HBM if index in away else pltpu.VMEM)
        for index in range(len(operands))
    ]
    return pl.pallas_call(
        kernel,
        out_shape=[jax.ShapeDtypeStruct(shape, F32) for shape in out_shapes],
        in_specs=specs,
        out_specs=[pl.BlockSpec(memory_space=pltpu.VMEM)] * len(out_shapes),
        scratch_shapes=[pltpu.VMEM(shape, F32) if isinstance(shape, tuple) else shape for shape in scratch],
        compiler_params=pltpu.CompilerParams(vmem_limit_bytes=24 << 20),
    )(*operands)


def restrict(field, labels):
    rows = []
    for label in range(LABELS):
        kept = jnp.sum(jnp.where(labels == label + 1.0, field, 0.0), axis=0)
        rows.append(jnp.sum(kept, axis=0, keepdims=True))
    sums = jnp.concatenate(rows, 0)
    even = lanes((8, 128)) % 2 == 0
    return sums + jnp.where(even, pltpu.roll(sums, 127, 1), pltpu.roll(sums, 1, 1))


def prolong(coarse, labels):
    row = lax.broadcasted_iota(jnp.int32, (16, 128), 0)
    field = jnp.zeros_like(labels)
    for label in range(LABELS):
        low, own, high = [coarse[step, label : label + 1, :] for step in range(3)]
        values = jnp.where(row < 3, low, jnp.where(row < 9, own, high))
        field = jnp.where(labels == label + 1.0, values[None], field)
    return field


def assemble(product_of, total_ref):
    total_ref[...] = jnp.zeros_like(total_ref)
    start = lanes((16, 128)) == 0
    for i in SPAN:
        low_a, high_a = {-1: (3, 4), 0: (0, 4), 1: (0, 3)}[i]
        for j in SPAN:
            product = product_of((i + 1) * 3 + j + 1)
            last = pltpu.roll(product[48:64], 1, 1)
            pieces = [
                product[0:16] + jnp.where(start, 0.0, last),
                product[16:32],
                product[32:48],
            ]
            for c in range(3):
                for b in range(4):
                    y = 3 * j + b
                    if 0 <= y < 6:
                        x = 3 * i + low_a
                        rows = pieces[c][4 * b + low_a : 4 * b + high_a]
                        total_ref[c * 6 + y, x : x + high_a - low_a, :] += rows


def unpack_kernel(source_hbm, potential_hbm, map_hbm, r_ref, ionic_ref, label_ref, coarse_ref,
                  rows_ref, turned_ref, source_ref, potential_ref, map_ref, sems):
    copies = [
        pltpu.make_async_copy(away, here, sems.at[index])
        for index, (away, here) in enumerate(
            ((source_hbm, source_ref), (potential_hbm, potential_ref), (map_hbm, map_ref))
        )
    ]
    for copy in copies:
        copy.start()
    rows_ref[...] = jnp.zeros_like(rows_ref)
    for copy in copies:
        copy.wait()
    for y in range(6):
        for x in range(6):
            row = y * 6 + x
            rows_ref[row : row + 1, :] = source_ref[x, y : y + 1, :]
            rows_ref[36 + row : 37 + row, :] = potential_ref[x, y : y + 1, :]
            rows_ref[72 + row : 73 + row, :] = map_ref[x, y : y + 1, :].astype(F32)
    for piece in range(3):
        turned_ref[128 * piece : 128 * piece + 128, :] = rows_ref[:, 128 * piece : 128 * piece + 128].T
    r_ref[...] = jnp.zeros_like(r_ref)
    ionic_ref[...] = jnp.zeros_like(ionic_ref)
    label_ref[...] = jnp.zeros_like(label_ref)
    for c in range(3):
        split = turned_ref[pl.ds(c, 128, stride=3), :].T
        for y in range(6):
            r_ref[c * 6 + y, 0:6, :] = split[6 * y : 6 * y + 6]
            tangent = jnp.tanh(split[36 + 6 * y : 42 + 6 * y])
            ionic_ref[c * 6 + y, 0:6, :] = 1.0 + 2.0 * (1.0 - tangent * tangent)
            label_ref[c * 6 + y, 0:6, :] = split[72 + 6 * y : 78 + 6 * y] + 1.0
    coarse_ref[...] = restrict(r_ref[...], label_ref[...])


def send_slab(field_ref, up_ref, down_ref, up_start, down_start):
    for n in range(18):
        up_ref[up_start + 3 * n : up_start + 3 * n + 3, :] = field_ref[n, 3:6, :]
        down_ref[down_start + n : down_start + n + 1, :] = field_ref[n, 0:1, :]


def diagonal_kernel(own_ref, beside_ref, below_ref, corner_ref, table_ref, matrix_ref, r_ref, ionic_ref, label_ref,
                    coarse_ref, sigma_ref, diagonal_ref, scaled_ref, message_ref, up_ref, down_ref, total_ref):
    def conductance(region):
        value = jnp.zeros(region.shape, F32)
        for index in range(4):
            value = jnp.where(region == index + 1, table_ref[index], value)
        return value

    sigma_ref[0:1, :] = conductance(corner_ref[...])
    sigma_ref[1:3, :] = conductance(below_ref[...])
    for i in range(2):
        sigma_ref[3 + 3 * i : 4 + 3 * i, :] = conductance(beside_ref[i : i + 1, :])
        sigma_ref[4 + 3 * i : 6 + 3 * i, :] = conductance(own_ref[i] + 1)
    square = (64, 64)
    eye = lax.broadcasted_iota(jnp.int32, square, 0) == lax.broadcasted_iota(jnp.int32, square, 1)
    corner = jnp.sum(jnp.where(eye, matrix_ref[...], 0.0), axis=1, keepdims=True)
    assemble(lambda e: corner * sigma_ref[e : e + 1, :], total_ref)
    labels = label_ref[...]
    diagonal = jnp.where(labels == 0.0, 1.0, total_ref[...] + ionic_ref[...])
    diagonal_ref[...] = diagonal
    coarse_diag = SHARE * restrict(diagonal, labels)
    even = lanes((8, 128)) % 2 == 0
    message = jnp.where(even, coarse_ref[...], coarse_diag)
    message_ref[...] = jnp.broadcast_to(message[None], message_ref.shape)
    scaled_ref[...] = r_ref[...] / diagonal
    up_ref[...] = jnp.zeros_like(up_ref)
    down_ref[...] = jnp.zeros_like(down_ref)
    send_slab(scaled_ref, up_ref, down_ref, 0, 0)
    send_slab(label_ref, up_ref, down_ref, 56, 20)


def along(values):
    lane = lanes(values.shape)
    row = lax.broadcasted_iota(jnp.int32, values.shape, 1)
    after = pltpu.roll(values, 7, 1)
    carried = jnp.where(lane < 126, pltpu.roll(after, 126, 2), 0.0)
    after = jnp.where(row == 7, carried, after)
    before = pltpu.roll(values, 1, 1)
    carried = jnp.where(lane >= 2, pltpu.roll(before, 2, 2), 0.0)
    return after + jnp.where(row == 0, carried, before)


def smooth(start, valid):
    level = start
    for sweep in range(REACH):
        beside = level[2:] + level[:-2] + along(level[1:-1])
        here = slice(sweep + 1, 2 * NEAR - sweep)
        level = start[here] + (1.0 - DAMPING) * level[1:-1] + (DAMPING * COUPLING) * beside
        level = level * valid[here]
    return level


def around(place_ref, count):
    rows, valid = [], []
    for step in range(-NEAR, NEAR + 1):
        row = place_ref[0] + step
        inside = jnp.logical_and(row >= 0, row < count)
        rows.append(jnp.clip(row, 0, count - 1))
        valid.append(jnp.where(inside, jnp.ones((1, 8, 128), F32), 0.0))
    return rows, jnp.concatenate(valid, 0)


def even_part(tiles):
    even = lanes(tiles.shape) % 2 == 0
    return jnp.where(even, tiles, pltpu.roll(tiles, 1, tiles.ndim - 1))


def odd_part(tiles):
    even = lanes(tiles.shape) % 2 == 0
    return jnp.where(even, pltpu.roll(tiles, 127, tiles.ndim - 1), tiles)


def widen(field_ref, low_ref, high_ref, low_start, high_start, wide_ref):
    wide_ref[...] = jnp.zeros_like(wide_ref)
    for n in range(18):
        wide_ref[n, 0:3, :] = low_ref[low_start + 3 * n : low_start + 3 * n + 3, :]
        wide_ref[n, 3:9, :] = field_ref[n, 0:6, :]
        wide_ref[n, 9:10, :] = high_ref[high_start + n : high_start + n + 1, :]


def send_cross(wide_ref, own_ref, up_ref, down_ref):
    own_ref[...] = jnp.zeros_like(own_ref)
    for n in range(18):
        own_ref[n, 0:6, :] = wide_ref[n, 3:9, :]
    up_ref[90:96, :] = jnp.zeros((6, 128), F32)
    down_ref[30:32, :] = jnp.zeros((2, 128), F32)
    for c in range(3):
        for y in range(3):
            row = (3 * c + y) * 10
            up_ref[row : row + 10, :] = wide_ref[6 * c + 3 + y, 0:10, :]
        down_ref[10 * c : 10 * c + 10, :] = wide_ref[6 * c, 0:10, :]


def first_solve_kernel(place_ref, gathered_ref, scaled_ref, label_ref, low_ref, high_ref,
                       wide_ref, z_ref, up_ref, down_ref, scale_ref, wide_label_ref):
    rows, valid = around(place_ref, gathered_ref.shape[0])
    near = jnp.concatenate([gathered_ref[pl.ds(row, 1)] for row in rows], 0)
    sums = jnp.sum(gathered_ref[...], axis=0)
    inverse = valid / jnp.sqrt(odd_part(near))
    share = 1.0 / odd_part(sums)
    scale_ref[0 : 2 * NEAR + 1] = inverse
    scale_ref[2 * NEAR + 1] = share
    level = smooth(DAMPING * even_part(near) * inverse, valid)
    coarse = level * inverse[REACH : REACH + 3] + (even_part(sums) * share)[None]
    widen(label_ref, low_ref, high_ref, 56, 20, wide_label_ref)
    widen(scaled_ref, low_ref, high_ref, 0, 0, wide_ref)
    wide_ref[...] += prolong(coarse, wide_label_ref[...])
    send_cross(wide_ref, z_ref, up_ref, down_ref)


def next_solve_kernel(place_ref, gathered_ref, scaled_ref, wide_label_ref, low_ref, high_ref, scale_ref,
                      wide_ref, w_ref, up_ref, down_ref):
    rows, valid = around(place_ref, gathered_ref.shape[0])
    near = jnp.concatenate([gathered_ref[pl.ds(row, 1)] for row in rows], 0)
    sums = jnp.sum(gathered_ref[...], axis=0)
    inverse = scale_ref[0 : 2 * NEAR + 1]
    level = smooth(DAMPING * near * inverse, valid)
    coarse = level * inverse[REACH : REACH + 3] + (sums * scale_ref[2 * NEAR + 1])[None]
    widen(scaled_ref, low_ref, high_ref, 0, 0, wide_ref)
    wide_ref[...] += prolong(coarse, wide_label_ref[...])
    send_cross(wide_ref, w_ref, up_ref, down_ref)


def operate(wide_ref, field_ref, above_ref, under_ref, sigma_ref, matrix_ref, ionic_ref,
            grid_ref, local_ref, product_ref, total_ref):
    for c in range(3):
        for y in range(10):
            n = c * 10 + y
            if y < 3:
                row = (3 * c + y) * 10
                grid_ref[n, 0:10, :] = above_ref[row : row + 10, :]
            elif y < 9:
                grid_ref[n, 0:10, :] = wide_ref[6 * c + y - 3, 0:10, :]
            else:
                grid_ref[n, 0:10, :] = under_ref[10 * c : 10 * c + 10, :]
    end = lanes((10, 128)) == 127
    for y in range(10):
        grid_ref[30 + y, 0:10, :] = jnp.where(end, 0.0, pltpu.roll(grid_ref[y, 0:10, :], 127, 1))
    for i in SPAN:
        for j in SPAN:
            left = ((i + 1) * 3 + j + 1) * 128
            for c in range(4):
                for b in range(4):
                    row = 16 * c + 4 * b
                    n = c * 10 + 3 * (j + 1) + b
                    local_ref[row : row + 4, left : left + 128] = grid_ref[n, 3 * i + 3 : 3 * i + 7, :]
    matrix = matrix_ref[...]
    matrix_high = matrix.astype(BF16)
    matrix_low = (matrix - matrix_high.astype(F32)).astype(BF16)
    local = local_ref[...]
    high = local.astype(BF16)
    low = (local - high.astype(F32)).astype(BF16)
    dot = functools.partial(jnp.dot, preferred_element_type=F32)
    product_ref[...] = dot(matrix_high, high) + (dot(matrix_high, low) + dot(matrix_low, high))
    assemble(lambda e: product_ref[:, 128 * e : 128 * e + 128] * sigma_ref[e : e + 1, :], total_ref)
    return total_ref[...] + ionic_ref[...] * field_ref[...]


def first_image_kernel(wide_ref, z_ref, above_ref, under_ref, sigma_ref, matrix_ref, ionic_ref, diagonal_ref, label_ref,
                       q_ref, scaled_ref, message_ref, up_ref, down_ref, *scratch):
    image = operate(wide_ref, z_ref, above_ref, under_ref, sigma_ref, matrix_ref, ionic_ref, *scratch)
    q_ref[...] = image
    message_ref[...] = jnp.broadcast_to(restrict(image, label_ref[...])[None], message_ref.shape)
    scaled_ref[...] = image / diagonal_ref[...]
    up_ref[...] = jnp.zeros_like(up_ref)
    down_ref[...] = jnp.zeros_like(down_ref)
    send_slab(scaled_ref, up_ref, down_ref, 0, 0)


def next_image_kernel(wide_ref, w_ref, above_ref, under_ref, sigma_ref, matrix_ref, ionic_ref,
                      r_ref, z_ref, q_ref, t_ref, message_ref, *scratch):
    image = operate(wide_ref, w_ref, above_ref, under_ref, sigma_ref, matrix_ref, ionic_ref, *scratch)
    t_ref[...] = image
    r, z, q, w = r_ref[...], z_ref[...], q_ref[...], w_ref[...]
    rows = []
    for left, right in ((r, z), (z, q), (r, w), (q, w), (z, image), (w, image)):
        rows.append(jnp.sum(jnp.sum(left * right, axis=0), axis=0, keepdims=True))
    rows.append(jnp.zeros((2, 128), F32))
    message_ref[...] = jnp.broadcast_to(jnp.concatenate(rows, 0)[None], message_ref.shape)


def finish_kernel(dots_ref, r_ref, z_ref, q_ref, w_ref, t_ref, solution_ref, residual_ref, rows_ref, turned_ref):
    dots = dots_ref[...]
    rz, zq, rw, qw, zt, wt = [dots[index : index + 1] for index in range(6)]
    alpha = rz / zq
    rz_next = alpha * (alpha * qw - rw)
    beta = rz_next / rz
    more = 1.0 + beta
    second = rz_next / (more * more * zq - more * alpha * (zt + qw) + alpha * alpha * wt)
    from_z = alpha + second * more
    from_w = second * alpha
    rows_ref[...] = jnp.zeros_like(rows_ref)
    for c in range(3):
        for y in range(6):
            n = 6 * c + y
            answer = from_z * z_ref[n] - from_w * w_ref[n]
            left = r_ref[n] - from_z * q_ref[n] + from_w * t_ref[n]
            rows_ref[6 * y : 6 * y + 6, :] = answer[0:6]
            rows_ref[36 + 6 * y : 42 + 6 * y, :] = left[0:6]
        turned_ref[pl.ds(c, 128, stride=3), :] = rows_ref[...].T
    for piece in range(3):
        back = turned_ref[128 * piece : 128 * piece + 128, :].T
        for y in range(6):
            for x in range(6):
                row = y * 6 + x
                solution_ref[x, y : y + 1, 128 * piece : 128 * piece + 128] = back[row : row + 1]
                residual_ref[x, y : y + 1, 128 * piece : 128 * piece + 128] = back[36 + row : 37 + row]


def body(adjoint_source, potential, element_matrix, region_labels, conductivity, restriction_map):
    n_slab = lax.axis_size("slab")
    n_cross = lax.axis_size("cross")
    place = lax.axis_index("slab").astype(jnp.int32).reshape(1)
    def shifted(value, axis, step):
        count = lax.axis_size(axis)
        pairs = [(source, source + step) for source in range(count) if 0 <= source + step < count]
        return lax.ppermute(value, axis, pairs)

    def gather(copies):
        return lax.all_to_all(copies, "slab", 0, 0, tiled=True)

    field, wide = (18, 8, 128), (18, 16, 128)
    space = [(40, 16, 128), (64, 1152), (64, 1152), field]
    regions = region_labels + 1
    beside = shifted(regions[:, 1], "cross", 1)
    below = shifted(regions[1], "slab", 1)
    pairs = [
        (slab * n_cross + cross, (slab + 1) * n_cross + cross + 1)
        for slab in range(n_slab - 1)
        for cross in range(n_cross - 1)
    ]
    corner = lax.ppermute(regions[1, 1:2], ("slab", "cross"), pairs)
    r, ionic, labels, coarse = call(
        unpack_kernel, [field] * 3 + [(8, 128)],
        [(128, 384), (384, 128), (6, 6, 384), (6, 6, 384), pltpu.VMEM((6, 6, 384), jnp.int32), pltpu.SemaphoreType.DMA((3,))],
        adjoint_source, potential, restriction_map, away=(0, 1, 2),
    )
    sigma, diagonal, scaled, message, up, down = call(
        diagonal_kernel, [(9, 128), field, field, (n_slab, 8, 128), (112, 128), (40, 128)], [field],
        region_labels, beside, below, corner, conductivity, element_matrix, r, ionic, labels, coarse, smem=(4,),
    )

    def beyond(up, down, axis):
        return shifted(up, axis, 1), shifted(down, axis, -1)

    faces = [(96, 128), (32, 128)]
    wide_z, z, up, down, scale, wide_labels = call(
        first_solve_kernel, [wide, field, *faces, (10, 8, 128), wide], [],
        place, gather(message), scaled, labels, *beyond(up, down, "slab"), smem=(0,),
    )
    q, scaled, message, up, down = call(
        first_image_kernel, [field, field, (n_slab, 8, 128), (56, 128), (24, 128)], space,
        wide_z, z, *beyond(up, down, "cross"), sigma, element_matrix, ionic, diagonal, labels,
    )
    wide_w, w, up, down = call(
        next_solve_kernel, [wide, field, *faces], [],
        place, gather(message), scaled, wide_labels, *beyond(up, down, "slab"), scale, smem=(0,),
    )
    t, message = call(
        next_image_kernel, [field, (n_slab, 8, 128)], space,
        wide_w, w, *beyond(up, down, "cross"), sigma, element_matrix, ionic, r, z, q,
    )
    dots = lax.psum(jnp.sum(gather(message), (0, 2)), "cross").reshape(8, 1)
    return tuple(call(finish_kernel, [(6, 6, 384)] * 2, [(128, 128), (384, 128)], dots, r, z, q, w, t))


def solution(mesh):
    return jax.shard_map(
        body,
        mesh=mesh,
        in_specs=(
            P("slab", "cross", None),
            P("slab", "cross", None),
            P(),
            P("slab", "cross", None),
            P(),
            P("slab", "cross", None),
        ),
        out_specs=(P("slab", "cross", None), P("slab", "cross", None)),
        check_vma=False,
    )
```

```python
import functools

import jax
import jax.numpy as jnp
from jax import lax
from jax.experimental import pallas as pl
from jax.experimental.pallas import tpu as pltpu
from jax.sharding import PartitionSpec as P

LABELS = 8
DAMPING = 0.8
COUPLING = 0.2
SHARE = 0.1
REACH = 3
NEAR = REACH + 1


F32 = jnp.float32
BF16 = jnp.bfloat16
SPAN = (-1, 0, 1)


def lanes(shape):
    return lax.broadcasted_iota(jnp.int32, shape, len(shape) - 1)


def call(kernel, out_shapes, scratch, *operands, smem=(), away=()):
    specs = [
        pl.BlockSpec(memory_space=pltpu.SMEM if index in smem else pltpu.HBM if index in away else pltpu.VMEM)
        for index in range(len(operands))
    ]
    operands = [
        pltpu.with_memory_space_constraint(operand, pltpu.HBM) if index in away else operand
        for index, operand in enumerate(operands)
    ]
    return pl.pallas_call(
        kernel,
        out_shape=[jax.ShapeDtypeStruct(shape, F32) for shape in out_shapes],
        in_specs=specs,
        out_specs=[pl.BlockSpec(memory_space=pltpu.VMEM)] * len(out_shapes),
        scratch_shapes=[pltpu.VMEM(shape, F32) if isinstance(shape, tuple) else shape for shape in scratch],
        compiler_params=pltpu.CompilerParams(vmem_limit_bytes=24 << 20),
    )(*operands)


def restrict(field, labels):
    rows = []
    for label in range(LABELS):
        kept = jnp.sum(jnp.where(labels == label + 1.0, field, 0.0), axis=0)
        rows.append(jnp.sum(kept, axis=0, keepdims=True))
    sums = jnp.concatenate(rows, 0)
    even = lanes((8, 128)) % 2 == 0
    return sums + jnp.where(even, pltpu.roll(sums, 127, 1), pltpu.roll(sums, 1, 1))


def prolong(coarse, labels):
    row = lax.broadcasted_iota(jnp.int32, (16, 128), 0)
    field = jnp.zeros_like(labels)
    for label in range(LABELS):
        low, own, high = [coarse[step, label : label + 1, :] for step in range(3)]
        values = jnp.where(row < 3, low, jnp.where(row < 9, own, high))
        field = jnp.where(labels == label + 1.0, values[None], field)
    return field


def assemble(product_of, total_ref):
    total_ref[...] = jnp.zeros_like(total_ref)
    start = lanes((16, 128)) == 0
    for i in SPAN:
        low_a, high_a = {-1: (3, 4), 0: (0, 4), 1: (0, 3)}[i]
        for j in SPAN:
            product = product_of((i + 1) * 3 + j + 1)
            last = pltpu.roll(product[48:64], 1, 1)
            pieces = [
                product[0:16] + jnp.where(start, 0.0, last),
                product[16:32],
                product[32:48],
            ]
            for c in range(3):
                for b in range(4):
                    y = 3 * j + b
                    if 0 <= y < 6:
                        x = 3 * i + low_a
                        rows = pieces[c][4 * b + low_a : 4 * b + high_a]
                        total_ref[c * 6 + y, x : x + high_a - low_a, :] += rows


def unpack_kernel(source_hbm, potential_hbm, map_hbm, region_hbm, table_hbm, r_ref, ionic_ref, label_ref, coarse_ref,
                  own_ref, beside_ref, below_ref, corner_ref,
                  rows_ref, turned_ref, source_ref, potential_ref, map_ref, region_ref, table_ref, sems):
    copies = [
        pltpu.make_async_copy(away, here, sems.at[index])
        for index, (away, here) in enumerate(
            (
                (source_hbm, source_ref),
                (potential_hbm, potential_ref),
                (map_hbm, map_ref),
                (region_hbm, region_ref),
                (table_hbm, table_ref),
            )
        )
    ]
    for copy in copies:
        copy.start()
    rows_ref[...] = jnp.zeros_like(rows_ref)
    for copy in copies:
        copy.wait()
    for i in range(2):
        region = region_ref[i]
        sigma = jnp.zeros(region.shape, F32)
        for index in range(4):
            sigma = jnp.where(region == index, table_ref[index], sigma)
        own_ref[2 * i : 2 * i + 2, :] = sigma
    beside_ref[0:1, :] = own_ref[1:2, :]
    beside_ref[1:2, :] = own_ref[3:4, :]
    below_ref[...] = own_ref[2:4, :]
    corner_ref[...] = own_ref[3:4, :]
    for y in range(6):
        for x in range(6):
            row = y * 6 + x
            rows_ref[row : row + 1, :] = source_ref[x, y : y + 1, :]
            rows_ref[36 + row : 37 + row, :] = potential_ref[x, y : y + 1, :]
            rows_ref[72 + row : 73 + row, :] = map_ref[x, y : y + 1, :].astype(F32)
    for piece in range(3):
        turned_ref[128 * piece : 128 * piece + 128, :] = rows_ref[:, 128 * piece : 128 * piece + 128].T
    r_ref[...] = jnp.zeros_like(r_ref)
    ionic_ref[...] = jnp.zeros_like(ionic_ref)
    label_ref[...] = jnp.zeros_like(label_ref)
    for c in range(3):
        split = turned_ref[pl.ds(c, 128, stride=3), :].T
        for y in range(6):
            r_ref[c * 6 + y, 0:6, :] = split[6 * y : 6 * y + 6]
            tangent = jnp.tanh(split[36 + 6 * y : 42 + 6 * y])
            ionic_ref[c * 6 + y, 0:6, :] = 1.0 + 2.0 * (1.0 - tangent * tangent)
            label_ref[c * 6 + y, 0:6, :] = split[72 + 6 * y : 78 + 6 * y] + 1.0
    coarse_ref[...] = restrict(r_ref[...], label_ref[...])


def send_slab(field_ref, up_ref, down_ref, up_start, down_start):
    for n in range(18):
        up_ref[up_start + 3 * n : up_start + 3 * n + 3, :] = field_ref[n, 3:6, :]
        down_ref[down_start + n : down_start + n + 1, :] = field_ref[n, 0:1, :]


def diagonal_kernel(own_ref, beside_ref, below_ref, corner_ref, matrix_ref, r_ref, ionic_ref, label_ref,
                    coarse_ref, sigma_ref, diagonal_ref, scaled_ref, message_ref, up_ref, down_ref, total_ref):
    sigma_ref[0:1, :] = corner_ref[...]
    sigma_ref[1:3, :] = below_ref[...]
    for i in range(2):
        sigma_ref[3 + 3 * i : 4 + 3 * i, :] = beside_ref[i : i + 1, :]
        sigma_ref[4 + 3 * i : 6 + 3 * i, :] = own_ref[2 * i : 2 * i + 2, :]
    square = (64, 64)
    eye = lax.broadcasted_iota(jnp.int32, square, 0) == lax.broadcasted_iota(jnp.int32, square, 1)
    corner = jnp.sum(jnp.where(eye, matrix_ref[...], 0.0), axis=1, keepdims=True)
    assemble(lambda e: corner * sigma_ref[e : e + 1, :], total_ref)
    labels = label_ref[...]
    diagonal = jnp.where(labels == 0.0, 1.0, total_ref[...] + ionic_ref[...])
    diagonal_ref[...] = diagonal
    coarse_diag = SHARE * restrict(diagonal, labels)
    even = lanes((8, 128)) % 2 == 0
    message = jnp.where(even, coarse_ref[...], coarse_diag)
    message_ref[...] = jnp.broadcast_to(message[None], message_ref.shape)
    scaled_ref[...] = r_ref[...] / diagonal
    up_ref[...] = jnp.zeros_like(up_ref)
    down_ref[...] = jnp.zeros_like(down_ref)
    send_slab(scaled_ref, up_ref, down_ref, 0, 0)
    send_slab(label_ref, up_ref, down_ref, 56, 20)


def along(values):
    lane = lanes(values.shape)
    row = lax.broadcasted_iota(jnp.int32, values.shape, 1)
    after = pltpu.roll(values, 7, 1)
    carried = jnp.where(lane < 126, pltpu.roll(after, 126, 2), 0.0)
    after = jnp.where(row == 7, carried, after)
    before = pltpu.roll(values, 1, 1)
    carried = jnp.where(lane >= 2, pltpu.roll(before, 2, 2), 0.0)
    return after + jnp.where(row == 0, carried, before)


def smooth(start, valid):
    level = start
    for sweep in range(REACH):
        beside = level[2:] + level[:-2] + along(level[1:-1])
        here = slice(sweep + 1, 2 * NEAR - sweep)
        level = start[here] + (1.0 - DAMPING) * level[1:-1] + (DAMPING * COUPLING) * beside
        level = level * valid[here]
    return level


def around(place_ref, count):
    rows, valid = [], []
    for step in range(-NEAR, NEAR + 1):
        row = place_ref[0] + step
        inside = jnp.logical_and(row >= 0, row < count)
        rows.append(jnp.clip(row, 0, count - 1))
        valid.append(jnp.where(inside, jnp.ones((1, 8, 128), F32), 0.0))
    return rows, jnp.concatenate(valid, 0)


def even_part(tiles):
    even = lanes(tiles.shape) % 2 == 0
    return jnp.where(even, tiles, pltpu.roll(tiles, 1, tiles.ndim - 1))


def odd_part(tiles):
    even = lanes(tiles.shape) % 2 == 0
    return jnp.where(even, pltpu.roll(tiles, 127, tiles.ndim - 1), tiles)


def widen(field_ref, low_ref, high_ref, low_start, high_start, wide_ref):
    wide_ref[...] = jnp.zeros_like(wide_ref)
    for n in range(18):
        wide_ref[n, 0:3, :] = low_ref[low_start + 3 * n : low_start + 3 * n + 3, :]
        wide_ref[n, 3:9, :] = field_ref[n, 0:6, :]
        wide_ref[n, 9:10, :] = high_ref[high_start + n : high_start + n + 1, :]


def send_cross(even, wide_ref, own_ref, near_ref, far_ref):
    own_ref[...] = jnp.zeros_like(own_ref)
    for n in range(18):
        own_ref[n, 0:6, :] = wide_ref[n, 3:9, :]
    near_ref[...] = jnp.zeros_like(near_ref)
    far_ref[...] = jnp.zeros_like(far_ref)

    def fill(up_ref, down_ref):
        for c in range(3):
            for y in range(3):
                row = (3 * c + y) * 10
                up_ref[row : row + 10, :] = wide_ref[6 * c + 3 + y, 0:10, :]
            down_ref[10 * c : 10 * c + 10, :] = wide_ref[6 * c, 0:10, :]

    @pl.when(even)
    def _():
        fill(near_ref, far_ref)

    @pl.when(jnp.logical_not(even))
    def _():
        fill(far_ref, near_ref)


def first_solve_kernel(place_ref, gathered_ref, scaled_ref, label_ref, low_ref, high_ref,
                       wide_ref, z_ref, near_ref, far_ref, scale_ref, wide_label_ref):
    rows, valid = around(place_ref, gathered_ref.shape[0])
    tiles = jnp.concatenate([gathered_ref[pl.ds(row, 1)] for row in rows], 0)
    sums = jnp.sum(gathered_ref[...], axis=0)
    inverse = valid / jnp.sqrt(odd_part(tiles))
    share = 1.0 / odd_part(sums)
    scale_ref[0 : 2 * NEAR + 1] = inverse
    scale_ref[2 * NEAR + 1] = share
    level = smooth(DAMPING * even_part(tiles) * inverse, valid)
    coarse = level * inverse[REACH : REACH + 3] + (even_part(sums) * share)[None]
    widen(label_ref, low_ref, high_ref, 56, 20, wide_label_ref)
    widen(scaled_ref, low_ref, high_ref, 0, 0, wide_ref)
    wide_ref[...] += prolong(coarse, wide_label_ref[...])
    send_cross(place_ref[1] == 0, wide_ref, z_ref, near_ref, far_ref)


def next_solve_kernel(place_ref, gathered_ref, scaled_ref, wide_label_ref, low_ref, high_ref, scale_ref,
                      wide_ref, w_ref, near_ref, far_ref):
    rows, valid = around(place_ref, gathered_ref.shape[0])
    tiles = jnp.concatenate([gathered_ref[pl.ds(row, 1)] for row in rows], 0)
    sums = jnp.sum(gathered_ref[...], axis=0)
    inverse = scale_ref[0 : 2 * NEAR + 1]
    level = smooth(DAMPING * tiles * inverse, valid)
    coarse = level * inverse[REACH : REACH + 3] + (sums * scale_ref[2 * NEAR + 1])[None]
    widen(scaled_ref, low_ref, high_ref, 0, 0, wide_ref)
    wide_ref[...] += prolong(coarse, wide_label_ref[...])
    send_cross(place_ref[1] == 0, wide_ref, w_ref, near_ref, far_ref)


def operate(place_ref, wide_ref, field_ref, near_ref, far_ref, sigma_ref, matrix_ref, ionic_ref,
            grid_ref, local_ref, product_ref, total_ref):
    for n in range(18):
        grid_ref[n // 6 * 10 + 3 + n % 6, 0:10, :] = wide_ref[n, 0:10, :]

    def fill(above_ref, under_ref):
        for c in range(3):
            for y in range(3):
                row = (3 * c + y) * 10
                grid_ref[10 * c + y, 0:10, :] = above_ref[row : row + 10, :]
            grid_ref[10 * c + 9, 0:10, :] = under_ref[10 * c : 10 * c + 10, :]

    even = place_ref[1] == 0

    @pl.when(even)
    def _():
        fill(far_ref, near_ref)

    @pl.when(jnp.logical_not(even))
    def _():
        fill(near_ref, far_ref)

    end = lanes((10, 128)) == 127
    for y in range(10):
        grid_ref[30 + y, 0:10, :] = jnp.where(end, 0.0, pltpu.roll(grid_ref[y, 0:10, :], 127, 1))
    for i in SPAN:
        for j in SPAN:
            left = ((i + 1) * 3 + j + 1) * 128
            for c in range(4):
                for b in range(4):
                    row = 16 * c + 4 * b
                    n = c * 10 + 3 * (j + 1) + b
                    local_ref[row : row + 4, left : left + 128] = grid_ref[n, 3 * i + 3 : 3 * i + 7, :]
    matrix = matrix_ref[...]
    matrix_high = matrix.astype(BF16)
    matrix_low = (matrix - matrix_high.astype(F32)).astype(BF16)
    local = local_ref[...]
    high = local.astype(BF16)
    low = (local - high.astype(F32)).astype(BF16)
    dot = functools.partial(jnp.dot, preferred_element_type=F32)
    product_ref[...] = dot(matrix_high, high) + (dot(matrix_high, low) + dot(matrix_low, high))
    assemble(lambda e: product_ref[:, 128 * e : 128 * e + 128] * sigma_ref[e : e + 1, :], total_ref)
    return total_ref[...] + ionic_ref[...] * field_ref[...]


def first_image_kernel(place_ref, wide_ref, z_ref, near_ref, far_ref, sigma_ref, matrix_ref, ionic_ref, diagonal_ref, label_ref,
                       q_ref, scaled_ref, message_ref, up_ref, down_ref, *scratch):
    image = operate(place_ref, wide_ref, z_ref, near_ref, far_ref, sigma_ref, matrix_ref, ionic_ref, *scratch)
    q_ref[...] = image
    message_ref[...] = jnp.broadcast_to(restrict(image, label_ref[...])[None], message_ref.shape)
    scaled_ref[...] = image / diagonal_ref[...]
    up_ref[...] = jnp.zeros_like(up_ref)
    down_ref[...] = jnp.zeros_like(down_ref)
    send_slab(scaled_ref, up_ref, down_ref, 0, 0)


def next_image_kernel(place_ref, wide_ref, w_ref, near_ref, far_ref, sigma_ref, matrix_ref, ionic_ref,
                      r_ref, z_ref, q_ref, t_ref, message_ref, *scratch):
    image = operate(place_ref, wide_ref, w_ref, near_ref, far_ref, sigma_ref, matrix_ref, ionic_ref, *scratch)
    t_ref[...] = image
    r, z, q, w = r_ref[...], z_ref[...], q_ref[...], w_ref[...]
    row = jnp.zeros((1, 128), F32)
    for index, (left, right) in enumerate(((r, z), (z, q), (r, w), (q, w), (z, image), (w, image))):
        part = jnp.sum(jnp.sum(left * right, axis=0), axis=0, keepdims=True)
        row = jnp.where(lanes((1, 128)) == index, jnp.sum(part, axis=1, keepdims=True), row)
    message_ref[...] = jnp.broadcast_to(row[None], message_ref.shape)


def finish_kernel(dots_ref, r_ref, z_ref, q_ref, w_ref, t_ref, solution_ref, residual_ref, rows_ref, turned_ref):
    dots = jnp.sum(dots_ref[...], axis=0)
    rz, zq, rw, qw, zt, wt = [dots[:, index : index + 1] for index in range(6)]
    alpha = rz / zq
    rz_next = alpha * (alpha * qw - rw)
    beta = rz_next / rz
    more = 1.0 + beta
    second = rz_next / (more * more * zq - more * alpha * (zt + qw) + alpha * alpha * wt)
    from_z = alpha + second * more
    from_w = second * alpha
    rows_ref[...] = jnp.zeros_like(rows_ref)
    for c in range(3):
        for y in range(6):
            n = 6 * c + y
            answer = from_z * z_ref[n] - from_w * w_ref[n]
            left = r_ref[n] - from_z * q_ref[n] + from_w * t_ref[n]
            rows_ref[6 * y : 6 * y + 6, :] = answer[0:6]
            rows_ref[36 + 6 * y : 42 + 6 * y, :] = left[0:6]
        turned_ref[pl.ds(c, 128, stride=3), :] = rows_ref[...].T
    for piece in range(3):
        back = turned_ref[128 * piece : 128 * piece + 128, :].T
        for y in range(6):
            for x in range(6):
                row = y * 6 + x
                solution_ref[x, y : y + 1, 128 * piece : 128 * piece + 128] = back[row : row + 1]
                residual_ref[x, y : y + 1, 128 * piece : 128 * piece + 128] = back[36 + row : 37 + row]


def body(adjoint_source, potential, element_matrix, region_labels, conductivity, restriction_map):
    n_slab = lax.axis_size("slab")
    n_cross = lax.axis_size("cross")
    slab, cross = lax.axis_index("slab"), lax.axis_index("cross")
    place = jnp.stack([slab, cross % 2]).astype(jnp.int32)
    columns = [
        [slab * n_cross + cross for slab in (2 * pair, 2 * pair + 1) for cross in range(n_cross)]
        for pair in range(n_slab // 2)
    ]
    planes = [[2 * pair + low for pair in range(n_slab // 2)] for low in range(2)]
    def shifted(value, axis, step):
        count = lax.axis_size(axis)
        pairs = [(source, source + step) for source in range(count) if 0 <= source + step < count]
        return lax.ppermute(value, axis, pairs)

    def gather(copies):
        return lax.all_to_all(copies, "slab", 0, 0, tiled=True)

    field, wide = (18, 8, 128), (18, 16, 128)
    space = [(40, 16, 128), (64, 1152), (64, 1152), field]
    pairs = [
        (slab * n_cross + cross, (slab + 1) * n_cross + cross + 1)
        for slab in range(n_slab - 1)
        for cross in range(n_cross - 1)
    ]
    r, ionic, labels, coarse, own, beside, below, corner = call(
        unpack_kernel, [field] * 3 + [(8, 128), (4, 128), (2, 128), (2, 128), (1, 128)],
        [(128, 384), (384, 128), (6, 6, 384), (6, 6, 384), pltpu.VMEM((6, 6, 384), jnp.int32),
         pltpu.VMEM((2, 2, 128), jnp.int32), pltpu.SMEM((4,), F32), pltpu.SemaphoreType.DMA((5,))],
        adjoint_source, potential, restriction_map, region_labels, conductivity, away=(0, 1, 2, 3, 4),
    )
    sigma, diagonal, scaled, message, up, down = call(
        diagonal_kernel, [(9, 128), field, field, (n_slab, 8, 128), (112, 128), (40, 128)], [field],
        own, shifted(beside, "cross", 1), shifted(below, "slab", 1), lax.ppermute(corner, ("slab", "cross"), pairs),
        element_matrix, r, ionic, labels, coarse,
    )

    def beyond(up, down):
        return shifted(up, "slab", 1), shifted(down, "slab", -1)

    def across(near, far):
        far_pairs = [(c, c + 1) for c in range(1, n_cross - 1, 2)]
        far_pairs += [(above, c) for c, above in far_pairs]
        far = lax.ppermute(far, "cross", far_pairs)
        return lax.ppermute(near, "cross", [(c, c ^ 1) for c in range(n_cross)]), far

    faces = [(96, 128), (96, 128)]
    wide_z, z, near, far, scale, wide_labels = call(
        first_solve_kernel, [wide, field, *faces, (10, 8, 128), wide], [],
        place, gather(message), scaled, labels, *beyond(up, down), smem=(0,),
    )
    q, scaled, message, up, down = call(
        first_image_kernel, [field, field, (n_slab, 8, 128), (56, 128), (24, 128)], space,
        place, wide_z, z, *across(near, far), sigma, element_matrix, ionic, diagonal, labels, smem=(0,),
    )
    wide_w, w, near, far = call(
        next_solve_kernel, [wide, field, *faces], [],
        place, gather(message), scaled, wide_labels, *beyond(up, down), scale, smem=(0,),
    )
    t, message = call(
        next_image_kernel, [field, (n_slab // 2, 1, 128)], space,
        place, wide_w, w, *across(near, far), sigma, element_matrix, ionic, r, z, q, smem=(0,),
    )
    parts = lax.all_to_all(message, "slab", 0, 0, axis_index_groups=planes, tiled=True)
    parts = jnp.broadcast_to(jnp.sum(parts, 0)[None], (2 * n_cross, 1, 128))
    dots = lax.all_to_all(parts, ("slab", "cross"), 0, 0, axis_index_groups=columns, tiled=True)
    return tuple(call(finish_kernel, [(6, 6, 384)] * 2, [(128, 128), (384, 128)], dots, r, z, q, w, t))


def solution(mesh):
    return jax.shard_map(
        body,
        mesh=mesh,
        in_specs=(
            P("slab", "cross", None),
            P("slab", "cross", None),
            P(),
            P("slab", "cross", None),
            P(),
            P("slab", "cross", None),
        ),
        out_specs=(P("slab", "cross", None), P("slab", "cross", None)),
        check_vma=False,
    )
```

```python
import functools

import jax
import jax.numpy as jnp
from jax import lax
from jax.experimental import pallas as pl
from jax.experimental.pallas import tpu as pltpu
from jax.sharding import PartitionSpec as P

LABELS = 8
DAMPING = 0.8
COUPLING = 0.2
SHARE = 0.1
REACH = 3
NEAR = REACH + 1


F32 = jnp.float32
BF16 = jnp.bfloat16
SPAN = (-1, 0, 1)


def lanes(shape):
    return lax.broadcasted_iota(jnp.int32, shape, len(shape) - 1)


def call(kernel, out_shapes, scratch, *operands, smem=(), away=(), sent=()):
    specs = [
        pl.BlockSpec(memory_space=pltpu.SMEM if index in smem else pltpu.HBM if index in away else pltpu.VMEM)
        for index in range(len(operands))
    ]
    operands = [
        pltpu.with_memory_space_constraint(operand, pltpu.HBM) if index in away else operand
        for index, operand in enumerate(operands)
    ]
    return pl.pallas_call(
        kernel,
        out_shape=[jax.ShapeDtypeStruct(shape, F32) for shape in out_shapes],
        in_specs=specs,
        out_specs=[
            pl.BlockSpec(memory_space=pl.ANY if index in sent else pltpu.VMEM) for index in range(len(out_shapes))
        ],
        scratch_shapes=[pltpu.VMEM(shape, F32) if isinstance(shape, tuple) else shape for shape in scratch],
        compiler_params=pltpu.CompilerParams(vmem_limit_bytes=24 << 20),
    )(*operands)


def restrict(field, labels):
    rows = []
    for label in range(LABELS):
        kept = jnp.sum(jnp.where(labels == label + 1.0, field, 0.0), axis=0)
        rows.append(jnp.sum(kept, axis=0, keepdims=True))
    sums = jnp.concatenate(rows, 0)
    even = lanes((8, 128)) % 2 == 0
    return sums + jnp.where(even, pltpu.roll(sums, 127, 1), pltpu.roll(sums, 1, 1))


def prolong(coarse, labels):
    row = lax.broadcasted_iota(jnp.int32, (16, 128), 0)
    field = jnp.zeros_like(labels)
    for label in range(LABELS):
        low, own, high = [coarse[step, label : label + 1, :] for step in range(3)]
        values = jnp.where(row < 3, low, jnp.where(row < 9, own, high))
        field = jnp.where(labels == label + 1.0, values[None], field)
    return field


def assemble(product_of, total_ref):
    total_ref[...] = jnp.zeros_like(total_ref)
    start = lanes((16, 128)) == 0
    for i in SPAN:
        low_a, high_a = {-1: (3, 4), 0: (0, 4), 1: (0, 3)}[i]
        for j in SPAN:
            product = product_of((i + 1) * 3 + j + 1)
            last = pltpu.roll(product[48:64], 1, 1)
            pieces = [
                product[0:16] + jnp.where(start, 0.0, last),
                product[16:32],
                product[32:48],
            ]
            for c in range(3):
                for b in range(4):
                    y = 3 * j + b
                    if 0 <= y < 6:
                        x = 3 * i + low_a
                        rows = pieces[c][4 * b + low_a : 4 * b + high_a]
                        total_ref[c * 6 + y, x : x + high_a - low_a, :] += rows


def unpack_kernel(source_hbm, potential_hbm, map_hbm, region_hbm, table_hbm, r_ref, ionic_ref, label_ref, coarse_ref,
                  own_ref, beside_ref,
                  rows_ref, turned_ref, source_ref, potential_ref, map_ref, region_ref, table_ref, sems):
    copies = [
        pltpu.make_async_copy(away, here, sems.at[index])
        for index, (away, here) in enumerate(
            (
                (source_hbm, source_ref),
                (potential_hbm, potential_ref),
                (map_hbm, map_ref),
                (region_hbm, region_ref),
                (table_hbm, table_ref),
            )
        )
    ]
    for copy in copies:
        copy.start()
    rows_ref[...] = jnp.zeros_like(rows_ref)
    for copy in copies:
        copy.wait()
    for i in range(2):
        region = region_ref[i]
        sigma = jnp.zeros(region.shape, F32)
        for index in range(4):
            sigma = jnp.where(region == index, table_ref[index], sigma)
        own_ref[2 * i : 2 * i + 2, :] = sigma
    beside_ref[0:1, :] = own_ref[1:2, :]
    beside_ref[1:2, :] = own_ref[3:4, :]
    for y in range(6):
        for x in range(6):
            row = y * 6 + x
            rows_ref[row : row + 1, :] = source_ref[x, y : y + 1, :]
            rows_ref[36 + row : 37 + row, :] = potential_ref[x, y : y + 1, :]
            rows_ref[72 + row : 73 + row, :] = map_ref[x, y : y + 1, :].astype(F32)
    for piece in range(3):
        turned_ref[128 * piece : 128 * piece + 128, :] = rows_ref[:, 128 * piece : 128 * piece + 128].T
    r_ref[...] = jnp.zeros_like(r_ref)
    ionic_ref[...] = jnp.zeros_like(ionic_ref)
    label_ref[...] = jnp.zeros_like(label_ref)
    for c in range(3):
        split = turned_ref[pl.ds(c, 128, stride=3), :].T
        for y in range(6):
            r_ref[c * 6 + y, 0:6, :] = split[6 * y : 6 * y + 6]
            tangent = jnp.tanh(split[36 + 6 * y : 42 + 6 * y])
            ionic_ref[c * 6 + y, 0:6, :] = 1.0 + 2.0 * (1.0 - tangent * tangent)
            label_ref[c * 6 + y, 0:6, :] = split[72 + 6 * y : 78 + 6 * y] + 1.0
    coarse_ref[...] = restrict(r_ref[...], label_ref[...])


def send_slab(even, fields, near_ref, far_ref, up_ref, down_ref):
    up_ref[...] = jnp.zeros_like(up_ref)
    down_ref[...] = jnp.zeros_like(down_ref)
    for index, field_ref in enumerate(fields):
        for n in range(18):
            row = 56 * index + 3 * n
            up_ref[row : row + 3, :] = field_ref[n, 3:6, :]
            down_ref[56 * index + n : 56 * index + n + 1, :] = field_ref[n, 0:1, :]
    near_ref[...] = jnp.where(even, up_ref[...], down_ref[...])
    far_ref[...] = jnp.where(even, down_ref[...], up_ref[...])


def diagonal_kernel(place_ref, own_ref, beside_ref, below_ref, matrix_ref, r_ref, ionic_ref, label_ref, coarse_ref,
                    sigma_ref, diagonal_ref, scaled_ref, message_ref, near_ref, far_ref,
                    total_ref, up_ref, down_ref, copies_ref, sem):
    sigma_ref[0:3, :] = below_ref[...]
    for i in range(2):
        sigma_ref[3 + 3 * i : 4 + 3 * i, :] = beside_ref[i : i + 1, :]
        sigma_ref[4 + 3 * i : 6 + 3 * i, :] = own_ref[2 * i : 2 * i + 2, :]
    square = (64, 64)
    eye = lax.broadcasted_iota(jnp.int32, square, 0) == lax.broadcasted_iota(jnp.int32, square, 1)
    corner = jnp.sum(jnp.where(eye, matrix_ref[...], 0.0), axis=1, keepdims=True)
    assemble(lambda e: corner * sigma_ref[e : e + 1, :], total_ref)
    labels = label_ref[...]
    diagonal = jnp.where(labels == 0.0, 1.0, total_ref[...] + ionic_ref[...])
    diagonal_ref[...] = diagonal
    coarse_diag = SHARE * restrict(diagonal, labels)
    even = lanes((8, 128)) % 2 == 0
    message = jnp.where(even, coarse_ref[...], coarse_diag)
    copies_ref[...] = jnp.broadcast_to(message[None], copies_ref.shape)
    sending = pltpu.make_async_copy(copies_ref, message_ref, sem)
    sending.start()
    scaled_ref[...] = r_ref[...] / diagonal
    send_slab(place_ref[1] == 0, (scaled_ref, label_ref), near_ref, far_ref, up_ref, down_ref)
    sending.wait()


def along(values):
    lane = lanes(values.shape)
    row = lax.broadcasted_iota(jnp.int32, values.shape, 1)
    after = pltpu.roll(values, 7, 1)
    carried = jnp.where(lane < 126, pltpu.roll(after, 126, 2), 0.0)
    after = jnp.where(row == 7, carried, after)
    before = pltpu.roll(values, 1, 1)
    carried = jnp.where(lane >= 2, pltpu.roll(before, 2, 2), 0.0)
    return after + jnp.where(row == 0, carried, before)


def smooth(start, valid):
    level = start
    for sweep in range(REACH):
        beside = level[2:] + level[:-2] + along(level[1:-1])
        here = slice(sweep + 1, 2 * NEAR - sweep)
        level = start[here] + (1.0 - DAMPING) * level[1:-1] + (DAMPING * COUPLING) * beside
        level = level * valid[here]
    return level


def around(place_ref, count):
    rows, valid = [], []
    for step in range(-NEAR, NEAR + 1):
        row = place_ref[0] + step
        inside = jnp.logical_and(row >= 0, row < count)
        rows.append(jnp.clip(row, 0, count - 1))
        valid.append(jnp.where(inside, jnp.ones((1, 8, 128), F32), 0.0))
    return rows, jnp.concatenate(valid, 0)


def even_part(tiles):
    even = lanes(tiles.shape) % 2 == 0
    return jnp.where(even, tiles, pltpu.roll(tiles, 1, tiles.ndim - 1))


def odd_part(tiles):
    even = lanes(tiles.shape) % 2 == 0
    return jnp.where(even, pltpu.roll(tiles, 127, tiles.ndim - 1), tiles)


def widen(field_ref, low, high, start, wide_ref):
    wide_ref[...] = jnp.zeros_like(wide_ref)
    for n in range(18):
        wide_ref[n, 0:3, :] = low[start + 3 * n : start + 3 * n + 3]
        wide_ref[n, 3:9, :] = field_ref[n, 0:6, :]
        wide_ref[n, 9:10, :] = high[start + n : start + n + 1]


def send_cross(even, wide_ref, own_ref, near_ref, far_ref, up_ref, down_ref):
    own_ref[...] = jnp.zeros_like(own_ref)
    for n in range(18):
        own_ref[n, 0:6, :] = wide_ref[n, 3:9, :]
    up_ref[...] = jnp.zeros_like(up_ref)
    down_ref[...] = jnp.zeros_like(down_ref)
    for c in range(3):
        for y in range(3):
            row = (3 * c + y) * 10
            up_ref[row : row + 10, :] = wide_ref[6 * c + 3 + y, 0:10, :]
        down_ref[10 * c : 10 * c + 10, :] = wide_ref[6 * c, 0:10, :]
    near_ref[...] = jnp.where(even, up_ref[...], down_ref[...])
    far_ref[...] = jnp.where(even, down_ref[...], up_ref[...])


def arrived(even, near_ref, far_ref):
    return jnp.where(even, far_ref[...], near_ref[...]), jnp.where(even, near_ref[...], far_ref[...])


def first_solve_kernel(place_ref, gathered_ref, scaled_ref, label_ref, left_ref, right_ref,
                       wide_ref, z_ref, near_ref, far_ref, scale_ref, wide_label_ref, up_ref, down_ref):
    low, high = arrived(place_ref[1] == 0, right_ref, left_ref)
    rows, valid = around(place_ref, gathered_ref.shape[0])
    tiles = jnp.concatenate([gathered_ref[pl.ds(row, 1)] for row in rows], 0)
    sums = jnp.sum(gathered_ref[...], axis=0)
    inverse = valid / jnp.sqrt(odd_part(tiles))
    share = 1.0 / odd_part(sums)
    scale_ref[0 : 2 * NEAR + 1] = inverse
    scale_ref[2 * NEAR + 1] = share
    level = smooth(DAMPING * even_part(tiles) * inverse, valid)
    coarse = level * inverse[REACH : REACH + 3] + (even_part(sums) * share)[None]
    widen(label_ref, low, high, 56, wide_label_ref)
    widen(scaled_ref, low, high, 0, wide_ref)
    wide_ref[...] += prolong(coarse, wide_label_ref[...])
    send_cross(place_ref[2] == 0, wide_ref, z_ref, near_ref, far_ref, up_ref, down_ref)


def next_solve_kernel(place_ref, gathered_ref, scaled_ref, wide_label_ref, left_ref, right_ref, scale_ref,
                      wide_ref, w_ref, near_ref, far_ref, up_ref, down_ref):
    low, high = arrived(place_ref[1] == 0, right_ref, left_ref)
    rows, valid = around(place_ref, gathered_ref.shape[0])
    tiles = jnp.concatenate([gathered_ref[pl.ds(row, 1)] for row in rows], 0)
    sums = jnp.sum(gathered_ref[...], axis=0)
    inverse = scale_ref[0 : 2 * NEAR + 1]
    level = smooth(DAMPING * tiles * inverse, valid)
    coarse = level * inverse[REACH : REACH + 3] + (sums * scale_ref[2 * NEAR + 1])[None]
    widen(scaled_ref, low, high, 0, wide_ref)
    wide_ref[...] += prolong(coarse, wide_label_ref[...])
    send_cross(place_ref[2] == 0, wide_ref, w_ref, near_ref, far_ref, up_ref, down_ref)


def operate(place_ref, wide_ref, field_ref, near_ref, far_ref, sigma_ref, matrix_ref, ionic_ref,
            grid_ref, local_ref, product_ref, total_ref):
    for n in range(18):
        grid_ref[n // 6 * 10 + 3 + n % 6, 0:10, :] = wide_ref[n, 0:10, :]

    above, under = arrived(place_ref[2] == 0, near_ref, far_ref)
    for c in range(3):
        for y in range(3):
            row = (3 * c + y) * 10
            grid_ref[10 * c + y, 0:10, :] = above[row : row + 10]
        grid_ref[10 * c + 9, 0:10, :] = under[10 * c : 10 * c + 10]
    end = lanes((10, 128)) == 127
    for y in range(10):
        grid_ref[30 + y, 0:10, :] = jnp.where(end, 0.0, pltpu.roll(grid_ref[y, 0:10, :], 127, 1))
    for i in SPAN:
        for j in SPAN:
            left = ((i + 1) * 3 + j + 1) * 128
            for c in range(4):
                for b in range(4):
                    row = 16 * c + 4 * b
                    n = c * 10 + 3 * (j + 1) + b
                    local_ref[row : row + 4, left : left + 128] = grid_ref[n, 3 * i + 3 : 3 * i + 7, :]
    matrix = matrix_ref[...]
    matrix_high = matrix.astype(BF16)
    matrix_low = (matrix - matrix_high.astype(F32)).astype(BF16)
    local = local_ref[...]
    high = local.astype(BF16)
    low = (local - high.astype(F32)).astype(BF16)
    dot = functools.partial(jnp.dot, preferred_element_type=F32)
    product_ref[...] = dot(matrix_high, high) + (dot(matrix_high, low) + dot(matrix_low, high))
    assemble(lambda e: product_ref[:, 128 * e : 128 * e + 128] * sigma_ref[e : e + 1, :], total_ref)
    return total_ref[...] + ionic_ref[...] * field_ref[...]


def first_image_kernel(place_ref, wide_ref, z_ref, far_ref, near_ref, sigma_ref, matrix_ref, ionic_ref, diagonal_ref, label_ref,
                       q_ref, scaled_ref, message_ref, left_ref, right_ref, up_ref, down_ref, copies_ref, sem, *scratch):
    image = operate(place_ref, wide_ref, z_ref, near_ref, far_ref, sigma_ref, matrix_ref, ionic_ref, *scratch)
    q_ref[...] = image
    copies_ref[...] = jnp.broadcast_to(restrict(image, label_ref[...])[None], copies_ref.shape)
    sending = pltpu.make_async_copy(copies_ref, message_ref, sem)
    sending.start()
    scaled_ref[...] = image / diagonal_ref[...]
    send_slab(place_ref[1] == 0, (scaled_ref,), left_ref, right_ref, up_ref, down_ref)
    sending.wait()


def next_image_kernel(place_ref, wide_ref, w_ref, far_ref, near_ref, sigma_ref, matrix_ref, ionic_ref,
                      r_ref, z_ref, q_ref, t_ref, message_ref, *scratch):
    image = operate(place_ref, wide_ref, w_ref, near_ref, far_ref, sigma_ref, matrix_ref, ionic_ref, *scratch)
    t_ref[...] = image
    r, z, q, w = r_ref[...], z_ref[...], q_ref[...], w_ref[...]
    row = jnp.zeros((1, 128), F32)
    for index, (left, right) in enumerate(((r, z), (z, q), (r, w), (q, w), (z, image), (w, image))):
        part = jnp.sum(jnp.sum(left * right, axis=0), axis=0, keepdims=True)
        row = jnp.where(lanes((1, 128)) == index, jnp.sum(part, axis=1, keepdims=True), row)
    message_ref[...] = jnp.broadcast_to(row[None], message_ref.shape)


def finish_kernel(dots_ref, r_ref, z_ref, q_ref, w_ref, t_ref, solution_ref, residual_ref, rows_ref, turned_ref):
    dots = jnp.sum(dots_ref[...], axis=0)
    rz, zq, rw, qw, zt, wt = [dots[:, index : index + 1] for index in range(6)]
    alpha = rz / zq
    rz_next = alpha * (alpha * qw - rw)
    beta = rz_next / rz
    more = 1.0 + beta
    second = rz_next / (more * more * zq - more * alpha * (zt + qw) + alpha * alpha * wt)
    from_z = alpha + second * more
    from_w = second * alpha
    rows_ref[...] = jnp.zeros_like(rows_ref)
    for c in range(3):
        for y in range(6):
            n = 6 * c + y
            answer = from_z * z_ref[n] - from_w * w_ref[n]
            left = r_ref[n] - from_z * q_ref[n] + from_w * t_ref[n]
            rows_ref[6 * y : 6 * y + 6, :] = answer[0:6]
            rows_ref[36 + 6 * y : 42 + 6 * y, :] = left[0:6]
        turned_ref[pl.ds(c, 128, stride=3), :] = rows_ref[...].T
    for piece in range(3):
        back = turned_ref[128 * piece : 128 * piece + 128, :].T
        for y in range(6):
            for x in range(6):
                row = y * 6 + x
                solution_ref[x, y : y + 1, 128 * piece : 128 * piece + 128] = back[row : row + 1]
                residual_ref[x, y : y + 1, 128 * piece : 128 * piece + 128] = back[36 + row : 37 + row]


def body(adjoint_source, potential, element_matrix, region_labels, conductivity, restriction_map):
    n_slab = lax.axis_size("slab")
    n_cross = lax.axis_size("cross")
    slab, cross = lax.axis_index("slab"), lax.axis_index("cross")
    place = jnp.stack([slab, slab % 2, cross % 2]).astype(jnp.int32)
    columns = [
        [slab * n_cross + cross for slab in (2 * pair, 2 * pair + 1) for cross in range(n_cross)]
        for pair in range(n_slab // 2)
    ]
    planes = [[2 * pair + low for pair in range(n_slab // 2)] for low in range(2)]
    def shifted(value, axis, step):
        count = lax.axis_size(axis)
        pairs = [(source, source + step) for source in range(count) if 0 <= source + step < count]
        return lax.ppermute(value, axis, pairs)

    def gather(copies):
        return lax.all_to_all(copies, "slab", 0, 0, tiled=True)

    field, wide = (18, 8, 128), (18, 16, 128)
    space = [(40, 16, 128), (64, 1152), (64, 1152), field]
    r, ionic, labels, coarse, own, beside = call(
        unpack_kernel, [field] * 3 + [(8, 128), (4, 128), (2, 128)],
        [(128, 384), (384, 128), (6, 6, 384), (6, 6, 384), pltpu.VMEM((6, 6, 384), jnp.int32),
         pltpu.VMEM((2, 2, 128), jnp.int32), pltpu.SMEM((4,), F32), pltpu.SemaphoreType.DMA((5,))],
        adjoint_source, potential, restriction_map, region_labels, conductivity, away=(0, 1, 2, 3, 4),
    )
    beside = shifted(beside, "cross", 1)
    below = shifted(jnp.concatenate([beside[1:2], own[2:4]], 0), "slab", 1)
    copies = [(n_slab, 8, 128), pltpu.SemaphoreType.DMA]
    sigma, diagonal, scaled, message, near, far = call(
        diagonal_kernel, [(9, 128), field, field, (n_slab, 8, 128), (112, 128), (112, 128)],
        [field, (112, 128), (112, 128), *copies],
        place, own, beside, below, element_matrix, r, ionic, labels, coarse, smem=(0,), sent=(3,),
    )

    def exchange(near, far, axis):
        count = lax.axis_size(axis)
        far_pairs = [(c, c + 1) for c in range(1, count - 1, 2)]
        far_pairs += [(above, c) for c, above in far_pairs]
        far = lax.ppermute(far, axis, far_pairs)
        return far, lax.ppermute(near, axis, [(c, c ^ 1) for c in range(count)])

    faces = [(96, 128), (96, 128)]
    wide_z, z, near, far, scale, wide_labels = call(
        first_solve_kernel, [wide, field, *faces, (10, 8, 128), wide], faces,
        place, gather(message), scaled, labels, *exchange(near, far, "slab"), smem=(0,),
    )
    q, scaled, message, near, far = call(
        first_image_kernel, [field, field, (n_slab, 8, 128), (56, 128), (56, 128)],
        [(56, 128), (56, 128), *copies, *space],
        place, wide_z, z, *exchange(near, far, "cross"), sigma, element_matrix, ionic, diagonal, labels,
        smem=(0,), sent=(2,),
    )
    wide_w, w, near, far = call(
        next_solve_kernel, [wide, field, *faces], faces,
        place, gather(message), scaled, wide_labels, *exchange(near, far, "slab"), scale, smem=(0,),
    )
    t, message = call(
        next_image_kernel, [field, (n_slab // 2, 1, 128)], space,
        place, wide_w, w, *exchange(near, far, "cross"), sigma, element_matrix, ionic, r, z, q, smem=(0,),
    )
    parts = lax.all_to_all(message, "slab", 0, 0, axis_index_groups=planes, tiled=True)
    parts = jnp.broadcast_to(jnp.sum(parts, 0)[None], (2 * n_cross, 1, 128))
    dots = lax.all_to_all(parts, ("slab", "cross"), 0, 0, axis_index_groups=columns, tiled=True)
    return tuple(call(finish_kernel, [(6, 6, 384)] * 2, [(128, 128), (384, 128)], dots, r, z, q, w, t))


def solution(mesh):
    return jax.shard_map(
        body,
        mesh=mesh,
        in_specs=(
            P("slab", "cross", None),
            P("slab", "cross", None),
            P(),
            P("slab", "cross", None),
            P(),
            P("slab", "cross", None),
        ),
        out_specs=(P("slab", "cross", None), P("slab", "cross", None)),
        check_vma=False,
    )
```

```python
import functools

import jax
import jax.numpy as jnp
from jax import lax
from jax.experimental import pallas as pl
from jax.experimental.pallas import tpu as pltpu
from jax.sharding import PartitionSpec as P

LABELS = 8
DAMPING = 0.8
COUPLING = 0.2
SHARE = 0.1
REACH = 3
NEAR = REACH + 1


F32 = jnp.float32
BF16 = jnp.bfloat16
SPAN = (-1, 0, 1)


def lanes(shape):
    return lax.broadcasted_iota(jnp.int32, shape, len(shape) - 1)


def call(kernel, out_shapes, scratch, *operands, smem=(), away=()):
    specs = [
        pl.BlockSpec(memory_space=pltpu.SMEM if index in smem else pltpu.HBM if index in away else pltpu.VMEM)
        for index in range(len(operands))
    ]
    operands = [
        pltpu.with_memory_space_constraint(operand, pltpu.HBM) if index in away else operand
        for index, operand in enumerate(operands)
    ]
    return pl.pallas_call(
        kernel,
        out_shape=[jax.ShapeDtypeStruct(shape, F32) for shape in out_shapes],
        in_specs=specs,
        out_specs=[pl.BlockSpec(memory_space=pltpu.VMEM)] * len(out_shapes),
        scratch_shapes=[pltpu.VMEM(shape, F32) if isinstance(shape, tuple) else shape for shape in scratch],
        compiler_params=pltpu.CompilerParams(vmem_limit_bytes=24 << 20),
    )(*operands)


def restrict(field, labels):
    rows = []
    for label in range(LABELS):
        kept = jnp.sum(jnp.where(labels == label + 1.0, field, 0.0), axis=0)
        rows.append(jnp.sum(kept, axis=0, keepdims=True))
    sums = jnp.concatenate(rows, 0)
    even = lanes((8, 128)) % 2 == 0
    return sums + jnp.where(even, pltpu.roll(sums, 127, 1), pltpu.roll(sums, 1, 1))


def prolong(coarse, labels):
    row = lax.broadcasted_iota(jnp.int32, (16, 128), 0)
    field = jnp.zeros_like(labels)
    for label in range(LABELS):
        low, own, high = [coarse[step, label : label + 1, :] for step in range(3)]
        values = jnp.where(row < 3, low, jnp.where(row < 9, own, high))
        field = jnp.where(labels == label + 1.0, values[None], field)
    return field


def assemble(product_of, total_ref):
    total_ref[...] = jnp.zeros_like(total_ref)
    start = lanes((16, 128)) == 0
    for i in SPAN:
        low_a, high_a = {-1: (3, 4), 0: (0, 4), 1: (0, 3)}[i]
        for j in SPAN:
            product = product_of((i + 1) * 3 + j + 1)
            last = pltpu.roll(product[48:64], 1, 1)
            pieces = [
                product[0:16] + jnp.where(start, 0.0, last),
                product[16:32],
                product[32:48],
            ]
            for c in range(3):
                for b in range(4):
                    y = 3 * j + b
                    if 0 <= y < 6:
                        x = 3 * i + low_a
                        rows = pieces[c][4 * b + low_a : 4 * b + high_a]
                        total_ref[c * 6 + y, x : x + high_a - low_a, :] += rows


def conductance(region, table_ref):
    value = jnp.zeros(region.shape, F32)
    for index in range(4):
        value = jnp.where(region == index + 1, table_ref[index : index + 1, :], value)
    return value


def unpack_kernel(source_hbm, potential_hbm, map_hbm, region_hbm, table_hbm, r_ref, ionic_ref, label_ref, coarse_ref,
                  own_ref, table_ref,
                  rows_ref, turned_ref, source_ref, potential_ref, map_ref, region_ref, values_ref, sems):
    copies = [
        pltpu.make_async_copy(away, here, sems.at[index])
        for index, (away, here) in enumerate(
            (
                (source_hbm, source_ref),
                (potential_hbm, potential_ref),
                (map_hbm, map_ref),
                (region_hbm, region_ref),
                (table_hbm, values_ref),
            )
        )
    ]
    for copy in copies:
        copy.start()
    rows_ref[...] = jnp.zeros_like(rows_ref)
    for copy in copies:
        copy.wait()
    for index in range(4):
        table_ref[index : index + 1, :] = jnp.full((1, 128), values_ref[index])
    for i in range(2):
        own_ref[2 * i : 2 * i + 2, :] = conductance(region_ref[i] + 1, table_ref)
    for y in range(6):
        for x in range(6):
            row = y * 6 + x
            rows_ref[row : row + 1, :] = source_ref[x, y : y + 1, :]
            rows_ref[36 + row : 37 + row, :] = potential_ref[x, y : y + 1, :]
            rows_ref[72 + row : 73 + row, :] = map_ref[x, y : y + 1, :].astype(F32)
    for piece in range(3):
        turned_ref[128 * piece : 128 * piece + 128, :] = rows_ref[:, 128 * piece : 128 * piece + 128].T
    r_ref[...] = jnp.zeros_like(r_ref)
    ionic_ref[...] = jnp.zeros_like(ionic_ref)
    label_ref[...] = jnp.zeros_like(label_ref)
    for c in range(3):
        split = turned_ref[pl.ds(c, 128, stride=3), :].T
        for y in range(6):
            r_ref[c * 6 + y, 0:6, :] = split[6 * y : 6 * y + 6]
            tangent = jnp.tanh(split[36 + 6 * y : 42 + 6 * y])
            ionic_ref[c * 6 + y, 0:6, :] = 1.0 + 2.0 * (1.0 - tangent * tangent)
            label_ref[c * 6 + y, 0:6, :] = split[72 + 6 * y : 78 + 6 * y] + 1.0
    coarse_ref[...] = restrict(r_ref[...], label_ref[...])


def send_slab(even, fields, near_ref, far_ref, up_ref, down_ref):
    up_ref[...] = jnp.zeros_like(up_ref)
    down_ref[...] = jnp.zeros_like(down_ref)
    for index, field_ref in enumerate(fields):
        for n in range(18):
            row = 56 * index + 3 * n
            up_ref[row : row + 3, :] = field_ref[n, 3:6, :]
            down_ref[56 * index + n : 56 * index + n + 1, :] = field_ref[n, 0:1, :]
    near_ref[...] = jnp.where(even, up_ref[...], down_ref[...])
    far_ref[...] = jnp.where(even, down_ref[...], up_ref[...])


def diagonal_kernel(place_ref, corner_ref, below_ref, beside_ref, own_ref, table_ref, matrix_ref, r_ref, ionic_ref, label_ref, coarse_ref,
                    sigma_ref, diagonal_ref, scaled_ref, message_ref, near_ref, far_ref,
                    total_ref, up_ref, down_ref):
    sigma_ref[0:1, :] = conductance(corner_ref[...], table_ref)
    sigma_ref[1:3, :] = conductance(below_ref[...], table_ref)
    for i in range(2):
        sigma_ref[3 + 3 * i : 4 + 3 * i, :] = conductance(beside_ref[i : i + 1, :], table_ref)
        sigma_ref[4 + 3 * i : 6 + 3 * i, :] = own_ref[2 * i : 2 * i + 2, :]
    square = (64, 64)
    eye = lax.broadcasted_iota(jnp.int32, square, 0) == lax.broadcasted_iota(jnp.int32, square, 1)
    corner = jnp.sum(jnp.where(eye, matrix_ref[...], 0.0), axis=1, keepdims=True)
    assemble(lambda e: corner * sigma_ref[e : e + 1, :], total_ref)
    labels = label_ref[...]
    diagonal = jnp.where(labels == 0.0, 1.0, total_ref[...] + ionic_ref[...])
    diagonal_ref[...] = diagonal
    coarse_diag = SHARE * restrict(diagonal, labels)
    even = lanes((8, 128)) % 2 == 0
    message = jnp.where(even, coarse_ref[...], coarse_diag)
    message_ref[...] = jnp.broadcast_to(message[None], message_ref.shape)
    scaled_ref[...] = r_ref[...] / diagonal
    send_slab(place_ref[1] == 0, (scaled_ref, label_ref), near_ref, far_ref, up_ref, down_ref)


def along(values):
    lane = lanes(values.shape)
    row = lax.broadcasted_iota(jnp.int32, values.shape, 1)
    after = pltpu.roll(values, 7, 1)
    carried = jnp.where(lane < 126, pltpu.roll(after, 126, 2), 0.0)
    after = jnp.where(row == 7, carried, after)
    before = pltpu.roll(values, 1, 1)
    carried = jnp.where(lane >= 2, pltpu.roll(before, 2, 2), 0.0)
    return after + jnp.where(row == 0, carried, before)


def smooth(start, valid):
    level = start
    for sweep in range(REACH):
        beside = level[2:] + level[:-2] + along(level[1:-1])
        here = slice(sweep + 1, 2 * NEAR - sweep)
        level = start[here] + (1.0 - DAMPING) * level[1:-1] + (DAMPING * COUPLING) * beside
        level = level * valid[here]
    return level


def around(place_ref, count):
    rows, valid = [], []
    for step in range(-NEAR, NEAR + 1):
        row = place_ref[0] + step
        inside = jnp.logical_and(row >= 0, row < count)
        rows.append(jnp.clip(row, 0, count - 1))
        valid.append(jnp.where(inside, jnp.ones((1, 8, 128), F32), 0.0))
    return rows, jnp.concatenate(valid, 0)


def even_part(tiles):
    even = lanes(tiles.shape) % 2 == 0
    return jnp.where(even, tiles, pltpu.roll(tiles, 1, tiles.ndim - 1))


def odd_part(tiles):
    even = lanes(tiles.shape) % 2 == 0
    return jnp.where(even, pltpu.roll(tiles, 127, tiles.ndim - 1), tiles)


def widen(field_ref, low, high, start, wide_ref):
    wide_ref[...] = jnp.zeros_like(wide_ref)
    for n in range(18):
        wide_ref[n, 0:3, :] = low[start + 3 * n : start + 3 * n + 3]
        wide_ref[n, 3:9, :] = field_ref[n, 0:6, :]
        wide_ref[n, 9:10, :] = high[start + n : start + n + 1]


def send_cross(even, wide_ref, own_ref, near_ref, far_ref, up_ref, down_ref):
    own_ref[...] = jnp.zeros_like(own_ref)
    for n in range(18):
        own_ref[n, 0:6, :] = wide_ref[n, 3:9, :]
    up_ref[...] = jnp.zeros_like(up_ref)
    down_ref[...] = jnp.zeros_like(down_ref)
    for c in range(3):
        for y in range(3):
            row = (3 * c + y) * 10
            up_ref[row : row + 10, :] = wide_ref[6 * c + 3 + y, 0:10, :]
        down_ref[10 * c : 10 * c + 10, :] = wide_ref[6 * c, 0:10, :]
    near_ref[...] = jnp.where(even, up_ref[...], down_ref[...])
    far_ref[...] = jnp.where(even, down_ref[...], up_ref[...])


def arrived(even, near_ref, far_ref):
    return jnp.where(even, far_ref[...], near_ref[...]), jnp.where(even, near_ref[...], far_ref[...])


def first_solve_kernel(place_ref, gathered_ref, scaled_ref, label_ref, left_ref, right_ref,
                       wide_ref, z_ref, near_ref, far_ref, scale_ref, wide_label_ref, up_ref, down_ref):
    low, high = arrived(place_ref[1] == 0, left_ref, right_ref)
    rows, valid = around(place_ref, gathered_ref.shape[0])
    tiles = jnp.concatenate([gathered_ref[pl.ds(row, 1)] for row in rows], 0)
    sums = jnp.sum(gathered_ref[...], axis=0)
    inverse = valid / jnp.sqrt(odd_part(tiles))
    share = 1.0 / odd_part(sums)
    scale_ref[0 : 2 * NEAR + 1] = inverse
    scale_ref[2 * NEAR + 1] = share
    level = smooth(DAMPING * even_part(tiles) * inverse, valid)
    coarse = level * inverse[REACH : REACH + 3] + (even_part(sums) * share)[None]
    widen(label_ref, low, high, 56, wide_label_ref)
    widen(scaled_ref, low, high, 0, wide_ref)
    wide_ref[...] += prolong(coarse, wide_label_ref[...])
    send_cross(place_ref[2] == 0, wide_ref, z_ref, near_ref, far_ref, up_ref, down_ref)


def next_solve_kernel(place_ref, gathered_ref, scaled_ref, wide_label_ref, left_ref, right_ref, scale_ref,
                      wide_ref, w_ref, near_ref, far_ref, up_ref, down_ref):
    low, high = arrived(place_ref[1] == 0, left_ref, right_ref)
    rows, valid = around(place_ref, gathered_ref.shape[0])
    tiles = jnp.concatenate([gathered_ref[pl.ds(row, 1)] for row in rows], 0)
    sums = jnp.sum(gathered_ref[...], axis=0)
    inverse = scale_ref[0 : 2 * NEAR + 1]
    level = smooth(DAMPING * tiles * inverse, valid)
    coarse = level * inverse[REACH : REACH + 3] + (sums * scale_ref[2 * NEAR + 1])[None]
    widen(scaled_ref, low, high, 0, wide_ref)
    wide_ref[...] += prolong(coarse, wide_label_ref[...])
    send_cross(place_ref[2] == 0, wide_ref, w_ref, near_ref, far_ref, up_ref, down_ref)


def operate(place_ref, wide_ref, field_ref, near_ref, far_ref, sigma_ref, matrix_ref, ionic_ref,
            grid_ref, local_ref, product_ref, total_ref):
    for n in range(18):
        grid_ref[n // 6 * 10 + 3 + n % 6, 0:10, :] = wide_ref[n, 0:10, :]

    above, under = arrived(place_ref[2] == 0, near_ref, far_ref)
    for c in range(3):
        for y in range(3):
            row = (3 * c + y) * 10
            grid_ref[10 * c + y, 0:10, :] = above[row : row + 10]
        grid_ref[10 * c + 9, 0:10, :] = under[10 * c : 10 * c + 10]
    end = lanes((10, 128)) == 127
    for y in range(10):
        grid_ref[30 + y, 0:10, :] = jnp.where(end, 0.0, pltpu.roll(grid_ref[y, 0:10, :], 127, 1))
    for i in SPAN:
        for j in SPAN:
            left = ((i + 1) * 3 + j + 1) * 128
            for c in range(4):
                for b in range(4):
                    row = 16 * c + 4 * b
                    n = c * 10 + 3 * (j + 1) + b
                    local_ref[row : row + 4, left : left + 128] = grid_ref[n, 3 * i + 3 : 3 * i + 7, :]
    matrix = matrix_ref[...]
    matrix_high = matrix.astype(BF16)
    matrix_low = (matrix - matrix_high.astype(F32)).astype(BF16)
    local = local_ref[...]
    high = local.astype(BF16)
    low = (local - high.astype(F32)).astype(BF16)
    dot = functools.partial(jnp.dot, preferred_element_type=F32)
    product_ref[...] = dot(matrix_high, high) + (dot(matrix_high, low) + dot(matrix_low, high))
    assemble(lambda e: product_ref[:, 128 * e : 128 * e + 128] * sigma_ref[e : e + 1, :], total_ref)
    return total_ref[...] + ionic_ref[...] * field_ref[...]


def first_image_kernel(place_ref, wide_ref, z_ref, far_ref, near_ref, sigma_ref, matrix_ref, ionic_ref, diagonal_ref, label_ref,
                       q_ref, scaled_ref, message_ref, left_ref, right_ref, up_ref, down_ref, *scratch):
    image = operate(place_ref, wide_ref, z_ref, near_ref, far_ref, sigma_ref, matrix_ref, ionic_ref, *scratch)
    q_ref[...] = image
    message_ref[...] = jnp.broadcast_to(restrict(image, label_ref[...])[None], message_ref.shape)
    scaled_ref[...] = image / diagonal_ref[...]
    send_slab(place_ref[1] == 0, (scaled_ref,), left_ref, right_ref, up_ref, down_ref)


def next_image_kernel(place_ref, wide_ref, w_ref, far_ref, near_ref, sigma_ref, matrix_ref, ionic_ref,
                      r_ref, z_ref, q_ref, t_ref, message_ref, *scratch):
    image = operate(place_ref, wide_ref, w_ref, near_ref, far_ref, sigma_ref, matrix_ref, ionic_ref, *scratch)
    t_ref[...] = image
    r, z, q, w = r_ref[...], z_ref[...], q_ref[...], w_ref[...]
    row = jnp.zeros((1, 128), F32)
    for index, (left, right) in enumerate(((r, z), (z, q), (r, w), (q, w), (z, image), (w, image))):
        part = jnp.sum(jnp.sum(left * right, axis=0), axis=0, keepdims=True)
        row = jnp.where(lanes((1, 128)) == index, jnp.sum(part, axis=1, keepdims=True), row)
    message_ref[...] = jnp.broadcast_to(row[None], message_ref.shape)


def finish_kernel(dots_ref, r_ref, z_ref, q_ref, w_ref, t_ref, solution_ref, residual_ref, rows_ref, turned_ref):
    dots = jnp.sum(dots_ref[...], axis=0)
    rz, zq, rw, qw, zt, wt = [dots[:, index : index + 1] for index in range(6)]
    alpha = rz / zq
    rz_next = alpha * (alpha * qw - rw)
    beta = rz_next / rz
    more = 1.0 + beta
    second = rz_next / (more * more * zq - more * alpha * (zt + qw) + alpha * alpha * wt)
    from_z = alpha + second * more
    from_w = second * alpha
    rows_ref[...] = jnp.zeros_like(rows_ref)
    for c in range(3):
        for y in range(6):
            n = 6 * c + y
            answer = from_z * z_ref[n] - from_w * w_ref[n]
            left = r_ref[n] - from_z * q_ref[n] + from_w * t_ref[n]
            rows_ref[6 * y : 6 * y + 6, :] = answer[0:6]
            rows_ref[36 + 6 * y : 42 + 6 * y, :] = left[0:6]
        turned_ref[pl.ds(c, 128, stride=3), :] = rows_ref[...].T
    for piece in range(3):
        back = turned_ref[128 * piece : 128 * piece + 128, :].T
        for y in range(6):
            for x in range(6):
                row = y * 6 + x
                solution_ref[x, y : y + 1, 128 * piece : 128 * piece + 128] = back[row : row + 1]
                residual_ref[x, y : y + 1, 128 * piece : 128 * piece + 128] = back[36 + row : 37 + row]


def body(adjoint_source, potential, element_matrix, region_labels, conductivity, restriction_map):
    n_slab = lax.axis_size("slab")
    n_cross = lax.axis_size("cross")
    slab, cross = lax.axis_index("slab"), lax.axis_index("cross")
    place = jnp.stack([slab, slab % 2, cross % 2]).astype(jnp.int32)
    columns = [
        [slab * n_cross + cross for slab in (2 * pair, 2 * pair + 1) for cross in range(n_cross)]
        for pair in range(n_slab // 2)
    ]
    planes = [[2 * pair + low for pair in range(n_slab // 2)] for low in range(2)]
    def shifted(value, axis, step):
        count = lax.axis_size(axis)
        pairs = [(source, source + step) for source in range(count) if 0 <= source + step < count]
        return lax.ppermute(value, axis, pairs)

    def gather(copies):
        return lax.all_to_all(copies, "slab", 0, 0, tiled=True)

    field, wide = (18, 8, 128), (18, 16, 128)
    space = [(40, 16, 128), (64, 1152), (64, 1152), field]
    regions = region_labels + 1
    pairs = [
        (here * n_cross + beside, (here + 1) * n_cross + beside + 1)
        for here in range(n_slab - 1)
        for beside in range(n_cross - 1)
    ]
    corner = lax.ppermute(regions[1, 1:2], ("slab", "cross"), pairs)
    below = shifted(regions[1], "slab", 1)
    beside = shifted(regions[:, 1], "cross", 1)
    r, ionic, labels, coarse, own, table = call(
        unpack_kernel, [field] * 3 + [(8, 128), (4, 128), (4, 128)],
        [(128, 384), (384, 128), (6, 6, 384), (6, 6, 384), pltpu.VMEM((6, 6, 384), jnp.int32),
         pltpu.VMEM((2, 2, 128), jnp.int32), pltpu.SMEM((4,), F32), pltpu.SemaphoreType.DMA((5,))],
        adjoint_source, potential, restriction_map, region_labels, conductivity, away=(0, 1, 2, 3, 4),
    )
    sigma, diagonal, scaled, message, near, far = call(
        diagonal_kernel, [(9, 128), field, field, (n_slab, 8, 128), (112, 128), (112, 128)],
        [field, (112, 128), (112, 128)],
        place, corner, below, beside, own, table, element_matrix, r, ionic, labels, coarse, smem=(0,),
    )

    def exchange(near, far, axis):
        count = lax.axis_size(axis)
        far_pairs = [(c, c + 1) for c in range(1, count - 1, 2)]
        far_pairs += [(above, c) for c, above in far_pairs]
        return lax.ppermute(near, axis, [(c, c ^ 1) for c in range(count)]), lax.ppermute(far, axis, far_pairs)

    faces = [(96, 128), (96, 128)]
    wide_z, z, near, far, scale, wide_labels = call(
        first_solve_kernel, [wide, field, *faces, (10, 8, 128), wide], faces,
        place, gather(message), scaled, labels, *exchange(near, far, "slab"), smem=(0,),
    )
    q, scaled, message, near, far = call(
        first_image_kernel, [field, field, (n_slab, 8, 128), (56, 128), (56, 128)],
        [(56, 128), (56, 128), *space],
        place, wide_z, z, *exchange(near, far, "cross")[::-1], sigma, element_matrix, ionic, diagonal, labels,
        smem=(0,),
    )
    wide_w, w, near, far = call(
        next_solve_kernel, [wide, field, *faces], faces,
        place, gather(message), scaled, wide_labels, *exchange(near, far, "slab"), scale, smem=(0,),
    )
    t, message = call(
        next_image_kernel, [field, (n_slab // 2, 1, 128)], space,
        place, wide_w, w, *exchange(near, far, "cross")[::-1], sigma, element_matrix, ionic, r, z, q, smem=(0,),
    )
    parts = lax.all_to_all(message, "slab", 0, 0, axis_index_groups=planes, tiled=True)
    parts = jnp.broadcast_to(jnp.sum(parts, 0)[None], (2 * n_cross, 1, 128))
    dots = lax.all_to_all(parts, ("slab", "cross"), 0, 0, axis_index_groups=columns, tiled=True)
    return tuple(call(finish_kernel, [(6, 6, 384)] * 2, [(128, 128), (384, 128)], dots, r, z, q, w, t))


def solution(mesh):
    return jax.shard_map(
        body,
        mesh=mesh,
        in_specs=(
            P("slab", "cross", None),
            P("slab", "cross", None),
            P(),
            P("slab", "cross", None),
            P(),
            P("slab", "cross", None),
        ),
        out_specs=(P("slab", "cross", None), P("slab", "cross", None)),
        check_vma=False,
    )
```

```python
import functools

import jax
import jax.numpy as jnp
from jax import lax
from jax.experimental import pallas as pl
from jax.experimental.pallas import tpu as pltpu
from jax.sharding import PartitionSpec as P

LABELS = 8
DAMPING = 0.8
COUPLING = 0.2
SHARE = 0.1
REACH = 3
NEAR = REACH + 1


F32 = jnp.float32
BF16 = jnp.bfloat16
SPAN = (-1, 0, 1)


def lanes(shape):
    return lax.broadcasted_iota(jnp.int32, shape, len(shape) - 1)


def call(kernel, out_shapes, scratch, *operands, smem=(), away=()):
    specs = [
        pl.BlockSpec(memory_space=pltpu.SMEM if index in smem else pltpu.HBM if index in away else pltpu.VMEM)
        for index in range(len(operands))
    ]
    operands = [
        pltpu.with_memory_space_constraint(operand, pltpu.HBM) if index in away else operand
        for index, operand in enumerate(operands)
    ]
    return pl.pallas_call(
        kernel,
        out_shape=[jax.ShapeDtypeStruct(shape, F32) for shape in out_shapes],
        in_specs=specs,
        out_specs=[pl.BlockSpec(memory_space=pltpu.VMEM)] * len(out_shapes),
        scratch_shapes=[pltpu.VMEM(shape, F32) if isinstance(shape, tuple) else shape for shape in scratch],
        compiler_params=pltpu.CompilerParams(vmem_limit_bytes=24 << 20),
    )(*operands)


def restrict(field, labels):
    rows = []
    for label in range(LABELS):
        kept = jnp.sum(jnp.where(labels == label + 1.0, field, 0.0), axis=0)
        rows.append(jnp.sum(kept, axis=0, keepdims=True))
    sums = jnp.concatenate(rows, 0)
    even = lanes((8, 128)) % 2 == 0
    return sums + jnp.where(even, pltpu.roll(sums, 127, 1), pltpu.roll(sums, 1, 1))


def prolong(coarse, labels):
    row = lax.broadcasted_iota(jnp.int32, (16, 128), 0)
    field = jnp.zeros_like(labels)
    for label in range(LABELS):
        low, own, high = [coarse[step, label : label + 1, :] for step in range(3)]
        values = jnp.where(row < 3, low, jnp.where(row < 9, own, high))
        field = jnp.where(labels == label + 1.0, values[None], field)
    return field


def assemble(product_of, total_ref):
    total_ref[...] = jnp.zeros_like(total_ref)
    start = lanes((16, 128)) == 0
    for i in SPAN:
        low_a, high_a = {-1: (3, 4), 0: (0, 4), 1: (0, 3)}[i]
        for j in SPAN:
            product = product_of((i + 1) * 3 + j + 1)
            last = pltpu.roll(product[48:64], 1, 1)
            pieces = [
                product[0:16] + jnp.where(start, 0.0, last),
                product[16:32],
                product[32:48],
            ]
            for c in range(3):
                for b in range(4):
                    y = 3 * j + b
                    if 0 <= y < 6:
                        x = 3 * i + low_a
                        rows = pieces[c][4 * b + low_a : 4 * b + high_a]
                        total_ref[c * 6 + y, x : x + high_a - low_a, :] += rows


def conductance(region, table_ref):
    value = jnp.zeros(region.shape, F32)
    for index in range(4):
        value = jnp.where(region == index + 1, table_ref[index : index + 1, :], value)
    return value


def unpack_kernel(source_hbm, potential_hbm, map_hbm, region_hbm, table_hbm, r_ref, ionic_ref, label_ref, coarse_ref,
                  own_ref, table_ref,
                  rows_ref, turned_ref, source_ref, potential_ref, map_ref, region_ref, values_ref, sems):
    copies = [
        pltpu.make_async_copy(away, here, sems.at[index])
        for index, (away, here) in enumerate(
            (
                (source_hbm, source_ref),
                (potential_hbm, potential_ref),
                (map_hbm, map_ref),
                (region_hbm, region_ref),
                (table_hbm, values_ref),
            )
        )
    ]
    for copy in copies:
        copy.start()
    rows_ref[...] = jnp.zeros_like(rows_ref)
    for copy in copies:
        copy.wait()
    for index in range(4):
        table_ref[index : index + 1, :] = jnp.full((1, 128), values_ref[index])
    for i in range(2):
        own_ref[2 * i : 2 * i + 2, :] = conductance(region_ref[i] + 1, table_ref)
    for y in range(6):
        for x in range(6):
            row = y * 6 + x
            rows_ref[row : row + 1, :] = source_ref[x, y : y + 1, :]
            rows_ref[36 + row : 37 + row, :] = potential_ref[x, y : y + 1, :]
            rows_ref[72 + row : 73 + row, :] = map_ref[x, y : y + 1, :].astype(F32)
    for piece in range(3):
        turned_ref[128 * piece : 128 * piece + 128, :] = rows_ref[:, 128 * piece : 128 * piece + 128].T
    r_ref[...] = jnp.zeros_like(r_ref)
    ionic_ref[...] = jnp.zeros_like(ionic_ref)
    label_ref[...] = jnp.zeros_like(label_ref)
    for c in range(3):
        split = turned_ref[pl.ds(c, 128, stride=3), :].T
        for y in range(6):
            r_ref[c * 6 + y, 0:6, :] = split[6 * y : 6 * y + 6]
            tangent = jnp.tanh(split[36 + 6 * y : 42 + 6 * y])
            ionic_ref[c * 6 + y, 0:6, :] = 1.0 + 2.0 * (1.0 - tangent * tangent)
            label_ref[c * 6 + y, 0:6, :] = split[72 + 6 * y : 78 + 6 * y] + 1.0
    coarse_ref[...] = restrict(r_ref[...], label_ref[...])


def send(odd, both_ref, near_ref, far_ref):
    near_ref[...] = both_ref[odd]
    far_ref[...] = both_ref[1 - odd]


def receive(odd, near_ref, far_ref, both_ref):
    both_ref[odd] = near_ref[...]
    both_ref[1 - odd] = far_ref[...]


def send_slab(odd, fields, near_ref, far_ref, both_ref):
    both_ref[...] = jnp.zeros_like(both_ref)
    for index, field_ref in enumerate(fields):
        for n in range(18):
            row = 56 * index + 3 * n
            both_ref[0, row : row + 3, :] = field_ref[n, 3:6, :]
            both_ref[1, 56 * index + n : 56 * index + n + 1, :] = field_ref[n, 0:1, :]
    send(odd, both_ref, near_ref, far_ref)


def diagonal_kernel(place_ref, corner_ref, below_ref, beside_ref, own_ref, table_ref, matrix_ref, r_ref, ionic_ref, label_ref, coarse_ref,
                    sigma_ref, diagonal_ref, scaled_ref, message_ref, near_ref, far_ref,
                    total_ref, both_ref):
    sigma_ref[0:1, :] = conductance(corner_ref[...], table_ref)
    sigma_ref[1:3, :] = conductance(below_ref[...], table_ref)
    for i in range(2):
        sigma_ref[3 + 3 * i : 4 + 3 * i, :] = conductance(beside_ref[i : i + 1, :], table_ref)
        sigma_ref[4 + 3 * i : 6 + 3 * i, :] = own_ref[2 * i : 2 * i + 2, :]
    square = (64, 64)
    eye = lax.broadcasted_iota(jnp.int32, square, 0) == lax.broadcasted_iota(jnp.int32, square, 1)
    corner = jnp.sum(jnp.where(eye, matrix_ref[...], 0.0), axis=1, keepdims=True)
    assemble(lambda e: corner * sigma_ref[e : e + 1, :], total_ref)
    labels = label_ref[...]
    diagonal = jnp.where(labels == 0.0, 1.0, total_ref[...] + ionic_ref[...])
    diagonal_ref[...] = diagonal
    coarse_diag = SHARE * restrict(diagonal, labels)
    even = lanes((8, 128)) % 2 == 0
    message = jnp.where(even, coarse_ref[...], coarse_diag)
    message_ref[...] = jnp.broadcast_to(message[None], message_ref.shape)
    scaled_ref[...] = r_ref[...] / diagonal
    send_slab(place_ref[1], (scaled_ref, label_ref), near_ref, far_ref, both_ref)


def along(values):
    lane = lanes(values.shape)
    row = lax.broadcasted_iota(jnp.int32, values.shape, 1)
    after = pltpu.roll(values, 7, 1)
    carried = jnp.where(lane < 126, pltpu.roll(after, 126, 2), 0.0)
    after = jnp.where(row == 7, carried, after)
    before = pltpu.roll(values, 1, 1)
    carried = jnp.where(lane >= 2, pltpu.roll(before, 2, 2), 0.0)
    return after + jnp.where(row == 0, carried, before)


def smooth(start, valid):
    level = start
    for sweep in range(REACH):
        beside = level[2:] + level[:-2] + along(level[1:-1])
        here = slice(sweep + 1, 2 * NEAR - sweep)
        level = start[here] + (1.0 - DAMPING) * level[1:-1] + (DAMPING * COUPLING) * beside
        level = level * valid[here]
    return level


def around(place_ref, count):
    rows, valid = [], []
    for step in range(-NEAR, NEAR + 1):
        row = place_ref[0] + step
        inside = jnp.logical_and(row >= 0, row < count)
        rows.append(jnp.clip(row, 0, count - 1))
        valid.append(jnp.where(inside, jnp.ones((1, 8, 128), F32), 0.0))
    return rows, jnp.concatenate(valid, 0)


def even_part(tiles):
    even = lanes(tiles.shape) % 2 == 0
    return jnp.where(even, tiles, pltpu.roll(tiles, 1, tiles.ndim - 1))


def odd_part(tiles):
    even = lanes(tiles.shape) % 2 == 0
    return jnp.where(even, pltpu.roll(tiles, 127, tiles.ndim - 1), tiles)


def widen(field_ref, both_ref, start, wide_ref):
    wide_ref[...] = jnp.zeros_like(wide_ref)
    for n in range(18):
        wide_ref[n, 0:3, :] = both_ref[1, start + 3 * n : start + 3 * n + 3, :]
        wide_ref[n, 3:9, :] = field_ref[n, 0:6, :]
        wide_ref[n, 9:10, :] = both_ref[0, start + n : start + n + 1, :]


def send_cross(odd, wide_ref, own_ref, near_ref, far_ref, both_ref):
    own_ref[...] = jnp.zeros_like(own_ref)
    for n in range(18):
        own_ref[n, 0:6, :] = wide_ref[n, 3:9, :]
    both_ref[...] = jnp.zeros_like(both_ref)
    for c in range(3):
        for y in range(3):
            row = (3 * c + y) * 10
            both_ref[0, row : row + 10, :] = wide_ref[6 * c + 3 + y, 0:10, :]
        both_ref[1, 10 * c : 10 * c + 10, :] = wide_ref[6 * c, 0:10, :]
    send(odd, both_ref, near_ref, far_ref)


def first_solve_kernel(place_ref, gathered_ref, scaled_ref, label_ref, left_ref, right_ref,
                       wide_ref, z_ref, near_ref, far_ref, scale_ref, wide_label_ref, slab_ref, cross_ref):
    receive(place_ref[1], right_ref, left_ref, slab_ref)
    rows, valid = around(place_ref, gathered_ref.shape[0])
    tiles = jnp.concatenate([gathered_ref[pl.ds(row, 1)] for row in rows], 0)
    sums = jnp.sum(gathered_ref[...], axis=0)
    inverse = valid / jnp.sqrt(odd_part(tiles))
    share = 1.0 / odd_part(sums)
    scale_ref[0 : 2 * NEAR + 1] = inverse
    scale_ref[2 * NEAR + 1] = share
    level = smooth(DAMPING * even_part(tiles) * inverse, valid)
    coarse = level * inverse[REACH : REACH + 3] + (even_part(sums) * share)[None]
    widen(label_ref, slab_ref, 56, wide_label_ref)
    widen(scaled_ref, slab_ref, 0, wide_ref)
    wide_ref[...] += prolong(coarse, wide_label_ref[...])
    send_cross(place_ref[2], wide_ref, z_ref, near_ref, far_ref, cross_ref)


def next_solve_kernel(place_ref, gathered_ref, scaled_ref, wide_label_ref, left_ref, right_ref, scale_ref,
                      wide_ref, w_ref, near_ref, far_ref, slab_ref, cross_ref):
    receive(place_ref[1], right_ref, left_ref, slab_ref)
    rows, valid = around(place_ref, gathered_ref.shape[0])
    tiles = jnp.concatenate([gathered_ref[pl.ds(row, 1)] for row in rows], 0)
    sums = jnp.sum(gathered_ref[...], axis=0)
    inverse = scale_ref[0 : 2 * NEAR + 1]
    level = smooth(DAMPING * tiles * inverse, valid)
    coarse = level * inverse[REACH : REACH + 3] + (sums * scale_ref[2 * NEAR + 1])[None]
    widen(scaled_ref, slab_ref, 0, wide_ref)
    wide_ref[...] += prolong(coarse, wide_label_ref[...])
    send_cross(place_ref[2], wide_ref, w_ref, near_ref, far_ref, cross_ref)


def operate(place_ref, wide_ref, field_ref, near_ref, far_ref, sigma_ref, matrix_ref, ionic_ref,
            cross_ref, grid_ref, local_ref, product_ref, total_ref):
    for n in range(18):
        grid_ref[n // 6 * 10 + 3 + n % 6, 0:10, :] = wide_ref[n, 0:10, :]

    receive(place_ref[2], near_ref, far_ref, cross_ref)
    for c in range(3):
        for y in range(3):
            row = (3 * c + y) * 10
            grid_ref[10 * c + y, 0:10, :] = cross_ref[1, row : row + 10, :]
        grid_ref[10 * c + 9, 0:10, :] = cross_ref[0, 10 * c : 10 * c + 10, :]
    end = lanes((10, 128)) == 127
    for y in range(10):
        grid_ref[30 + y, 0:10, :] = jnp.where(end, 0.0, pltpu.roll(grid_ref[y, 0:10, :], 127, 1))
    for i in SPAN:
        for j in SPAN:
            left = ((i + 1) * 3 + j + 1) * 128
            for c in range(4):
                for b in range(4):
                    row = 16 * c + 4 * b
                    n = c * 10 + 3 * (j + 1) + b
                    local_ref[row : row + 4, left : left + 128] = grid_ref[n, 3 * i + 3 : 3 * i + 7, :]
    matrix = matrix_ref[...]
    matrix_high = matrix.astype(BF16)
    matrix_low = (matrix - matrix_high.astype(F32)).astype(BF16)
    local = local_ref[...]
    high = local.astype(BF16)
    low = (local - high.astype(F32)).astype(BF16)
    dot = functools.partial(jnp.dot, preferred_element_type=F32)
    product_ref[...] = dot(matrix_high, high) + (dot(matrix_high, low) + dot(matrix_low, high))
    assemble(lambda e: product_ref[:, 128 * e : 128 * e + 128] * sigma_ref[e : e + 1, :], total_ref)
    return total_ref[...] + ionic_ref[...] * field_ref[...]


def first_image_kernel(place_ref, wide_ref, z_ref, far_ref, near_ref, sigma_ref, matrix_ref, ionic_ref, diagonal_ref, label_ref,
                       q_ref, scaled_ref, message_ref, left_ref, right_ref, both_ref, *scratch):
    image = operate(place_ref, wide_ref, z_ref, near_ref, far_ref, sigma_ref, matrix_ref, ionic_ref, *scratch)
    q_ref[...] = image
    message_ref[...] = jnp.broadcast_to(restrict(image, label_ref[...])[None], message_ref.shape)
    scaled_ref[...] = image / diagonal_ref[...]
    send_slab(place_ref[1], (scaled_ref,), left_ref, right_ref, both_ref)


def next_image_kernel(place_ref, wide_ref, w_ref, far_ref, near_ref, sigma_ref, matrix_ref, ionic_ref,
                      r_ref, z_ref, q_ref, t_ref, message_ref, *scratch):
    image = operate(place_ref, wide_ref, w_ref, near_ref, far_ref, sigma_ref, matrix_ref, ionic_ref, *scratch)
    t_ref[...] = image
    r, z, q, w = r_ref[...], z_ref[...], q_ref[...], w_ref[...]
    row = jnp.zeros((1, 128), F32)
    for index, (left, right) in enumerate(((r, z), (z, q), (r, w), (q, w), (z, image), (w, image))):
        part = jnp.sum(jnp.sum(left * right, axis=0), axis=0, keepdims=True)
        row = jnp.where(lanes((1, 128)) == index, jnp.sum(part, axis=1, keepdims=True), row)
    message_ref[...] = jnp.broadcast_to(row[None], message_ref.shape)


def finish_kernel(dots_ref, r_ref, z_ref, q_ref, w_ref, t_ref, solution_ref, residual_ref, rows_ref, turned_ref):
    dots = jnp.sum(dots_ref[...], axis=0)
    rz, zq, rw, qw, zt, wt = [dots[:, index : index + 1] for index in range(6)]
    alpha = rz / zq
    rz_next = alpha * (alpha * qw - rw)
    beta = rz_next / rz
    more = 1.0 + beta
    second = rz_next / (more * more * zq - more * alpha * (zt + qw) + alpha * alpha * wt)
    from_z = alpha + second * more
    from_w = second * alpha
    rows_ref[...] = jnp.zeros_like(rows_ref)
    for c in range(3):
        for y in range(6):
            n = 6 * c + y
            answer = from_z * z_ref[n] - from_w * w_ref[n]
            left = r_ref[n] - from_z * q_ref[n] + from_w * t_ref[n]
            rows_ref[6 * y : 6 * y + 6, :] = answer[0:6]
            rows_ref[36 + 6 * y : 42 + 6 * y, :] = left[0:6]
        turned_ref[pl.ds(c, 128, stride=3), :] = rows_ref[...].T
    for piece in range(3):
        back = turned_ref[128 * piece : 128 * piece + 128, :].T
        for y in range(6):
            for x in range(6):
                row = y * 6 + x
                solution_ref[x, y : y + 1, 128 * piece : 128 * piece + 128] = back[row : row + 1]
                residual_ref[x, y : y + 1, 128 * piece : 128 * piece + 128] = back[36 + row : 37 + row]


def body(adjoint_source, potential, element_matrix, region_labels, conductivity, restriction_map):
    n_slab = lax.axis_size("slab")
    n_cross = lax.axis_size("cross")
    slab, cross = lax.axis_index("slab"), lax.axis_index("cross")
    place = jnp.stack([slab, slab % 2, cross % 2]).astype(jnp.int32)
    columns = [
        [slab * n_cross + cross for slab in (2 * pair, 2 * pair + 1) for cross in range(n_cross)]
        for pair in range(n_slab // 2)
    ]
    planes = [[2 * pair + low for pair in range(n_slab // 2)] for low in range(2)]
    def shifted(value, axis, step):
        count = lax.axis_size(axis)
        pairs = [(source, source + step) for source in range(count) if 0 <= source + step < count]
        return lax.ppermute(value, axis, pairs)

    def gather(copies):
        return lax.all_to_all(copies, "slab", 0, 0, tiled=True)

    field, wide = (18, 8, 128), (18, 16, 128)
    space = [(2, 96, 128), (40, 16, 128), (64, 1152), (64, 1152), field]
    regions = region_labels + 1
    pairs = [
        (here * n_cross + beside, (here + 1) * n_cross + beside + 1)
        for here in range(n_slab - 1)
        for beside in range(n_cross - 1)
    ]
    corner = lax.ppermute(regions[1, 1:2], ("slab", "cross"), pairs)
    below = shifted(regions[1], "slab", 1)
    beside = shifted(regions[:, 1], "cross", 1)
    r, ionic, labels, coarse, own, table = call(
        unpack_kernel, [field] * 3 + [(8, 128), (4, 128), (4, 128)],
        [(128, 384), (384, 128), (6, 6, 384), (6, 6, 384), pltpu.VMEM((6, 6, 384), jnp.int32),
         pltpu.VMEM((2, 2, 128), jnp.int32), pltpu.SMEM((4,), F32), pltpu.SemaphoreType.DMA((5,))],
        adjoint_source, potential, restriction_map, region_labels, conductivity, away=(0, 1, 2, 3, 4),
    )
    sigma, diagonal, scaled, message, near, far = call(
        diagonal_kernel, [(9, 128), field, field, (n_slab, 8, 128), (112, 128), (112, 128)],
        [field, (2, 112, 128)],
        place, corner, below, beside, own, table, element_matrix, r, ionic, labels, coarse, smem=(0,),
    )

    def exchange(near, far, axis):
        count = lax.axis_size(axis)
        far_pairs = [(c, c + 1) for c in range(1, count - 1, 2)]
        far_pairs += [(above, c) for c, above in far_pairs]
        far = lax.ppermute(far, axis, far_pairs)
        return far, lax.ppermute(near, axis, [(c, c ^ 1) for c in range(count)])

    faces = [(96, 128), (96, 128)]
    wide_z, z, near, far, scale, wide_labels = call(
        first_solve_kernel, [wide, field, *faces, (10, 8, 128), wide], [(2, 112, 128), (2, 96, 128)],
        place, gather(message), scaled, labels, *exchange(near, far, "slab"), smem=(0,),
    )
    q, scaled, message, near, far = call(
        first_image_kernel, [field, field, (n_slab, 8, 128), (56, 128), (56, 128)],
        [(2, 56, 128), *space],
        place, wide_z, z, *exchange(near, far, "cross"), sigma, element_matrix, ionic, diagonal, labels,
        smem=(0,),
    )
    wide_w, w, near, far = call(
        next_solve_kernel, [wide, field, *faces], [(2, 56, 128), (2, 96, 128)],
        place, gather(message), scaled, wide_labels, *exchange(near, far, "slab"), scale, smem=(0,),
    )
    t, message = call(
        next_image_kernel, [field, (n_slab // 2, 1, 128)], space,
        place, wide_w, w, *exchange(near, far, "cross"), sigma, element_matrix, ionic, r, z, q, smem=(0,),
    )
    parts = lax.all_to_all(message, "slab", 0, 0, axis_index_groups=planes, tiled=True)
    parts = jnp.broadcast_to(jnp.sum(parts, 0)[None], (2 * n_cross, 1, 128))
    dots = lax.all_to_all(parts, ("slab", "cross"), 0, 0, axis_index_groups=columns, tiled=True)
    return tuple(call(finish_kernel, [(6, 6, 384)] * 2, [(128, 128), (384, 128)], dots, r, z, q, w, t))


def solution(mesh):
    return jax.shard_map(
        body,
        mesh=mesh,
        in_specs=(
            P("slab", "cross", None),
            P("slab", "cross", None),
            P(),
            P("slab", "cross", None),
            P(),
            P("slab", "cross", None),
        ),
        out_specs=(P("slab", "cross", None), P("slab", "cross", None)),
        check_vma=False,
    )
```

```python
import functools

import jax
import jax.numpy as jnp
from jax import lax
from jax.experimental import pallas as pl
from jax.experimental.pallas import tpu as pltpu
from jax.sharding import PartitionSpec as P

LABELS = 8
DAMPING = 0.8
COUPLING = 0.2
SHARE = 0.1
REACH = 3
NEAR = REACH + 1


F32 = jnp.float32
BF16 = jnp.bfloat16
SPAN = (-1, 0, 1)


def parity(axis):
    return lax.rem(lax.axis_index(axis), 2)


def lanes(shape):
    return lax.broadcasted_iota(jnp.int32, shape, len(shape) - 1)


def call(kernel, out_shapes, scratch, *operands, away=()):
    specs = [
        pl.BlockSpec(memory_space=pltpu.HBM if index in away else pltpu.VMEM)
        for index in range(len(operands))
    ]
    operands = [
        pltpu.with_memory_space_constraint(operand, pltpu.HBM) if index in away else operand
        for index, operand in enumerate(operands)
    ]
    return pl.pallas_call(
        kernel,
        out_shape=[jax.ShapeDtypeStruct(shape, F32) for shape in out_shapes],
        in_specs=specs,
        out_specs=[pl.BlockSpec(memory_space=pltpu.VMEM)] * len(out_shapes),
        scratch_shapes=[pltpu.VMEM(shape, F32) if isinstance(shape, tuple) else shape for shape in scratch],
        compiler_params=pltpu.CompilerParams(vmem_limit_bytes=24 << 20),
    )(*operands)


def restrict(field, labels):
    rows = []
    for label in range(LABELS):
        kept = jnp.sum(jnp.where(labels == label + 1.0, field, 0.0), axis=0)
        rows.append(jnp.sum(kept, axis=0, keepdims=True))
    sums = jnp.concatenate(rows, 0)
    even = lanes((8, 128)) % 2 == 0
    return sums + jnp.where(even, pltpu.roll(sums, 127, 1), pltpu.roll(sums, 1, 1))


def prolong(coarse, labels):
    row = lax.broadcasted_iota(jnp.int32, (16, 128), 0)
    field = jnp.zeros_like(labels)
    for label in range(LABELS):
        low, own, high = [coarse[step, label : label + 1, :] for step in range(3)]
        values = jnp.where(row < 3, low, jnp.where(row < 9, own, high))
        field = jnp.where(labels == label + 1.0, values[None], field)
    return field


def assemble(product_of, total_ref):
    total_ref[...] = jnp.zeros_like(total_ref)
    start = lanes((16, 128)) == 0
    for i in SPAN:
        low_a, high_a = {-1: (3, 4), 0: (0, 4), 1: (0, 3)}[i]
        for j in SPAN:
            product = product_of((i + 1) * 3 + j + 1)
            last = pltpu.roll(product[48:64], 1, 1)
            pieces = [
                product[0:16] + jnp.where(start, 0.0, last),
                product[16:32],
                product[32:48],
            ]
            for c in range(3):
                for b in range(4):
                    y = 3 * j + b
                    if 0 <= y < 6:
                        x = 3 * i + low_a
                        rows = pieces[c][4 * b + low_a : 4 * b + high_a]
                        total_ref[c * 6 + y, x : x + high_a - low_a, :] += rows


def conductance(region, table_ref):
    value = jnp.zeros(region.shape, F32)
    for index in range(4):
        value = jnp.where(region == index + 1, table_ref[index : index + 1, :], value)
    return value


def unpack_kernel(source_hbm, potential_hbm, map_hbm, region_hbm, table_hbm, r_ref, ionic_ref, label_ref, coarse_ref,
                  own_ref, table_ref,
                  rows_ref, turned_ref, source_ref, potential_ref, map_ref, region_ref, values_ref, sems):
    copies = [
        pltpu.make_async_copy(away, here, sems.at[index])
        for index, (away, here) in enumerate(
            (
                (source_hbm, source_ref),
                (potential_hbm, potential_ref),
                (map_hbm, map_ref),
                (region_hbm, region_ref),
                (table_hbm, values_ref),
            )
        )
    ]
    for copy in copies:
        copy.start()
    rows_ref[...] = jnp.zeros_like(rows_ref)
    for copy in copies:
        copy.wait()
    for index in range(4):
        table_ref[index : index + 1, :] = jnp.full((1, 128), values_ref[index])
    for i in range(2):
        own_ref[2 * i : 2 * i + 2, :] = conductance(region_ref[i] + 1, table_ref)
    for y in range(6):
        for x in range(6):
            row = y * 6 + x
            rows_ref[row : row + 1, :] = source_ref[x, y : y + 1, :]
            rows_ref[36 + row : 37 + row, :] = potential_ref[x, y : y + 1, :]
            rows_ref[72 + row : 73 + row, :] = map_ref[x, y : y + 1, :].astype(F32)
    for piece in range(3):
        turned_ref[128 * piece : 128 * piece + 128, :] = rows_ref[:, 128 * piece : 128 * piece + 128].T
    r_ref[...] = jnp.zeros_like(r_ref)
    ionic_ref[...] = jnp.zeros_like(ionic_ref)
    label_ref[...] = jnp.zeros_like(label_ref)
    for c in range(3):
        split = turned_ref[pl.ds(c, 128, stride=3), :].T
        for y in range(6):
            r_ref[c * 6 + y, 0:6, :] = split[6 * y : 6 * y + 6]
            tangent = jnp.tanh(split[36 + 6 * y : 42 + 6 * y])
            ionic_ref[c * 6 + y, 0:6, :] = 1.0 + 2.0 * (1.0 - tangent * tangent)
            label_ref[c * 6 + y, 0:6, :] = split[72 + 6 * y : 78 + 6 * y] + 1.0
    coarse_ref[...] = restrict(r_ref[...], label_ref[...])


def send(odd, both_ref, near_ref, far_ref):
    near_ref[...] = both_ref[odd]
    far_ref[...] = both_ref[1 - odd]


def receive(odd, near_ref, far_ref, both_ref):
    both_ref[odd] = near_ref[...]
    both_ref[1 - odd] = far_ref[...]


def send_slab(odd, fields, near_ref, far_ref, both_ref):
    both_ref[...] = jnp.zeros_like(both_ref)
    for index, field_ref in enumerate(fields):
        for n in range(18):
            row = 56 * index + 3 * n
            both_ref[0, row : row + 3, :] = field_ref[n, 3:6, :]
            both_ref[1, 56 * index + n : 56 * index + n + 1, :] = field_ref[n, 0:1, :]
    send(odd, both_ref, near_ref, far_ref)


def diagonal_kernel(corner_ref, below_ref, beside_ref, own_ref, table_ref, matrix_ref, r_ref, ionic_ref, label_ref,
                    sigma_ref, diagonal_ref, scaled_ref, near_ref, far_ref,
                    total_ref, both_ref):
    sigma_ref[0:1, :] = conductance(corner_ref[...], table_ref)
    sigma_ref[1:3, :] = conductance(below_ref[...], table_ref)
    for i in range(2):
        sigma_ref[3 + 3 * i : 4 + 3 * i, :] = conductance(beside_ref[i : i + 1, :], table_ref)
        sigma_ref[4 + 3 * i : 6 + 3 * i, :] = own_ref[2 * i : 2 * i + 2, :]
    square = (64, 64)
    eye = lax.broadcasted_iota(jnp.int32, square, 0) == lax.broadcasted_iota(jnp.int32, square, 1)
    corner = jnp.sum(jnp.where(eye, matrix_ref[...], 0.0), axis=1, keepdims=True)
    assemble(lambda e: corner * sigma_ref[e : e + 1, :], total_ref)
    labels = label_ref[...]
    diagonal = jnp.where(labels == 0.0, 1.0, total_ref[...] + ionic_ref[...])
    diagonal_ref[...] = diagonal
    scaled_ref[...] = r_ref[...] / diagonal
    send_slab(parity("slab"), (scaled_ref, label_ref), near_ref, far_ref, both_ref)


def first_message_kernel(diagonal_ref, label_ref, coarse_ref, held_ref, message_ref, near_ref):
    labels = label_ref[...]
    coarse_diag = SHARE * restrict(diagonal_ref[...], labels)
    even = lanes((8, 128)) % 2 == 0
    message = jnp.where(even, coarse_ref[...], coarse_diag)
    message_ref[...] = jnp.broadcast_to(message[None], message_ref.shape)
    near_ref[...] = held_ref[...]


def next_message_kernel(q_ref, label_ref, held_ref, message_ref, near_ref):
    message_ref[...] = jnp.broadcast_to(restrict(q_ref[...], label_ref[...])[None], message_ref.shape)
    near_ref[...] = held_ref[...]


def along(values):
    lane = lanes(values.shape)
    row = lax.broadcasted_iota(jnp.int32, values.shape, 1)
    after = pltpu.roll(values, 7, 1)
    carried = jnp.where(lane < 126, pltpu.roll(after, 126, 2), 0.0)
    after = jnp.where(row == 7, carried, after)
    before = pltpu.roll(values, 1, 1)
    carried = jnp.where(lane >= 2, pltpu.roll(before, 2, 2), 0.0)
    return after + jnp.where(row == 0, carried, before)


def smooth(start, valid):
    level = start
    for sweep in range(REACH):
        beside = level[2:] + level[:-2] + along(level[1:-1])
        here = slice(sweep + 1, 2 * NEAR - sweep)
        level = start[here] + (1.0 - DAMPING) * level[1:-1] + (DAMPING * COUPLING) * beside
        level = level * valid[here]
    return level


def around(count):
    rows, valid = [], []
    for step in range(-NEAR, NEAR + 1):
        row = lax.axis_index("slab") + step
        inside = jnp.logical_and(row >= 0, row < count)
        rows.append(jnp.clip(row, 0, count - 1))
        valid.append(jnp.where(inside, jnp.ones((1, 8, 128), F32), 0.0))
    return rows, jnp.concatenate(valid, 0)


def even_part(tiles):
    even = lanes(tiles.shape) % 2 == 0
    return jnp.where(even, tiles, pltpu.roll(tiles, 1, tiles.ndim - 1))


def odd_part(tiles):
    even = lanes(tiles.shape) % 2 == 0
    return jnp.where(even, pltpu.roll(tiles, 127, tiles.ndim - 1), tiles)


def widen(field_ref, both_ref, start, wide_ref):
    wide_ref[...] = jnp.zeros_like(wide_ref)
    for n in range(18):
        wide_ref[n, 0:3, :] = both_ref[1, start + 3 * n : start + 3 * n + 3, :]
        wide_ref[n, 3:9, :] = field_ref[n, 0:6, :]
        wide_ref[n, 9:10, :] = both_ref[0, start + n : start + n + 1, :]


def send_cross(odd, wide_ref, own_ref, near_ref, far_ref, both_ref):
    own_ref[...] = jnp.zeros_like(own_ref)
    for n in range(18):
        own_ref[n, 0:6, :] = wide_ref[n, 3:9, :]
    both_ref[...] = jnp.zeros_like(both_ref)
    for c in range(3):
        for y in range(3):
            row = (3 * c + y) * 10
            both_ref[0, row : row + 10, :] = wide_ref[6 * c + 3 + y, 0:10, :]
        both_ref[1, 10 * c : 10 * c + 10, :] = wide_ref[6 * c, 0:10, :]
    send(odd, both_ref, near_ref, far_ref)


def first_solve_kernel(gathered_ref, scaled_ref, label_ref, left_ref, right_ref,
                       wide_ref, z_ref, near_ref, far_ref, scale_ref, wide_label_ref, slab_ref, cross_ref):
    receive(parity("slab"), right_ref, left_ref, slab_ref)
    rows, valid = around(gathered_ref.shape[0])
    tiles = jnp.concatenate([gathered_ref[pl.ds(row, 1)] for row in rows], 0)
    sums = jnp.sum(gathered_ref[...], axis=0)
    inverse = valid / jnp.sqrt(odd_part(tiles))
    share = 1.0 / odd_part(sums)
    scale_ref[0 : 2 * NEAR + 1] = inverse
    scale_ref[2 * NEAR + 1] = share
    level = smooth(DAMPING * even_part(tiles) * inverse, valid)
    coarse = level * inverse[REACH : REACH + 3] + (even_part(sums) * share)[None]
    widen(label_ref, slab_ref, 56, wide_label_ref)
    widen(scaled_ref, slab_ref, 0, wide_ref)
    wide_ref[...] += prolong(coarse, wide_label_ref[...])
    send_cross(parity("cross"), wide_ref, z_ref, near_ref, far_ref, cross_ref)


def next_solve_kernel(gathered_ref, scaled_ref, wide_label_ref, left_ref, right_ref, scale_ref,
                      wide_ref, w_ref, near_ref, far_ref, slab_ref, cross_ref):
    receive(parity("slab"), right_ref, left_ref, slab_ref)
    rows, valid = around(gathered_ref.shape[0])
    tiles = jnp.concatenate([gathered_ref[pl.ds(row, 1)] for row in rows], 0)
    sums = jnp.sum(gathered_ref[...], axis=0)
    inverse = scale_ref[0 : 2 * NEAR + 1]
    level = smooth(DAMPING * tiles * inverse, valid)
    coarse = level * inverse[REACH : REACH + 3] + (sums * scale_ref[2 * NEAR + 1])[None]
    widen(scaled_ref, slab_ref, 0, wide_ref)
    wide_ref[...] += prolong(coarse, wide_label_ref[...])
    send_cross(parity("cross"), wide_ref, w_ref, near_ref, far_ref, cross_ref)


def operate(wide_ref, field_ref, near_ref, far_ref, sigma_ref, matrix_ref, ionic_ref,
            cross_ref, grid_ref, local_ref, product_ref, total_ref):
    for n in range(18):
        grid_ref[n // 6 * 10 + 3 + n % 6, 0:10, :] = wide_ref[n, 0:10, :]

    receive(parity("cross"), near_ref, far_ref, cross_ref)
    for c in range(3):
        for y in range(3):
            row = (3 * c + y) * 10
            grid_ref[10 * c + y, 0:10, :] = cross_ref[1, row : row + 10, :]
        grid_ref[10 * c + 9, 0:10, :] = cross_ref[0, 10 * c : 10 * c + 10, :]
    end = lanes((10, 128)) == 127
    for y in range(10):
        grid_ref[30 + y, 0:10, :] = jnp.where(end, 0.0, pltpu.roll(grid_ref[y, 0:10, :], 127, 1))
    for i in SPAN:
        for j in SPAN:
            left = ((i + 1) * 3 + j + 1) * 128
            for c in range(4):
                for b in range(4):
                    row = 16 * c + 4 * b
                    n = c * 10 + 3 * (j + 1) + b
                    local_ref[row : row + 4, left : left + 128] = grid_ref[n, 3 * i + 3 : 3 * i + 7, :]
    matrix = matrix_ref[...]
    matrix_high = matrix.astype(BF16)
    matrix_low = (matrix - matrix_high.astype(F32)).astype(BF16)
    local = local_ref[...]
    high = local.astype(BF16)
    low = (local - high.astype(F32)).astype(BF16)
    dot = functools.partial(jnp.dot, preferred_element_type=F32)
    product_ref[...] = dot(matrix_high, high) + (dot(matrix_high, low) + dot(matrix_low, high))
    assemble(lambda e: product_ref[:, 128 * e : 128 * e + 128] * sigma_ref[e : e + 1, :], total_ref)
    return total_ref[...] + ionic_ref[...] * field_ref[...]


def first_image_kernel(wide_ref, z_ref, far_ref, near_ref, sigma_ref, matrix_ref, ionic_ref, diagonal_ref,
                       q_ref, scaled_ref, left_ref, right_ref, both_ref, *scratch):
    image = operate(wide_ref, z_ref, near_ref, far_ref, sigma_ref, matrix_ref, ionic_ref, *scratch)
    q_ref[...] = image
    scaled_ref[...] = image / diagonal_ref[...]
    send_slab(parity("slab"), (scaled_ref,), left_ref, right_ref, both_ref)


def next_image_kernel(wide_ref, w_ref, far_ref, near_ref, sigma_ref, matrix_ref, ionic_ref,
                      r_ref, z_ref, q_ref, t_ref, message_ref, *scratch):
    image = operate(wide_ref, w_ref, near_ref, far_ref, sigma_ref, matrix_ref, ionic_ref, *scratch)
    t_ref[...] = image
    r, z, q, w = r_ref[...], z_ref[...], q_ref[...], w_ref[...]
    row = jnp.zeros((1, 128), F32)
    for index, (left, right) in enumerate(((r, z), (z, q), (r, w), (q, w), (z, image), (w, image))):
        part = jnp.sum(jnp.sum(left * right, axis=0), axis=0, keepdims=True)
        row = jnp.where(lanes((1, 128)) == index, jnp.sum(part, axis=1, keepdims=True), row)
    message_ref[...] = jnp.broadcast_to(row[None], message_ref.shape)


def finish_kernel(dots_ref, r_ref, z_ref, q_ref, w_ref, t_ref, solution_ref, residual_ref, rows_ref, turned_ref):
    dots = jnp.sum(dots_ref[...], axis=0)
    rz, zq, rw, qw, zt, wt = [dots[:, index : index + 1] for index in range(6)]
    alpha = rz / zq
    rz_next = alpha * (alpha * qw - rw)
    beta = rz_next / rz
    more = 1.0 + beta
    second = rz_next / (more * more * zq - more * alpha * (zt + qw) + alpha * alpha * wt)
    from_z = alpha + second * more
    from_w = second * alpha
    rows_ref[...] = jnp.zeros_like(rows_ref)
    for c in range(3):
        for y in range(6):
            n = 6 * c + y
            answer = from_z * z_ref[n] - from_w * w_ref[n]
            left = r_ref[n] - from_z * q_ref[n] + from_w * t_ref[n]
            rows_ref[6 * y : 6 * y + 6, :] = answer[0:6]
            rows_ref[36 + 6 * y : 42 + 6 * y, :] = left[0:6]
        turned_ref[pl.ds(c, 128, stride=3), :] = rows_ref[...].T
    for piece in range(3):
        back = turned_ref[128 * piece : 128 * piece + 128, :].T
        for y in range(6):
            for x in range(6):
                row = y * 6 + x
                solution_ref[x, y : y + 1, 128 * piece : 128 * piece + 128] = back[row : row + 1]
                residual_ref[x, y : y + 1, 128 * piece : 128 * piece + 128] = back[36 + row : 37 + row]


def body(adjoint_source, potential, element_matrix, region_labels, conductivity, restriction_map):
    n_slab = lax.axis_size("slab")
    n_cross = lax.axis_size("cross")
    columns = [
        [slab * n_cross + cross for slab in (2 * pair, 2 * pair + 1) for cross in range(n_cross)]
        for pair in range(n_slab // 2)
    ]
    planes = [[2 * pair + low for pair in range(n_slab // 2)] for low in range(2)]
    def shifted(value, axis, step):
        count = lax.axis_size(axis)
        pairs = [(source, source + step) for source in range(count) if 0 <= source + step < count]
        return lax.ppermute(value, axis, pairs)

    def gather(copies):
        return lax.all_to_all(copies, "slab", 0, 0, tiled=True)

    field, wide = (18, 8, 128), (18, 16, 128)
    space = [(2, 96, 128), (40, 16, 128), (64, 1152), (64, 1152), field]
    regions = region_labels + 1
    pairs = [
        (here * n_cross + beside, (here + 1) * n_cross + beside + 1)
        for here in range(n_slab - 1)
        for beside in range(n_cross - 1)
    ]
    corner = lax.ppermute(regions[1, 1:2], ("slab", "cross"), pairs)
    below = shifted(regions[1], "slab", 1)
    beside = shifted(regions[:, 1], "cross", 1)
    r, ionic, labels, coarse, own, table = call(
        unpack_kernel, [field] * 3 + [(8, 128), (4, 128), (4, 128)],
        [(128, 384), (384, 128), (6, 6, 384), (6, 6, 384), pltpu.VMEM((6, 6, 384), jnp.int32),
         pltpu.VMEM((2, 2, 128), jnp.int32), pltpu.SMEM((4,), F32), pltpu.SemaphoreType.DMA((5,))],
        adjoint_source, potential, restriction_map, region_labels, conductivity, away=(0, 1, 2, 3, 4),
    )
    sigma, diagonal, scaled, near, far = call(
        diagonal_kernel, [(9, 128), field, field, (112, 128), (112, 128)],
        [field, (2, 112, 128)],
        corner, below, beside, own, table, element_matrix, r, ionic, labels,
    )
    message, near = call(
        first_message_kernel, [(n_slab, 8, 128), (112, 128)], [], diagonal, labels, coarse, near
    )

    def exchange(near, far, axis):
        count = lax.axis_size(axis)
        far_pairs = [(c, c + 1) for c in range(1, count - 1, 2)]
        far_pairs += [(above, c) for c, above in far_pairs]
        far = lax.ppermute(far, axis, far_pairs)
        return far, lax.ppermute(near, axis, [(c, c ^ 1) for c in range(count)])

    faces = [(96, 128), (96, 128)]
    wide_z, z, near, far, scale, wide_labels = call(
        first_solve_kernel, [wide, field, *faces, (10, 8, 128), wide], [(2, 112, 128), (2, 96, 128)],
        gather(message), scaled, labels, *exchange(near, far, "slab"),
    )
    q, scaled, near, far = call(
        first_image_kernel, [field, field, (56, 128), (56, 128)],
        [(2, 56, 128), *space],
        wide_z, z, *exchange(near, far, "cross"), sigma, element_matrix, ionic, diagonal,
    )
    message, near = call(next_message_kernel, [(n_slab, 8, 128), (56, 128)], [], q, labels, near)
    wide_w, w, near, far = call(
        next_solve_kernel, [wide, field, *faces], [(2, 56, 128), (2, 96, 128)],
        gather(message), scaled, wide_labels, *exchange(near, far, "slab"), scale,
    )
    t, message = call(
        next_image_kernel, [field, (n_slab // 2, 1, 128)], space,
        wide_w, w, *exchange(near, far, "cross"), sigma, element_matrix, ionic, r, z, q,
    )
    parts = lax.all_to_all(message, "slab", 0, 0, axis_index_groups=planes, tiled=True)
    parts = jnp.broadcast_to(jnp.sum(parts, 0)[None], (2 * n_cross, 1, 128))
    dots = lax.all_to_all(parts, ("slab", "cross"), 0, 0, axis_index_groups=columns, tiled=True)
    return tuple(call(finish_kernel, [(6, 6, 384)] * 2, [(128, 128), (384, 128)], dots, r, z, q, w, t))


def solution(mesh):
    return jax.shard_map(
        body,
        mesh=mesh,
        in_specs=(
            P("slab", "cross", None),
            P("slab", "cross", None),
            P(),
            P("slab", "cross", None),
            P(),
            P("slab", "cross", None),
        ),
        out_specs=(P("slab", "cross", None), P("slab", "cross", None)),
        check_vma=False,
    )
```

```python
import functools

import jax
import jax.numpy as jnp
from jax import lax
from jax.experimental import pallas as pl
from jax.experimental.pallas import tpu as pltpu
from jax.sharding import PartitionSpec as P

LABELS = 8
DAMPING = 0.8
COUPLING = 0.2
SHARE = 0.1
REACH = 3
NEAR = REACH + 1


F32 = jnp.float32
BF16 = jnp.bfloat16
SPAN = (-1, 0, 1)


def parity(axis):
    return lax.rem(lax.axis_index(axis), 2)


def lanes(shape):
    return lax.broadcasted_iota(jnp.int32, shape, len(shape) - 1)


def call(kernel, out_shapes, scratch, *operands, away=()):
    specs = [
        pl.BlockSpec(memory_space=pltpu.HBM if index in away else pltpu.VMEM)
        for index in range(len(operands))
    ]
    operands = [
        pltpu.with_memory_space_constraint(operand, pltpu.HBM) if index in away else operand
        for index, operand in enumerate(operands)
    ]
    return pl.pallas_call(
        kernel,
        out_shape=[jax.ShapeDtypeStruct(shape, F32) for shape in out_shapes],
        in_specs=specs,
        out_specs=[pl.BlockSpec(memory_space=pltpu.VMEM)] * len(out_shapes),
        scratch_shapes=[pltpu.VMEM(shape, F32) if isinstance(shape, tuple) else shape for shape in scratch],
        compiler_params=pltpu.CompilerParams(vmem_limit_bytes=24 << 20),
    )(*operands)


def restrict(field, labels):
    rows = []
    for label in range(LABELS):
        kept = jnp.sum(jnp.where(labels == label + 1.0, field, 0.0), axis=0)
        rows.append(jnp.sum(kept, axis=0, keepdims=True))
    sums = jnp.concatenate(rows, 0)
    even = lanes((8, 128)) % 2 == 0
    return sums + jnp.where(even, pltpu.roll(sums, 127, 1), pltpu.roll(sums, 1, 1))


def prolong(coarse, labels):
    row = lax.broadcasted_iota(jnp.int32, (16, 128), 0)
    field = jnp.zeros_like(labels)
    for label in range(LABELS):
        low, own, high = [coarse[step, label : label + 1, :] for step in range(3)]
        values = jnp.where(row < 3, low, jnp.where(row < 9, own, high))
        field = jnp.where(labels == label + 1.0, values[None], field)
    return field


def assemble(product_of, limit, total_ref):
    total_ref[...] = jnp.zeros_like(total_ref)
    start = lanes((16, 128)) == 0
    for i in range(-1, (limit + 2) // 3):
        low_a, high_a = max(0, -3 * i), min(4, limit - 3 * i)
        for j in SPAN:
            product = product_of((i + 1) * 3 + j + 1)
            last = pltpu.roll(product[48:64], 1, 1)
            pieces = [
                product[0:16] + jnp.where(start, 0.0, last),
                product[16:32],
                product[32:48],
            ]
            for c in range(3):
                for b in range(4):
                    y = 3 * j + b
                    if 0 <= y < 6:
                        x = 3 * i + low_a
                        rows = pieces[c][4 * b + low_a : 4 * b + high_a]
                        total_ref[c * 6 + y, x : x + high_a - low_a, :] += rows


def conductance(region, table_ref):
    value = jnp.zeros(region.shape, F32)
    for index in range(4):
        value = jnp.where(region == index + 1, table_ref[index : index + 1, :], value)
    return value


def unpack_kernel(source_hbm, potential_hbm, map_hbm, region_hbm, table_hbm, r_ref, ionic_ref, label_ref, coarse_ref,
                  own_ref, table_ref,
                  rows_ref, turned_ref, source_ref, potential_ref, map_ref, region_ref, values_ref, sems):
    copies = [
        pltpu.make_async_copy(away, here, sems.at[index])
        for index, (away, here) in enumerate(
            (
                (source_hbm, source_ref),
                (potential_hbm, potential_ref),
                (map_hbm, map_ref),
                (region_hbm, region_ref),
                (table_hbm, values_ref),
            )
        )
    ]
    for copy in copies:
        copy.start()
    rows_ref[...] = jnp.zeros_like(rows_ref)
    for copy in copies:
        copy.wait()
    for index in range(4):
        table_ref[index : index + 1, :] = jnp.full((1, 128), values_ref[index])
    for i in range(2):
        own_ref[2 * i : 2 * i + 2, :] = conductance(region_ref[i] + 1, table_ref)
    for y in range(6):
        for x in range(6):
            row = y * 6 + x
            rows_ref[row : row + 1, :] = source_ref[x, y : y + 1, :]
            rows_ref[36 + row : 37 + row, :] = potential_ref[x, y : y + 1, :]
            rows_ref[72 + row : 73 + row, :] = map_ref[x, y : y + 1, :].astype(F32)
    for piece in range(3):
        turned_ref[128 * piece : 128 * piece + 128, :] = rows_ref[:, 128 * piece : 128 * piece + 128].T
    r_ref[...] = jnp.zeros_like(r_ref)
    ionic_ref[...] = jnp.zeros_like(ionic_ref)
    label_ref[...] = jnp.zeros_like(label_ref)
    for c in range(3):
        split = turned_ref[pl.ds(c, 128, stride=3), :].T
        for y in range(6):
            r_ref[c * 6 + y, 0:6, :] = split[6 * y : 6 * y + 6]
            tangent = jnp.tanh(split[36 + 6 * y : 42 + 6 * y])
            ionic_ref[c * 6 + y, 0:6, :] = 1.0 + 2.0 * (1.0 - tangent * tangent)
            label_ref[c * 6 + y, 0:6, :] = split[72 + 6 * y : 78 + 6 * y] + 1.0
    coarse_ref[...] = restrict(r_ref[...], label_ref[...])


def send(odd, both_ref, near_ref, far_ref):
    near_ref[...] = both_ref[odd]
    far_ref[...] = both_ref[1 - odd]


def receive(odd, near_ref, far_ref, both_ref):
    both_ref[odd] = near_ref[...]
    both_ref[1 - odd] = far_ref[...]


def diagonal_kernel(corner_ref, below_ref, beside_ref, own_ref, table_ref, matrix_ref, r_ref, ionic_ref, label_ref, coarse_ref,
                    sigma_ref, diagonal_ref, scaled_ref, message_ref, near_ref, far_ref,
                    total_ref, both_ref):
    sigma_ref[0:1, :] = conductance(corner_ref[...], table_ref)
    sigma_ref[1:3, :] = conductance(below_ref[...], table_ref)
    for i in range(2):
        sigma_ref[3 + 3 * i : 4 + 3 * i, :] = conductance(beside_ref[i : i + 1, :], table_ref)
        sigma_ref[4 + 3 * i : 6 + 3 * i, :] = own_ref[2 * i : 2 * i + 2, :]
    square = (64, 64)
    eye = lax.broadcasted_iota(jnp.int32, square, 0) == lax.broadcasted_iota(jnp.int32, square, 1)
    corner = jnp.sum(jnp.where(eye, matrix_ref[...], 0.0), axis=1, keepdims=True)
    assemble(lambda e: corner * sigma_ref[e : e + 1, :], 6, total_ref)
    labels = label_ref[...]
    diagonal = jnp.where(labels == 0.0, 1.0, total_ref[...] + ionic_ref[...])
    diagonal_ref[...] = diagonal
    even = lanes((8, 128)) % 2 == 0
    message = jnp.where(even, coarse_ref[...], SHARE * restrict(diagonal, labels))
    message_ref[...] = jnp.broadcast_to(message[None], message_ref.shape)
    scaled_ref[...] = r_ref[...] / diagonal
    both_ref[...] = jnp.zeros_like(both_ref)
    for n in range(18):
        both_ref[0, 3 * n : 3 * n + 3, :] = scaled_ref[n, 3:6, :]
        both_ref[0, 56 + 3 * n : 59 + 3 * n, :] = label_ref[n, 3:6, :]
        both_ref[1, 4 * n : 4 * n + 4, :] = scaled_ref[n, 0:4, :]
        both_ref[1, 72 + 4 * n : 76 + 4 * n, :] = label_ref[n, 0:4, :]
        both_ref[1, 144 + n : 145 + n, :] = ionic_ref[n, 0:1, :]
        both_ref[1, 162 + n : 163 + n, :] = diagonal_ref[n, 0:1, :]
    both_ref[1, 180:183, :] = sigma_ref[3:6, :]
    send(parity("slab"), both_ref, near_ref, far_ref)


def along(values):
    lane = lanes(values.shape)
    row = lax.broadcasted_iota(jnp.int32, values.shape, 1)
    after = pltpu.roll(values, 7, 1)
    carried = jnp.where(lane < 126, pltpu.roll(after, 126, 2), 0.0)
    after = jnp.where(row == 7, carried, after)
    before = pltpu.roll(values, 1, 1)
    carried = jnp.where(lane >= 2, pltpu.roll(before, 2, 2), 0.0)
    return after + jnp.where(row == 0, carried, before)


def smooth(start, valid):
    level = start
    for sweep in range(REACH):
        beside = level[2:] + level[:-2] + along(level[1:-1])
        here = slice(sweep + 1, 2 * NEAR - sweep)
        level = start[here] + (1.0 - DAMPING) * level[1:-1] + (DAMPING * COUPLING) * beside
        level = level * valid[here]
    return level


def around(count):
    rows, valid = [], []
    for step in range(-NEAR, NEAR + 1):
        row = lax.axis_index("slab") + step
        inside = jnp.logical_and(row >= 0, row < count)
        rows.append(jnp.clip(row, 0, count - 1))
        valid.append(jnp.where(inside, jnp.ones((1, 8, 128), F32), 0.0))
    return rows, jnp.concatenate(valid, 0)


def even_part(tiles):
    even = lanes(tiles.shape) % 2 == 0
    return jnp.where(even, tiles, pltpu.roll(tiles, 1, tiles.ndim - 1))


def odd_part(tiles):
    even = lanes(tiles.shape) % 2 == 0
    return jnp.where(even, pltpu.roll(tiles, 127, tiles.ndim - 1), tiles)


def widen(field_ref, both_ref, up_start, down_start, wide_ref):
    wide_ref[...] = jnp.zeros_like(wide_ref)
    for n in range(18):
        wide_ref[n, 0:3, :] = both_ref[1, up_start + 3 * n : up_start + 3 * n + 3, :]
        wide_ref[n, 3:9, :] = field_ref[n, 0:6, :]
        wide_ref[n, 9:13, :] = both_ref[0, down_start + 4 * n : down_start + 4 * n + 4, :]


def send_cross(odd, width, wide_ref, own_ref, near_ref, far_ref, both_ref):
    own_ref[...] = jnp.zeros_like(own_ref)
    for n in range(18):
        own_ref[n, 0:6, :] = wide_ref[n, 3:9, :]
    both_ref[...] = jnp.zeros_like(both_ref)
    for c in range(3):
        for y in range(3):
            row = (3 * c + y) * width
            both_ref[0, row : row + width, :] = wide_ref[6 * c + 3 + y, 0:width, :]
        both_ref[1, width * c : width * c + width, :] = wide_ref[6 * c, 0:width, :]
    send(odd, both_ref, near_ref, far_ref)


def first_solve_kernel(gathered_ref, scaled_ref, label_ref, left_ref, right_ref,
                       wide_ref, z_ref, near_ref, far_ref, scale_ref, wide_label_ref, edge_ref, slab_ref, cross_ref):
    receive(parity("slab"), right_ref, left_ref, slab_ref)
    rows, valid = around(gathered_ref.shape[0])
    tiles = jnp.concatenate([gathered_ref[pl.ds(row, 1)] for row in rows], 0)
    sums = jnp.sum(gathered_ref[...], axis=0)
    inverse = valid / jnp.sqrt(odd_part(tiles))
    share = 1.0 / odd_part(sums)
    scale_ref[0 : 2 * NEAR + 1] = inverse
    scale_ref[2 * NEAR + 1] = share
    level = smooth(DAMPING * even_part(tiles) * inverse, valid)
    coarse = level * inverse[REACH : REACH + 3] + (even_part(sums) * share)[None]
    edge_ref[...] = slab_ref[0, 144:184, :]
    widen(label_ref, slab_ref, 56, 72, wide_label_ref)
    widen(scaled_ref, slab_ref, 0, 0, wide_ref)
    wide_ref[...] += prolong(coarse, wide_label_ref[...])
    send_cross(parity("cross"), 13, wide_ref, z_ref, near_ref, far_ref, cross_ref)


def next_solve_kernel(gathered_ref, scaled_ref, wide_label_ref, low_ref, scale_ref,
                      wide_ref, w_ref, near_ref, far_ref, cross_ref):
    rows, valid = around(gathered_ref.shape[0])
    tiles = jnp.concatenate([gathered_ref[pl.ds(row, 1)] for row in rows], 0)
    sums = jnp.sum(gathered_ref[...], axis=0)
    inverse = scale_ref[0 : 2 * NEAR + 1]
    level = smooth(DAMPING * tiles * inverse, valid)
    coarse = level * inverse[REACH : REACH + 3] + (sums * scale_ref[2 * NEAR + 1])[None]
    wide_ref[...] = jnp.zeros_like(wide_ref)
    for n in range(18):
        wide_ref[n, 0:3, :] = low_ref[3 * n : 3 * n + 3, :]
        wide_ref[n, 3:10, :] = scaled_ref[n, 0:7, :]
    wide_ref[...] += prolong(coarse, wide_label_ref[...])
    send_cross(parity("cross"), 10, wide_ref, w_ref, near_ref, far_ref, cross_ref)


def operate(limit, wide_ref, near_ref, far_ref, sigma_ref, matrix_ref, ionic_ref,
            cross_ref, grid_ref, local_ref, product_ref, total_ref):
    columns = range(-1, (limit + 2) // 3)
    width = 3 * len(columns) + 1
    for n in range(18):
        grid_ref[n // 6 * 10 + 3 + n % 6, 0:width, :] = wide_ref[n, 0:width, :]
    receive(parity("cross"), near_ref, far_ref, cross_ref)
    for c in range(3):
        for y in range(3):
            row = (3 * c + y) * width
            grid_ref[10 * c + y, 0:width, :] = cross_ref[1, row : row + width, :]
        grid_ref[10 * c + 9, 0:width, :] = cross_ref[0, width * c : width * c + width, :]
    end = lanes((width, 128)) == 127
    for y in range(10):
        grid_ref[30 + y, 0:width, :] = jnp.where(end, 0.0, pltpu.roll(grid_ref[y, 0:width, :], 127, 1))
    for i in columns:
        for j in SPAN:
            left = ((i + 1) * 3 + j + 1) * 128
            for c in range(4):
                for b in range(4):
                    row = 16 * c + 4 * b
                    n = c * 10 + 3 * (j + 1) + b
                    local_ref[row : row + 4, left : left + 128] = grid_ref[n, 3 * i + 3 : 3 * i + 7, :]
    matrix = matrix_ref[...]
    matrix_high = matrix.astype(BF16)
    matrix_low = (matrix - matrix_high.astype(F32)).astype(BF16)
    local = local_ref[...]
    high = local.astype(BF16)
    low = (local - high.astype(F32)).astype(BF16)
    dot = functools.partial(jnp.dot, preferred_element_type=F32)
    product_ref[...] = dot(matrix_high, high) + (dot(matrix_high, low) + dot(matrix_low, high))
    assemble(lambda e: product_ref[:, 128 * e : 128 * e + 128] * sigma_ref[e : e + 1, :], limit, total_ref)
    for n in range(18):
        total_ref[n, 0:limit, :] += ionic_ref[n, 0:limit, :] * wide_ref[n, 3 : 3 + limit, :]


def first_image_kernel(wide_ref, far_ref, near_ref, sigma_ref, matrix_ref, ionic_ref, diagonal_ref, label_ref, edge_ref,
                       q_ref, scaled_ref, message_ref, up_ref,
                       all_sigma_ref, all_ionic_ref, all_diagonal_ref, *scratch):
    all_sigma_ref[0:9, :] = sigma_ref[...]
    all_sigma_ref[9:12, :] = edge_ref[36:39, :]
    all_ionic_ref[...] = ionic_ref[...]
    all_diagonal_ref[...] = diagonal_ref[...]
    for n in range(18):
        all_ionic_ref[n, 6:7, :] = edge_ref[n : n + 1, :]
        beyond = edge_ref[18 + n : 19 + n, :]
        all_diagonal_ref[n, 6:7, :] = jnp.where(beyond == 0.0, jnp.inf, beyond)
    operate(7, wide_ref, near_ref, far_ref, all_sigma_ref, matrix_ref, all_ionic_ref, *scratch)
    image = scratch[-1][...]
    q_ref[...] = image
    message_ref[...] = jnp.broadcast_to(restrict(image, label_ref[...])[None], message_ref.shape)
    scaled_ref[...] = image / all_diagonal_ref[...]
    up_ref[...] = jnp.zeros_like(up_ref)
    for n in range(18):
        up_ref[3 * n : 3 * n + 3, :] = scaled_ref[n, 3:6, :]


def next_image_kernel(wide_ref, far_ref, near_ref, sigma_ref, matrix_ref, ionic_ref,
                      w_ref, r_ref, z_ref, q_ref, t_ref, message_ref, *scratch):
    operate(6, wide_ref, near_ref, far_ref, sigma_ref, matrix_ref, ionic_ref, *scratch)
    image = scratch[-1][...]
    t_ref[...] = image
    r, z, q, w = r_ref[...], z_ref[...], q_ref[...], w_ref[...]
    row = jnp.zeros((1, 128), F32)
    for index, (left, right) in enumerate(((r, z), (z, q), (r, w), (q, w), (z, image), (w, image))):
        part = jnp.sum(jnp.sum(left * right, axis=0), axis=0, keepdims=True)
        row = jnp.where(lanes((1, 128)) == index, jnp.sum(part, axis=1, keepdims=True), row)
    message_ref[...] = jnp.broadcast_to(row[None], message_ref.shape)


def finish_kernel(dots_ref, r_ref, z_ref, q_ref, w_ref, t_ref, solution_ref, residual_ref, rows_ref, turned_ref):
    dots = jnp.sum(dots_ref[...], axis=0)
    rz, zq, rw, qw, zt, wt = [dots[:, index : index + 1] for index in range(6)]
    alpha = rz / zq
    rz_next = alpha * (alpha * qw - rw)
    beta = rz_next / rz
    more = 1.0 + beta
    second = rz_next / (more * more * zq - more * alpha * (zt + qw) + alpha * alpha * wt)
    from_z = alpha + second * more
    from_w = second * alpha
    rows_ref[...] = jnp.zeros_like(rows_ref)
    for c in range(3):
        for y in range(6):
            n = 6 * c + y
            answer = from_z * z_ref[n] - from_w * w_ref[n]
            left = r_ref[n] - from_z * q_ref[n] + from_w * t_ref[n]
            rows_ref[6 * y : 6 * y + 6, :] = answer[0:6]
            rows_ref[36 + 6 * y : 42 + 6 * y, :] = left[0:6]
        turned_ref[pl.ds(c, 128, stride=3), :] = rows_ref[...].T
    for piece in range(3):
        back = turned_ref[128 * piece : 128 * piece + 128, :].T
        for y in range(6):
            for x in range(6):
                row = y * 6 + x
                solution_ref[x, y : y + 1, 128 * piece : 128 * piece + 128] = back[row : row + 1]
                residual_ref[x, y : y + 1, 128 * piece : 128 * piece + 128] = back[36 + row : 37 + row]


def body(adjoint_source, potential, element_matrix, region_labels, conductivity, restriction_map):
    n_slab = lax.axis_size("slab")
    n_cross = lax.axis_size("cross")
    columns = [
        [slab * n_cross + cross for slab in (2 * pair, 2 * pair + 1) for cross in range(n_cross)]
        for pair in range(n_slab // 2)
    ]
    planes = [[2 * pair + low for pair in range(n_slab // 2)] for low in range(2)]
    def shifted(value, axis, step):
        count = lax.axis_size(axis)
        pairs = [(source, source + step) for source in range(count) if 0 <= source + step < count]
        return lax.ppermute(value, axis, pairs)

    def gather(copies):
        return lax.all_to_all(copies, "slab", 0, 0, tiled=True)

    field, wide = (18, 8, 128), (18, 16, 128)

    def space(columns, rows):
        return [(2, rows, 128), (40, 16, 128), (64, 384 * columns), (64, 384 * columns), field]

    regions = region_labels + 1
    pairs = [
        (here * n_cross + beside, (here + 1) * n_cross + beside + 1)
        for here in range(n_slab - 1)
        for beside in range(n_cross - 1)
    ]
    corner = lax.ppermute(regions[1, 1:2], ("slab", "cross"), pairs)
    below = shifted(regions[1], "slab", 1)
    beside = shifted(regions[:, 1], "cross", 1)
    r, ionic, labels, coarse, own, table = call(
        unpack_kernel, [field] * 3 + [(8, 128), (4, 128), (4, 128)],
        [(128, 384), (384, 128), (6, 6, 384), (6, 6, 384), pltpu.VMEM((6, 6, 384), jnp.int32),
         pltpu.VMEM((2, 2, 128), jnp.int32), pltpu.SMEM((4,), F32), pltpu.SemaphoreType.DMA((5,))],
        adjoint_source, potential, restriction_map, region_labels, conductivity, away=(0, 1, 2, 3, 4),
    )
    sigma, diagonal, scaled, message, near, far = call(
        diagonal_kernel, [(9, 128), field, field, (n_slab, 8, 128), (184, 128), (184, 128)],
        [field, (2, 184, 128)],
        corner, below, beside, own, table, element_matrix, r, ionic, labels, coarse,
    )

    def exchange(near, far, axis):
        count = lax.axis_size(axis)
        far_pairs = [(c, c + 1) for c in range(1, count - 1, 2)]
        far_pairs += [(above, c) for c, above in far_pairs]
        far = lax.ppermute(far, axis, far_pairs)
        return far, lax.ppermute(near, axis, [(c, c ^ 1) for c in range(count)])

    wide_z, z, near, far, scale, wide_labels, edge = call(
        first_solve_kernel, [wide, field, (120, 128), (120, 128), (10, 8, 128), wide, (40, 128)],
        [(2, 184, 128), (2, 120, 128)],
        gather(message), scaled, labels, *exchange(near, far, "slab"),
    )
    q, scaled, message, up = call(
        first_image_kernel, [field, field, (n_slab, 8, 128), (56, 128)],
        [(12, 128), field, field, *space(4, 120)],
        wide_z, *exchange(near, far, "cross"), sigma, element_matrix, ionic, diagonal, labels, edge,
    )
    wide_w, w, near, far = call(
        next_solve_kernel, [wide, field, (96, 128), (96, 128)], [(2, 96, 128)],
        gather(message), scaled, wide_labels, shifted(up, "slab", 1), scale,
    )
    t, message = call(
        next_image_kernel, [field, (n_slab // 2, 1, 128)], space(3, 96),
        wide_w, *exchange(near, far, "cross"), sigma, element_matrix, ionic, w, r, z, q,
    )
    parts = lax.all_to_all(message, "slab", 0, 0, axis_index_groups=planes, tiled=True)
    parts = jnp.broadcast_to(jnp.sum(parts, 0)[None], (2 * n_cross, 1, 128))
    dots = lax.all_to_all(parts, ("slab", "cross"), 0, 0, axis_index_groups=columns, tiled=True)
    return tuple(call(finish_kernel, [(6, 6, 384)] * 2, [(128, 128), (384, 128)], dots, r, z, q, w, t))


def solution(mesh):
    return jax.shard_map(
        body,
        mesh=mesh,
        in_specs=(
            P("slab", "cross", None),
            P("slab", "cross", None),
            P(),
            P("slab", "cross", None),
            P(),
            P("slab", "cross", None),
        ),
        out_specs=(P("slab", "cross", None), P("slab", "cross", None)),
        check_vma=False,
    )
```

```python
import functools

import jax
import jax.numpy as jnp
from jax import lax
from jax.experimental import pallas as pl
from jax.experimental.pallas import tpu as pltpu
from jax.sharding import PartitionSpec as P

LABELS = 8
DAMPING = 0.8
COUPLING = 0.2
SHARE = 0.1
REACH = 3
NEAR = REACH + 1


F32 = jnp.float32
BF16 = jnp.bfloat16
SPAN = (-1, 0, 1)


def parity(axis):
    return lax.rem(lax.axis_index(axis), 2)


def lanes(shape):
    return lax.broadcasted_iota(jnp.int32, shape, len(shape) - 1)


def call(kernel, out_shapes, scratch, *operands, away=()):
    specs = [
        pl.BlockSpec(memory_space=pltpu.HBM if index in away else pltpu.VMEM)
        for index in range(len(operands))
    ]
    operands = [
        pltpu.with_memory_space_constraint(operand, pltpu.HBM) if index in away else operand
        for index, operand in enumerate(operands)
    ]
    return pl.pallas_call(
        kernel,
        out_shape=[jax.ShapeDtypeStruct(shape, F32) for shape in out_shapes],
        in_specs=specs,
        out_specs=[pl.BlockSpec(memory_space=pltpu.VMEM)] * len(out_shapes),
        scratch_shapes=[pltpu.VMEM(shape, F32) if isinstance(shape, tuple) else shape for shape in scratch],
        compiler_params=pltpu.CompilerParams(vmem_limit_bytes=24 << 20),
    )(*operands)


def restrict(field, labels):
    rows = []
    for label in range(LABELS):
        kept = jnp.sum(jnp.where(labels == label + 1.0, field, 0.0), axis=0)
        rows.append(jnp.sum(kept, axis=0, keepdims=True))
    sums = jnp.concatenate(rows, 0)
    even = lanes((8, 128)) % 2 == 0
    return sums + jnp.where(even, pltpu.roll(sums, 127, 1), pltpu.roll(sums, 1, 1))


def prolong(coarse, labels):
    row = lax.broadcasted_iota(jnp.int32, (16, 128), 0)
    field = jnp.zeros_like(labels)
    for label in range(LABELS):
        low, own, high = [coarse[step, label : label + 1, :] for step in range(3)]
        values = jnp.where(row < 3, low, jnp.where(row < 9, own, high))
        field = jnp.where(labels == label + 1.0, values[None], field)
    return field


def assemble(product_of, limit, total_ref):
    total_ref[...] = jnp.zeros_like(total_ref)
    start = lanes((16, 128)) == 0
    for i in range(-1, (limit + 2) // 3):
        low_a, high_a = max(0, -3 * i), min(4, limit - 3 * i)
        for j in SPAN:
            product = product_of((i + 1) * 3 + j + 1)
            last = pltpu.roll(product[48:64], 1, 1)
            pieces = [
                product[0:16] + jnp.where(start, 0.0, last),
                product[16:32],
                product[32:48],
            ]
            for c in range(3):
                for b in range(4):
                    y = 3 * j + b
                    if 0 <= y < 6:
                        x = 3 * i + low_a
                        rows = pieces[c][4 * b + low_a : 4 * b + high_a]
                        total_ref[c * 6 + y, x : x + high_a - low_a, :] += rows


def conductance(region, table_ref):
    value = jnp.zeros(region.shape, F32)
    for index in range(4):
        value = jnp.where(region == index + 1, table_ref[index : index + 1, :], value)
    return value


def unpack_kernel(source_hbm, potential_hbm, map_hbm, region_hbm, table_hbm, r_ref, ionic_ref, label_ref, coarse_ref,
                  own_ref, table_ref,
                  rows_ref, turned_ref, source_ref, potential_ref, map_ref, region_ref, values_ref, sems):
    copies = [
        pltpu.make_async_copy(away, here, sems.at[index])
        for index, (away, here) in enumerate(
            (
                (source_hbm, source_ref),
                (potential_hbm, potential_ref),
                (map_hbm, map_ref),
                (region_hbm, region_ref),
                (table_hbm, values_ref),
            )
        )
    ]
    for copy in copies:
        copy.start()
    rows_ref[...] = jnp.zeros_like(rows_ref)
    for copy in copies:
        copy.wait()
    for index in range(4):
        table_ref[index : index + 1, :] = jnp.full((1, 128), values_ref[index])
    for i in range(2):
        own_ref[2 * i : 2 * i + 2, :] = conductance(region_ref[i] + 1, table_ref)
    for y in range(6):
        for x in range(6):
            row = y * 6 + x
            rows_ref[row : row + 1, :] = source_ref[x, y : y + 1, :]
            rows_ref[36 + row : 37 + row, :] = potential_ref[x, y : y + 1, :]
            rows_ref[72 + row : 73 + row, :] = map_ref[x, y : y + 1, :].astype(F32)
    for piece in range(3):
        turned_ref[128 * piece : 128 * piece + 128, :] = rows_ref[:, 128 * piece : 128 * piece + 128].T
    r_ref[...] = jnp.zeros_like(r_ref)
    ionic_ref[...] = jnp.zeros_like(ionic_ref)
    label_ref[...] = jnp.zeros_like(label_ref)
    for c in range(3):
        split = turned_ref[pl.ds(c, 128, stride=3), :].T
        for y in range(6):
            r_ref[c * 6 + y, 0:6, :] = split[6 * y : 6 * y + 6]
            tangent = jnp.tanh(split[36 + 6 * y : 42 + 6 * y])
            ionic_ref[c * 6 + y, 0:6, :] = 1.0 + 2.0 * (1.0 - tangent * tangent)
            label_ref[c * 6 + y, 0:6, :] = split[72 + 6 * y : 78 + 6 * y] + 1.0
    coarse_ref[...] = restrict(r_ref[...], label_ref[...])


def send(odd, both_ref, near_ref, far_ref):
    near_ref[...] = both_ref[odd]
    far_ref[...] = both_ref[1 - odd]


def receive(odd, near_ref, far_ref, both_ref):
    both_ref[odd] = near_ref[...]
    both_ref[1 - odd] = far_ref[...]


def diagonal_kernel(own_ref, corner_ref, below_ref, beside_ref, table_ref, matrix_ref, r_ref, ionic_ref, label_ref, coarse_ref,
                    sigma_ref, diagonal_ref, scaled_ref, message_ref, near_ref, far_ref,
                    total_ref, both_ref):
    sigma_ref[0:1, :] = conductance(corner_ref[...], table_ref)
    sigma_ref[1:3, :] = conductance(below_ref[...], table_ref)
    for i in range(2):
        sigma_ref[3 + 3 * i : 4 + 3 * i, :] = conductance(beside_ref[i : i + 1, :], table_ref)
        sigma_ref[4 + 3 * i : 6 + 3 * i, :] = own_ref[2 * i : 2 * i + 2, :]
    square = (64, 64)
    eye = lax.broadcasted_iota(jnp.int32, square, 0) == lax.broadcasted_iota(jnp.int32, square, 1)
    corner = jnp.sum(jnp.where(eye, matrix_ref[...], 0.0), axis=1, keepdims=True)
    assemble(lambda e: corner * sigma_ref[e : e + 1, :], 6, total_ref)
    labels = label_ref[...]
    diagonal = jnp.where(labels == 0.0, 1.0, total_ref[...] + ionic_ref[...])
    diagonal_ref[...] = diagonal
    even = lanes((8, 128)) % 2 == 0
    message = jnp.where(even, coarse_ref[...], SHARE * restrict(diagonal, labels))
    message_ref[...] = jnp.broadcast_to(message[None], message_ref.shape)
    scaled_ref[...] = r_ref[...] / diagonal
    both_ref[...] = jnp.zeros_like(both_ref)
    for n in range(18):
        both_ref[0, 3 * n : 3 * n + 3, :] = scaled_ref[n, 3:6, :]
        both_ref[0, 56 + 3 * n : 59 + 3 * n, :] = label_ref[n, 3:6, :]
        both_ref[1, 4 * n : 4 * n + 4, :] = scaled_ref[n, 0:4, :]
        both_ref[1, 72 + 4 * n : 76 + 4 * n, :] = label_ref[n, 0:4, :]
        both_ref[1, 144 + n : 145 + n, :] = ionic_ref[n, 0:1, :]
        both_ref[1, 162 + n : 163 + n, :] = diagonal_ref[n, 0:1, :]
    both_ref[1, 180:183, :] = sigma_ref[3:6, :]
    send(parity("slab"), both_ref, near_ref, far_ref)


def halved(coarse):
    return jnp.where(lanes((4, 128)) % 2 == 0, coarse[0:4], coarse[4:8])


def restored(tiles):
    return jnp.concatenate([even_part(tiles), odd_part(tiles)], tiles.ndim - 2)


def along(values):
    lane = lanes(values.shape)
    row = lax.broadcasted_iota(jnp.int32, values.shape, 1)
    after = pltpu.roll(values, 7, 1)
    carried = jnp.where(lane < 126, pltpu.roll(after, 126, 2), 0.0)
    after = jnp.where(row == 7, carried, after)
    before = pltpu.roll(values, 1, 1)
    carried = jnp.where(lane >= 2, pltpu.roll(before, 2, 2), 0.0)
    return after + jnp.where(row == 0, carried, before)


def smooth(start, valid):
    level = start
    for sweep in range(REACH):
        beside = level[2:] + level[:-2] + along(level[1:-1])
        here = slice(sweep + 1, 2 * NEAR - sweep)
        level = start[here] + (1.0 - DAMPING) * level[1:-1] + (DAMPING * COUPLING) * beside
        level = level * valid[here]
    return level


def around(count):
    rows, valid = [], []
    for step in range(-NEAR, NEAR + 1):
        row = lax.axis_index("slab") + step
        inside = jnp.logical_and(row >= 0, row < count)
        rows.append(jnp.clip(row, 0, count - 1))
        valid.append(jnp.where(inside, jnp.ones((1, 8, 128), F32), 0.0))
    return rows, jnp.concatenate(valid, 0)


def even_part(tiles):
    even = lanes(tiles.shape) % 2 == 0
    return jnp.where(even, tiles, pltpu.roll(tiles, 1, tiles.ndim - 1))


def odd_part(tiles):
    even = lanes(tiles.shape) % 2 == 0
    return jnp.where(even, pltpu.roll(tiles, 127, tiles.ndim - 1), tiles)


def widen(field_ref, both_ref, up_start, down_start, wide_ref):
    wide_ref[...] = jnp.zeros_like(wide_ref)
    for n in range(18):
        wide_ref[n, 0:3, :] = both_ref[1, up_start + 3 * n : up_start + 3 * n + 3, :]
        wide_ref[n, 3:9, :] = field_ref[n, 0:6, :]
        wide_ref[n, 9:13, :] = both_ref[0, down_start + 4 * n : down_start + 4 * n + 4, :]


def send_cross(odd, width, wide_ref, own_ref, near_ref, far_ref, both_ref):
    own_ref[...] = jnp.zeros_like(own_ref)
    for n in range(18):
        own_ref[n, 0:6, :] = wide_ref[n, 3:9, :]
    both_ref[...] = jnp.zeros_like(both_ref)
    for c in range(3):
        for y in range(3):
            row = (3 * c + y) * width
            both_ref[0, row : row + width, :] = wide_ref[6 * c + 3 + y, 0:width, :]
        both_ref[1, width * c : width * c + width, :] = wide_ref[6 * c, 0:width, :]
    send(odd, both_ref, near_ref, far_ref)


def first_solve_kernel(gathered_ref, scaled_ref, label_ref, left_ref, right_ref,
                       wide_ref, z_ref, near_ref, far_ref, scale_ref, wide_label_ref, edge_ref, slab_ref, cross_ref):
    receive(parity("slab"), right_ref, left_ref, slab_ref)
    rows, valid = around(gathered_ref.shape[0])
    tiles = jnp.concatenate([gathered_ref[pl.ds(row, 1)] for row in rows], 0)
    sums = jnp.sum(gathered_ref[...], axis=0)
    inverse = valid / jnp.sqrt(odd_part(tiles))
    share = 1.0 / odd_part(sums)
    scale_ref[0 : 2 * NEAR + 1] = inverse
    scale_ref[2 * NEAR + 1] = share
    level = smooth(DAMPING * even_part(tiles) * inverse, valid)
    coarse = level * inverse[REACH : REACH + 3] + (even_part(sums) * share)[None]
    edge_ref[...] = slab_ref[0, 144:184, :]
    widen(label_ref, slab_ref, 56, 72, wide_label_ref)
    widen(scaled_ref, slab_ref, 0, 0, wide_ref)
    wide_ref[...] += prolong(coarse, wide_label_ref[...])
    send_cross(parity("cross"), 13, wide_ref, z_ref, near_ref, far_ref, cross_ref)


def next_solve_kernel(gathered_ref, scaled_ref, wide_label_ref, low_ref, scale_ref,
                      wide_ref, w_ref, near_ref, far_ref, cross_ref):
    rows, valid = around(gathered_ref.shape[0])
    tiles = jnp.concatenate([gathered_ref[pl.ds(row, 1)] for row in rows], 0)
    tiles = restored(tiles)
    sums = restored(jnp.sum(gathered_ref[...], axis=0))
    inverse = scale_ref[0 : 2 * NEAR + 1]
    level = smooth(DAMPING * tiles * inverse, valid)
    coarse = level * inverse[REACH : REACH + 3] + (sums * scale_ref[2 * NEAR + 1])[None]
    wide_ref[...] = jnp.zeros_like(wide_ref)
    for n in range(18):
        wide_ref[n, 0:3, :] = low_ref[3 * n : 3 * n + 3, :]
        wide_ref[n, 3:10, :] = scaled_ref[n, 0:7, :]
    wide_ref[...] += prolong(coarse, wide_label_ref[...])
    send_cross(parity("cross"), 10, wide_ref, w_ref, near_ref, far_ref, cross_ref)


def operate(limit, wide_ref, near_ref, far_ref, sigma_ref, matrix_ref, ionic_ref,
            cross_ref, grid_ref, local_ref, product_ref, total_ref):
    columns = range(-1, (limit + 2) // 3)
    width = 3 * len(columns) + 1
    for n in range(18):
        grid_ref[n // 6 * 10 + 3 + n % 6, 0:width, :] = wide_ref[n, 0:width, :]
    receive(parity("cross"), near_ref, far_ref, cross_ref)
    for c in range(3):
        for y in range(3):
            row = (3 * c + y) * width
            grid_ref[10 * c + y, 0:width, :] = cross_ref[1, row : row + width, :]
        grid_ref[10 * c + 9, 0:width, :] = cross_ref[0, width * c : width * c + width, :]
    end = lanes((width, 128)) == 127
    for y in range(10):
        grid_ref[30 + y, 0:width, :] = jnp.where(end, 0.0, pltpu.roll(grid_ref[y, 0:width, :], 127, 1))
    for i in columns:
        for j in SPAN:
            left = ((i + 1) * 3 + j + 1) * 128
            for c in range(4):
                for b in range(4):
                    row = 16 * c + 4 * b
                    n = c * 10 + 3 * (j + 1) + b
                    local_ref[row : row + 4, left : left + 128] = grid_ref[n, 3 * i + 3 : 3 * i + 7, :]
    matrix = matrix_ref[...]
    matrix_high = matrix.astype(BF16)
    matrix_low = (matrix - matrix_high.astype(F32)).astype(BF16)
    local = local_ref[...]
    high = local.astype(BF16)
    low = (local - high.astype(F32)).astype(BF16)
    dot = functools.partial(jnp.dot, preferred_element_type=F32)
    product_ref[...] = dot(matrix_high, high) + (dot(matrix_high, low) + dot(matrix_low, high))
    assemble(lambda e: product_ref[:, 128 * e : 128 * e + 128] * sigma_ref[e : e + 1, :], limit, total_ref)
    for n in range(18):
        total_ref[n, 0:limit, :] += ionic_ref[n, 0:limit, :] * wide_ref[n, 3 : 3 + limit, :]


def first_image_kernel(wide_ref, far_ref, near_ref, sigma_ref, matrix_ref, ionic_ref, diagonal_ref, label_ref, edge_ref,
                       q_ref, scaled_ref, message_ref, up_ref,
                       all_sigma_ref, all_ionic_ref, all_diagonal_ref, *scratch):
    all_sigma_ref[0:9, :] = sigma_ref[...]
    all_sigma_ref[9:12, :] = edge_ref[36:39, :]
    all_ionic_ref[...] = ionic_ref[...]
    all_diagonal_ref[...] = diagonal_ref[...]
    for n in range(18):
        all_ionic_ref[n, 6:7, :] = edge_ref[n : n + 1, :]
        beyond = edge_ref[18 + n : 19 + n, :]
        all_diagonal_ref[n, 6:7, :] = jnp.where(beyond == 0.0, jnp.inf, beyond)
    operate(7, wide_ref, near_ref, far_ref, all_sigma_ref, matrix_ref, all_ionic_ref, *scratch)
    image = scratch[-1][...]
    q_ref[...] = image
    message_ref[...] = jnp.broadcast_to(halved(restrict(image, label_ref[...]))[None], message_ref.shape)
    scaled_ref[...] = image / all_diagonal_ref[...]
    up_ref[...] = jnp.zeros_like(up_ref)
    for n in range(18):
        up_ref[3 * n : 3 * n + 3, :] = scaled_ref[n, 3:6, :]


def next_image_kernel(wide_ref, far_ref, near_ref, sigma_ref, matrix_ref, ionic_ref,
                      w_ref, r_ref, z_ref, q_ref, t_ref, message_ref, *scratch):
    operate(6, wide_ref, near_ref, far_ref, sigma_ref, matrix_ref, ionic_ref, *scratch)
    image = scratch[-1][...]
    t_ref[...] = image
    r, z, q, w = r_ref[...], z_ref[...], q_ref[...], w_ref[...]
    row = jnp.zeros((1, 128), F32)
    for index, (left, right) in enumerate(((r, z), (z, q), (r, w), (q, w), (z, image), (w, image))):
        part = jnp.sum(jnp.sum(left * right, axis=0), axis=0, keepdims=True)
        row = jnp.where(lanes((1, 128)) == index, jnp.sum(part, axis=1, keepdims=True), row)
    message_ref[...] = jnp.broadcast_to(row[None], message_ref.shape)


def finish_kernel(dots_ref, r_ref, z_ref, q_ref, w_ref, t_ref, solution_ref, residual_ref, rows_ref, turned_ref):
    dots = jnp.sum(dots_ref[...], axis=0)
    rz, zq, rw, qw, zt, wt = [dots[:, index : index + 1] for index in range(6)]
    alpha = rz / zq
    rz_next = alpha * (alpha * qw - rw)
    beta = rz_next / rz
    more = 1.0 + beta
    second = rz_next / (more * more * zq - more * alpha * (zt + qw) + alpha * alpha * wt)
    from_z = alpha + second * more
    from_w = second * alpha
    rows_ref[...] = jnp.zeros_like(rows_ref)
    for c in range(3):
        for y in range(6):
            n = 6 * c + y
            answer = from_z * z_ref[n] - from_w * w_ref[n]
            left = r_ref[n] - from_z * q_ref[n] + from_w * t_ref[n]
            rows_ref[6 * y : 6 * y + 6, :] = answer[0:6]
            rows_ref[36 + 6 * y : 42 + 6 * y, :] = left[0:6]
        turned_ref[pl.ds(c, 128, stride=3), :] = rows_ref[...].T
    for piece in range(3):
        back = turned_ref[128 * piece : 128 * piece + 128, :].T
        for y in range(6):
            for x in range(6):
                row = y * 6 + x
                solution_ref[x, y : y + 1, 128 * piece : 128 * piece + 128] = back[row : row + 1]
                residual_ref[x, y : y + 1, 128 * piece : 128 * piece + 128] = back[36 + row : 37 + row]


def body(adjoint_source, potential, element_matrix, region_labels, conductivity, restriction_map):
    n_slab = lax.axis_size("slab")
    n_cross = lax.axis_size("cross")
    columns = [
        [slab * n_cross + cross for slab in (2 * pair, 2 * pair + 1) for cross in range(n_cross)]
        for pair in range(n_slab // 2)
    ]
    planes = [[2 * pair + low for pair in range(n_slab // 2)] for low in range(2)]
    def shifted(value, axis, step):
        count = lax.axis_size(axis)
        pairs = [(source, source + step) for source in range(count) if 0 <= source + step < count]
        return lax.ppermute(value, axis, pairs)

    def gather(copies):
        return lax.all_to_all(copies, "slab", 0, 0, tiled=True)

    field, wide = (18, 8, 128), (18, 16, 128)

    def space(columns, rows):
        return [(2, rows, 128), (40, 16, 128), (64, 384 * columns), (64, 384 * columns), field]

    regions = region_labels + 1
    pairs = [
        (here * n_cross + beside, (here + 1) * n_cross + beside + 1)
        for here in range(n_slab - 1)
        for beside in range(n_cross - 1)
    ]
    corner = lax.ppermute(regions[1, 1:2], ("slab", "cross"), pairs)
    below = shifted(regions[1], "slab", 1)
    beside = shifted(regions[:, 1], "cross", 1)
    r, ionic, labels, coarse, own, table = call(
        unpack_kernel, [field] * 3 + [(8, 128), (4, 128), (4, 128)],
        [(128, 384), (384, 128), (6, 6, 384), (6, 6, 384), pltpu.VMEM((6, 6, 384), jnp.int32),
         pltpu.VMEM((2, 2, 128), jnp.int32), pltpu.SMEM((4,), F32), pltpu.SemaphoreType.DMA((5,))],
        adjoint_source, potential, restriction_map, region_labels, conductivity, away=(0, 1, 2, 3, 4),
    )
    sigma, diagonal, scaled, message, near, far = call(
        diagonal_kernel, [(9, 128), field, field, (n_slab, 8, 128), (184, 128), (184, 128)],
        [field, (2, 184, 128)],
        own, corner, below, beside, table, element_matrix, r, ionic, labels, coarse,
    )

    def exchange(near, far, axis):
        count = lax.axis_size(axis)
        far_pairs = [(c, c + 1) for c in range(1, count - 1, 2)]
        far_pairs += [(above, c) for c, above in far_pairs]
        far = lax.ppermute(far, axis, far_pairs)
        return far, lax.ppermute(near, axis, [(c, c ^ 1) for c in range(count)])

    wide_z, z, near, far, scale, wide_labels, edge = call(
        first_solve_kernel, [wide, field, (120, 128), (120, 128), (10, 8, 128), wide, (40, 128)],
        [(2, 184, 128), (2, 120, 128)],
        gather(message), scaled, labels, *exchange(near, far, "slab"),
    )
    q, scaled, message, up = call(
        first_image_kernel, [field, field, (n_slab, 4, 128), (56, 128)],
        [(12, 128), field, field, *space(4, 120)],
        wide_z, *exchange(near, far, "cross"), sigma, element_matrix, ionic, diagonal, labels, edge,
    )
    wide_w, w, near, far = call(
        next_solve_kernel, [wide, field, (96, 128), (96, 128)], [(2, 96, 128)],
        gather(message), scaled, wide_labels, shifted(up, "slab", 1), scale,
    )
    t, message = call(
        next_image_kernel, [field, (n_slab // 2, 1, 128)], space(3, 96),
        wide_w, *exchange(near, far, "cross"), sigma, element_matrix, ionic, w, r, z, q,
    )
    parts = lax.all_to_all(message, "slab", 0, 0, axis_index_groups=planes, tiled=True)
    parts = jnp.broadcast_to(jnp.sum(parts, 0)[None], (2 * n_cross, 1, 128))
    dots = lax.all_to_all(parts, ("slab", "cross"), 0, 0, axis_index_groups=columns, tiled=True)
    return tuple(call(finish_kernel, [(6, 6, 384)] * 2, [(128, 128), (384, 128)], dots, r, z, q, w, t))


def solution(mesh):
    return jax.shard_map(
        body,
        mesh=mesh,
        in_specs=(
            P("slab", "cross", None),
            P("slab", "cross", None),
            P(),
            P("slab", "cross", None),
            P(),
            P("slab", "cross", None),
        ),
        out_specs=(P("slab", "cross", None), P("slab", "cross", None)),
        check_vma=False,
    )
```

```python
import functools

import jax
import jax.numpy as jnp
from jax import lax
from jax.experimental import pallas as pl
from jax.experimental.pallas import tpu as pltpu
from jax.sharding import PartitionSpec as P

LABELS = 8
DAMPING = 0.8
COUPLING = 0.2
SHARE = 0.1
REACH = 3
NEAR = REACH + 1


F32 = jnp.float32
BF16 = jnp.bfloat16
SPAN = (-1, 0, 1)


def parity(axis):
    return lax.rem(lax.axis_index(axis), 2)


def lanes(shape):
    return lax.broadcasted_iota(jnp.int32, shape, len(shape) - 1)


def call(kernel, out_shapes, scratch, *operands, away=()):
    specs = [
        pl.BlockSpec(memory_space=pltpu.HBM if index in away else pltpu.VMEM)
        for index in range(len(operands))
    ]
    operands = [
        pltpu.with_memory_space_constraint(operand, pltpu.HBM) if index in away else operand
        for index, operand in enumerate(operands)
    ]
    return pl.pallas_call(
        kernel,
        out_shape=[jax.ShapeDtypeStruct(shape, F32) for shape in out_shapes],
        in_specs=specs,
        out_specs=[pl.BlockSpec(memory_space=pltpu.VMEM)] * len(out_shapes),
        scratch_shapes=[pltpu.VMEM(shape, F32) if isinstance(shape, tuple) else shape for shape in scratch],
        compiler_params=pltpu.CompilerParams(vmem_limit_bytes=24 << 20),
    )(*operands)


def restrict(field, labels):
    rows = []
    for label in range(LABELS):
        kept = jnp.sum(jnp.where(labels == label + 1.0, field, 0.0), axis=0)
        rows.append(jnp.sum(kept, axis=0, keepdims=True))
    sums = jnp.concatenate(rows, 0)
    even = lanes((8, 128)) % 2 == 0
    return sums + jnp.where(even, pltpu.roll(sums, 127, 1), pltpu.roll(sums, 1, 1))


def prolong(coarse, labels):
    row = lax.broadcasted_iota(jnp.int32, (16, 128), 0)
    field = jnp.zeros_like(labels)
    for label in range(LABELS):
        low, own, high = [coarse[step, label : label + 1, :] for step in range(3)]
        values = jnp.where(row < 3, low, jnp.where(row < 9, own, high))
        field = jnp.where(labels == label + 1.0, values[None], field)
    return field


def assemble(product_of, limit, total_ref):
    total_ref[...] = jnp.zeros_like(total_ref)
    start = lanes((16, 128)) == 0
    for i in range(-1, (limit + 2) // 3):
        low_a, high_a = max(0, -3 * i), min(4, limit - 3 * i)
        for j in SPAN:
            product = product_of((i + 1) * 3 + j + 1)
            last = pltpu.roll(product[48:64], 1, 1)
            pieces = [
                product[0:16] + jnp.where(start, 0.0, last),
                product[16:32],
                product[32:48],
            ]
            for c in range(3):
                for b in range(4):
                    y = 3 * j + b
                    if 0 <= y < 6:
                        x = 3 * i + low_a
                        rows = pieces[c][4 * b + low_a : 4 * b + high_a]
                        total_ref[c * 6 + y, x : x + high_a - low_a, :] += rows


def conductance(region, table_ref):
    value = jnp.zeros(region.shape, F32)
    for index in range(4):
        value = jnp.where(region == index + 1, table_ref[index : index + 1, :], value)
    return value


def unpack_kernel(source_hbm, potential_hbm, map_hbm, region_hbm, table_hbm, r_ref, ionic_ref, label_ref, coarse_ref,
                  own_ref, table_ref,
                  rows_ref, turned_ref, source_ref, potential_ref, map_ref, region_ref, values_ref, sems):
    copies = [
        pltpu.make_async_copy(away, here, sems.at[index])
        for index, (away, here) in enumerate(
            (
                (source_hbm, source_ref),
                (potential_hbm, potential_ref),
                (map_hbm, map_ref),
                (region_hbm, region_ref),
                (table_hbm, values_ref),
            )
        )
    ]
    for copy in copies:
        copy.start()
    rows_ref[...] = jnp.zeros_like(rows_ref)
    for copy in copies:
        copy.wait()
    for index in range(4):
        table_ref[index : index + 1, :] = jnp.full((1, 128), values_ref[index])
    for i in range(2):
        own_ref[2 * i : 2 * i + 2, :] = conductance(region_ref[i] + 1, table_ref)
    for y in range(6):
        for x in range(6):
            row = y * 6 + x
            rows_ref[row : row + 1, :] = source_ref[x, y : y + 1, :]
            rows_ref[36 + row : 37 + row, :] = potential_ref[x, y : y + 1, :]
            rows_ref[72 + row : 73 + row, :] = map_ref[x, y : y + 1, :].astype(F32)
    for piece in range(3):
        turned_ref[128 * piece : 128 * piece + 128, :] = rows_ref[:, 128 * piece : 128 * piece + 128].T
    r_ref[...] = jnp.zeros_like(r_ref)
    ionic_ref[...] = jnp.zeros_like(ionic_ref)
    label_ref[...] = jnp.zeros_like(label_ref)
    for c in range(3):
        split = turned_ref[pl.ds(c, 128, stride=3), :].T
        for y in range(6):
            r_ref[c * 6 + y, 0:6, :] = split[6 * y : 6 * y + 6]
            tangent = jnp.tanh(split[36 + 6 * y : 42 + 6 * y])
            ionic_ref[c * 6 + y, 0:6, :] = 1.0 + 2.0 * (1.0 - tangent * tangent)
            label_ref[c * 6 + y, 0:6, :] = split[72 + 6 * y : 78 + 6 * y] + 1.0
    coarse_ref[...] = restrict(r_ref[...], label_ref[...])


def send(odd, both_ref, near_ref, far_ref):
    near_ref[...] = both_ref[odd]
    far_ref[...] = both_ref[1 - odd]


def receive(odd, near_ref, far_ref, both_ref):
    both_ref[odd] = near_ref[...]
    both_ref[1 - odd] = far_ref[...]


def diagonal_kernel(own_ref, corner_ref, below_ref, beside_ref, table_ref, matrix_ref, r_ref, ionic_ref, label_ref, coarse_ref,
                    sigma_ref, diagonal_ref, scaled_ref, message_ref, near_ref, far_ref,
                    total_ref, both_ref):
    sigma_ref[0:1, :] = conductance(corner_ref[3:4, :], table_ref)
    sigma_ref[1:3, :] = conductance(below_ref[...], table_ref)
    for i in range(2):
        sigma_ref[3 + 3 * i : 4 + 3 * i, :] = conductance(beside_ref[i : i + 1, :], table_ref)
        sigma_ref[4 + 3 * i : 6 + 3 * i, :] = own_ref[2 * i : 2 * i + 2, :]
    square = (64, 64)
    eye = lax.broadcasted_iota(jnp.int32, square, 0) == lax.broadcasted_iota(jnp.int32, square, 1)
    corner = jnp.sum(jnp.where(eye, matrix_ref[...], 0.0), axis=1, keepdims=True)
    assemble(lambda e: corner * sigma_ref[e : e + 1, :], 6, total_ref)
    labels = label_ref[...]
    diagonal = jnp.where(labels == 0.0, 1.0, total_ref[...] + ionic_ref[...])
    diagonal_ref[...] = diagonal
    even = lanes((8, 128)) % 2 == 0
    message = jnp.where(even, coarse_ref[...], SHARE * restrict(diagonal, labels))
    message_ref[...] = jnp.broadcast_to(message[None], message_ref.shape)
    scaled_ref[...] = r_ref[...] / diagonal
    both_ref[...] = jnp.zeros_like(both_ref)
    for n in range(18):
        both_ref[0, 3 * n : 3 * n + 3, :] = scaled_ref[n, 3:6, :]
        both_ref[0, 56 + 3 * n : 59 + 3 * n, :] = label_ref[n, 3:6, :]
        both_ref[1, 4 * n : 4 * n + 4, :] = scaled_ref[n, 0:4, :]
        both_ref[1, 72 + 4 * n : 76 + 4 * n, :] = label_ref[n, 0:4, :]
        both_ref[1, 144 + n : 145 + n, :] = ionic_ref[n, 0:1, :]
        both_ref[1, 162 + n : 163 + n, :] = diagonal_ref[n, 0:1, :]
    both_ref[1, 180:183, :] = sigma_ref[3:6, :]
    send(parity("slab"), both_ref, near_ref, far_ref)


def halved(coarse):
    return jnp.where(lanes((4, 128)) % 2 == 0, coarse[0:4], coarse[4:8])


def restored(tiles):
    return jnp.concatenate([even_part(tiles), odd_part(tiles)], tiles.ndim - 2)


def along(values):
    lane = lanes(values.shape)
    row = lax.broadcasted_iota(jnp.int32, values.shape, 1)
    after = pltpu.roll(values, 7, 1)
    carried = jnp.where(lane < 126, pltpu.roll(after, 126, 2), 0.0)
    after = jnp.where(row == 7, carried, after)
    before = pltpu.roll(values, 1, 1)
    carried = jnp.where(lane >= 2, pltpu.roll(before, 2, 2), 0.0)
    return after + jnp.where(row == 0, carried, before)


def smooth(start, valid):
    level = start
    for sweep in range(REACH):
        beside = level[2:] + level[:-2] + along(level[1:-1])
        here = slice(sweep + 1, 2 * NEAR - sweep)
        level = start[here] + (1.0 - DAMPING) * level[1:-1] + (DAMPING * COUPLING) * beside
        level = level * valid[here]
    return level


def around(count):
    rows, valid = [], []
    for step in range(-NEAR, NEAR + 1):
        row = lax.axis_index("slab") + step
        inside = jnp.logical_and(row >= 0, row < count)
        rows.append(jnp.clip(row, 0, count - 1))
        valid.append(jnp.where(inside, jnp.ones((1, 8, 128), F32), 0.0))
    return rows, jnp.concatenate(valid, 0)


def even_part(tiles):
    even = lanes(tiles.shape) % 2 == 0
    return jnp.where(even, tiles, pltpu.roll(tiles, 1, tiles.ndim - 1))


def odd_part(tiles):
    even = lanes(tiles.shape) % 2 == 0
    return jnp.where(even, pltpu.roll(tiles, 127, tiles.ndim - 1), tiles)


def widen(field_ref, both_ref, up_start, down_start, wide_ref):
    wide_ref[...] = jnp.zeros_like(wide_ref)
    for n in range(18):
        wide_ref[n, 0:3, :] = both_ref[1, up_start + 3 * n : up_start + 3 * n + 3, :]
        wide_ref[n, 3:9, :] = field_ref[n, 0:6, :]
        wide_ref[n, 9:13, :] = both_ref[0, down_start + 4 * n : down_start + 4 * n + 4, :]


def send_cross(odd, width, wide_ref, own_ref, near_ref, far_ref, both_ref):
    own_ref[...] = jnp.zeros_like(own_ref)
    for n in range(18):
        own_ref[n, 0:6, :] = wide_ref[n, 3:9, :]
    both_ref[...] = jnp.zeros_like(both_ref)
    for c in range(3):
        for y in range(3):
            row = (3 * c + y) * width
            both_ref[0, row : row + width, :] = wide_ref[6 * c + 3 + y, 0:width, :]
        both_ref[1, width * c : width * c + width, :] = wide_ref[6 * c, 0:width, :]
    send(odd, both_ref, near_ref, far_ref)


def first_solve_kernel(gathered_ref, scaled_ref, label_ref, left_ref, right_ref,
                       wide_ref, z_ref, near_ref, far_ref, scale_ref, wide_label_ref, edge_ref, slab_ref, cross_ref):
    receive(parity("slab"), right_ref, left_ref, slab_ref)
    rows, valid = around(gathered_ref.shape[0])
    tiles = jnp.concatenate([gathered_ref[pl.ds(row, 1)] for row in rows], 0)
    sums = jnp.sum(gathered_ref[...], axis=0)
    inverse = valid / jnp.sqrt(odd_part(tiles))
    share = 1.0 / odd_part(sums)
    scale_ref[0 : 2 * NEAR + 1] = inverse
    scale_ref[2 * NEAR + 1] = share
    level = smooth(DAMPING * even_part(tiles) * inverse, valid)
    coarse = level * inverse[REACH : REACH + 3] + (even_part(sums) * share)[None]
    edge_ref[...] = slab_ref[0, 144:184, :]
    widen(label_ref, slab_ref, 56, 72, wide_label_ref)
    widen(scaled_ref, slab_ref, 0, 0, wide_ref)
    wide_ref[...] += prolong(coarse, wide_label_ref[...])
    send_cross(parity("cross"), 13, wide_ref, z_ref, near_ref, far_ref, cross_ref)


def next_solve_kernel(gathered_ref, scaled_ref, wide_label_ref, low_ref, scale_ref,
                      wide_ref, w_ref, near_ref, far_ref, cross_ref):
    rows, valid = around(gathered_ref.shape[0])
    tiles = jnp.concatenate([gathered_ref[pl.ds(row, 1)] for row in rows], 0)
    tiles = restored(tiles)
    sums = restored(jnp.sum(gathered_ref[...], axis=0))
    inverse = scale_ref[0 : 2 * NEAR + 1]
    level = smooth(DAMPING * tiles * inverse, valid)
    coarse = level * inverse[REACH : REACH + 3] + (sums * scale_ref[2 * NEAR + 1])[None]
    wide_ref[...] = jnp.zeros_like(wide_ref)
    for n in range(18):
        wide_ref[n, 0:3, :] = low_ref[3 * n : 3 * n + 3, :]
        wide_ref[n, 3:10, :] = scaled_ref[n, 0:7, :]
    wide_ref[...] += prolong(coarse, wide_label_ref[...])
    send_cross(parity("cross"), 10, wide_ref, w_ref, near_ref, far_ref, cross_ref)


def operate(limit, wide_ref, near_ref, far_ref, sigma_ref, matrix_ref, ionic_ref,
            cross_ref, grid_ref, local_ref, product_ref, total_ref):
    columns = range(-1, (limit + 2) // 3)
    width = 3 * len(columns) + 1
    for n in range(18):
        grid_ref[n // 6 * 10 + 3 + n % 6, 0:width, :] = wide_ref[n, 0:width, :]
    receive(parity("cross"), near_ref, far_ref, cross_ref)
    for c in range(3):
        for y in range(3):
            row = (3 * c + y) * width
            grid_ref[10 * c + y, 0:width, :] = cross_ref[1, row : row + width, :]
        grid_ref[10 * c + 9, 0:width, :] = cross_ref[0, width * c : width * c + width, :]
    end = lanes((width, 128)) == 127
    for y in range(10):
        grid_ref[30 + y, 0:width, :] = jnp.where(end, 0.0, pltpu.roll(grid_ref[y, 0:width, :], 127, 1))
    for i in columns:
        for j in SPAN:
            left = ((i + 1) * 3 + j + 1) * 128
            for c in range(4):
                for b in range(4):
                    row = 16 * c + 4 * b
                    n = c * 10 + 3 * (j + 1) + b
                    local_ref[row : row + 4, left : left + 128] = grid_ref[n, 3 * i + 3 : 3 * i + 7, :]
    matrix = matrix_ref[...]
    matrix_high = matrix.astype(BF16)
    matrix_low = (matrix - matrix_high.astype(F32)).astype(BF16)
    local = local_ref[...]
    high = local.astype(BF16)
    low = (local - high.astype(F32)).astype(BF16)
    dot = functools.partial(jnp.dot, preferred_element_type=F32)
    product_ref[...] = dot(matrix_high, high) + (dot(matrix_high, low) + dot(matrix_low, high))
    assemble(lambda e: product_ref[:, 128 * e : 128 * e + 128] * sigma_ref[e : e + 1, :], limit, total_ref)
    for n in range(18):
        total_ref[n, 0:limit, :] += ionic_ref[n, 0:limit, :] * wide_ref[n, 3 : 3 + limit, :]


def first_image_kernel(wide_ref, far_ref, near_ref, sigma_ref, matrix_ref, ionic_ref, diagonal_ref, label_ref, edge_ref,
                       q_ref, scaled_ref, message_ref, up_ref,
                       all_sigma_ref, all_ionic_ref, all_diagonal_ref, *scratch):
    all_sigma_ref[0:9, :] = sigma_ref[...]
    all_sigma_ref[9:12, :] = edge_ref[36:39, :]
    all_ionic_ref[...] = ionic_ref[...]
    all_diagonal_ref[...] = diagonal_ref[...]
    for n in range(18):
        all_ionic_ref[n, 6:7, :] = edge_ref[n : n + 1, :]
        beyond = edge_ref[18 + n : 19 + n, :]
        all_diagonal_ref[n, 6:7, :] = jnp.where(beyond == 0.0, jnp.inf, beyond)
    operate(7, wide_ref, near_ref, far_ref, all_sigma_ref, matrix_ref, all_ionic_ref, *scratch)
    image = scratch[-1][...]
    q_ref[...] = image
    message_ref[...] = jnp.broadcast_to(halved(restrict(image, label_ref[...]))[None], message_ref.shape)
    scaled_ref[...] = image / all_diagonal_ref[...]
    up_ref[...] = jnp.zeros_like(up_ref)
    for n in range(18):
        up_ref[3 * n : 3 * n + 3, :] = scaled_ref[n, 3:6, :]


def next_image_kernel(wide_ref, far_ref, near_ref, sigma_ref, matrix_ref, ionic_ref,
                      w_ref, r_ref, z_ref, q_ref, t_ref, message_ref, *scratch):
    operate(6, wide_ref, near_ref, far_ref, sigma_ref, matrix_ref, ionic_ref, *scratch)
    image = scratch[-1][...]
    t_ref[...] = image
    r, z, q, w = r_ref[...], z_ref[...], q_ref[...], w_ref[...]
    row = jnp.zeros((1, 128), F32)
    for index, (left, right) in enumerate(((r, z), (z, q), (r, w), (q, w), (z, image), (w, image))):
        part = jnp.sum(jnp.sum(left * right, axis=0), axis=0, keepdims=True)
        row = jnp.where(lanes((1, 128)) == index, jnp.sum(part, axis=1, keepdims=True), row)
    message_ref[...] = jnp.broadcast_to(row[None], message_ref.shape)


def finish_kernel(dots_ref, r_ref, z_ref, q_ref, w_ref, t_ref, solution_ref, residual_ref, rows_ref, turned_ref):
    dots = jnp.sum(dots_ref[...], axis=0)
    rz, zq, rw, qw, zt, wt = [dots[:, index : index + 1] for index in range(6)]
    alpha = rz / zq
    rz_next = alpha * (alpha * qw - rw)
    beta = rz_next / rz
    more = 1.0 + beta
    second = rz_next / (more * more * zq - more * alpha * (zt + qw) + alpha * alpha * wt)
    from_z = alpha + second * more
    from_w = second * alpha
    rows_ref[...] = jnp.zeros_like(rows_ref)
    for c in range(3):
        for y in range(6):
            n = 6 * c + y
            answer = from_z * z_ref[n] - from_w * w_ref[n]
            left = r_ref[n] - from_z * q_ref[n] + from_w * t_ref[n]
            rows_ref[6 * y : 6 * y + 6, :] = answer[0:6]
            rows_ref[36 + 6 * y : 42 + 6 * y, :] = left[0:6]
        turned_ref[pl.ds(c, 128, stride=3), :] = rows_ref[...].T
    for piece in range(3):
        back = turned_ref[128 * piece : 128 * piece + 128, :].T
        for y in range(6):
            for x in range(6):
                row = y * 6 + x
                solution_ref[x, y : y + 1, 128 * piece : 128 * piece + 128] = back[row : row + 1]
                residual_ref[x, y : y + 1, 128 * piece : 128 * piece + 128] = back[36 + row : 37 + row]


def body(adjoint_source, potential, element_matrix, region_labels, conductivity, restriction_map):
    n_slab = lax.axis_size("slab")
    n_cross = lax.axis_size("cross")
    columns = [
        [slab * n_cross + cross for slab in (2 * pair, 2 * pair + 1) for cross in range(n_cross)]
        for pair in range(n_slab // 2)
    ]
    planes = [[2 * pair + low for pair in range(n_slab // 2)] for low in range(2)]
    def shifted(value, axis, step):
        count = lax.axis_size(axis)
        pairs = [(source, source + step) for source in range(count) if 0 <= source + step < count]
        return lax.ppermute(value, axis, pairs)

    def gather(copies):
        return lax.all_to_all(copies, "slab", 0, 0, tiled=True)

    field, wide = (18, 8, 128), (18, 16, 128)

    def space(columns, rows):
        return [(2, rows, 128), (40, 16, 128), (64, 384 * columns), (64, 384 * columns), field]

    regions = region_labels + 1
    pairs = [
        (here * n_cross + beside, (here + 1) * n_cross + beside + 1)
        for here in range(n_slab - 1)
        for beside in range(n_cross - 1)
    ]
    corner = lax.ppermute(regions.reshape(4, 128), ("slab", "cross"), pairs)
    below = shifted(regions[1], "slab", 1)
    beside = shifted(regions[:, 1], "cross", 1)
    r, ionic, labels, coarse, own, table = call(
        unpack_kernel, [field] * 3 + [(8, 128), (4, 128), (4, 128)],
        [(128, 384), (384, 128), (6, 6, 384), (6, 6, 384), pltpu.VMEM((6, 6, 384), jnp.int32),
         pltpu.VMEM((2, 2, 128), jnp.int32), pltpu.SMEM((4,), F32), pltpu.SemaphoreType.DMA((5,))],
        adjoint_source, potential, restriction_map, region_labels, conductivity, away=(0, 1, 2, 3, 4),
    )
    sigma, diagonal, scaled, message, near, far = call(
        diagonal_kernel, [(9, 128), field, field, (n_slab, 8, 128), (184, 128), (184, 128)],
        [field, (2, 184, 128)],
        own, corner, below, beside, table, element_matrix, r, ionic, labels, coarse,
    )

    def exchange(near, far, axis):
        count = lax.axis_size(axis)
        far_pairs = [(c, c + 1) for c in range(1, count - 1, 2)]
        far_pairs += [(above, c) for c, above in far_pairs]
        far = lax.ppermute(far, axis, far_pairs)
        return far, lax.ppermute(near, axis, [(c, c ^ 1) for c in range(count)])

    wide_z, z, near, far, scale, wide_labels, edge = call(
        first_solve_kernel, [wide, field, (120, 128), (120, 128), (10, 8, 128), wide, (40, 128)],
        [(2, 184, 128), (2, 120, 128)],
        gather(message), scaled, labels, *exchange(near, far, "slab"),
    )
    q, scaled, message, up = call(
        first_image_kernel, [field, field, (n_slab, 4, 128), (56, 128)],
        [(12, 128), field, field, *space(4, 120)],
        wide_z, *exchange(near, far, "cross"), sigma, element_matrix, ionic, diagonal, labels, edge,
    )
    wide_w, w, near, far = call(
        next_solve_kernel, [wide, field, (96, 128), (96, 128)], [(2, 96, 128)],
        gather(message), scaled, wide_labels, shifted(up, "slab", 1), scale,
    )
    t, message = call(
        next_image_kernel, [field, (n_slab // 2, 1, 128)], space(3, 96),
        wide_w, *exchange(near, far, "cross"), sigma, element_matrix, ionic, w, r, z, q,
    )
    parts = lax.all_to_all(message, "slab", 0, 0, axis_index_groups=planes, tiled=True)
    parts = jnp.broadcast_to(jnp.sum(parts, 0)[None], (2 * n_cross, 1, 128))
    dots = lax.all_to_all(parts, ("slab", "cross"), 0, 0, axis_index_groups=columns, tiled=True)
    return tuple(call(finish_kernel, [(6, 6, 384)] * 2, [(128, 128), (384, 128)], dots, r, z, q, w, t))


def solution(mesh):
    return jax.shard_map(
        body,
        mesh=mesh,
        in_specs=(
            P("slab", "cross", None),
            P("slab", "cross", None),
            P(),
            P("slab", "cross", None),
            P(),
            P("slab", "cross", None),
        ),
        out_specs=(P("slab", "cross", None), P("slab", "cross", None)),
        check_vma=False,
    )
```

```python
import functools

import jax
import jax.numpy as jnp
from jax import lax
from jax.experimental import pallas as pl
from jax.experimental.pallas import tpu as pltpu
from jax.sharding import PartitionSpec as P

LABELS = 8
DAMPING = 0.8
COUPLING = 0.2
SHARE = 0.1
REACH = 3
NEAR = REACH + 1


F32 = jnp.float32
BF16 = jnp.bfloat16
SPAN = (-1, 0, 1)


def parity(axis):
    return lax.rem(lax.axis_index(axis), 2)


def lanes(shape):
    return lax.broadcasted_iota(jnp.int32, shape, len(shape) - 1)


def call(kernel, out_shapes, scratch, *operands, away=()):
    specs = [
        pl.BlockSpec(memory_space=pltpu.HBM if index in away else pltpu.VMEM)
        for index in range(len(operands))
    ]
    operands = [
        pltpu.with_memory_space_constraint(operand, pltpu.HBM) if index in away else operand
        for index, operand in enumerate(operands)
    ]
    return pl.pallas_call(
        kernel,
        out_shape=[jax.ShapeDtypeStruct(shape, F32) for shape in out_shapes],
        in_specs=specs,
        out_specs=[pl.BlockSpec(memory_space=pltpu.VMEM)] * len(out_shapes),
        scratch_shapes=[pltpu.VMEM(shape, F32) if isinstance(shape, tuple) else shape for shape in scratch],
        compiler_params=pltpu.CompilerParams(vmem_limit_bytes=24 << 20),
    )(*operands)


def restrict(field, labels):
    rows = []
    for label in range(LABELS):
        kept = jnp.sum(jnp.where(labels == label + 1.0, field, 0.0), axis=0)
        rows.append(jnp.sum(kept, axis=0, keepdims=True))
    sums = jnp.concatenate(rows, 0)
    even = lanes((8, 128)) % 2 == 0
    return sums + jnp.where(even, pltpu.roll(sums, 127, 1), pltpu.roll(sums, 1, 1))


def prolong(coarse, labels):
    row = lax.broadcasted_iota(jnp.int32, (16, 128), 0)
    field = jnp.zeros_like(labels)
    for label in range(LABELS):
        low, own, high = [coarse[step, label : label + 1, :] for step in range(3)]
        values = jnp.where(row < 3, low, jnp.where(row < 9, own, high))
        field = jnp.where(labels == label + 1.0, values[None], field)
    return field


def assemble(product_of, limit, total_ref):
    total_ref[...] = jnp.zeros_like(total_ref)
    start = lanes((16, 128)) == 0
    for i in range(-1, (limit + 2) // 3):
        low_a, high_a = max(0, -3 * i), min(4, limit - 3 * i)
        for j in SPAN:
            product = product_of((i + 1) * 3 + j + 1)
            last = pltpu.roll(product[48:64], 1, 1)
            pieces = [
                product[0:16] + jnp.where(start, 0.0, last),
                product[16:32],
                product[32:48],
            ]
            for c in range(3):
                for b in range(4):
                    y = 3 * j + b
                    if 0 <= y < 6:
                        x = 3 * i + low_a
                        rows = pieces[c][4 * b + low_a : 4 * b + high_a]
                        total_ref[c * 6 + y, x : x + high_a - low_a, :] += rows


def conductance(region, table_ref):
    value = jnp.zeros(region.shape, F32)
    for index in range(4):
        value = jnp.where(region == index + 1, table_ref[index : index + 1, :], value)
    return value


def unpack_kernel(source_hbm, potential_hbm, map_hbm, region_hbm, table_hbm, r_ref, ionic_ref, label_ref, coarse_ref,
                  own_ref, table_ref,
                  rows_ref, turned_ref, source_ref, potential_ref, map_ref, region_ref, values_ref, sems):
    copies = [
        pltpu.make_async_copy(away, here, sems.at[index])
        for index, (away, here) in enumerate(
            (
                (source_hbm, source_ref),
                (potential_hbm, potential_ref),
                (map_hbm, map_ref),
                (region_hbm, region_ref),
                (table_hbm, values_ref),
            )
        )
    ]
    for copy in copies:
        copy.start()
    rows_ref[...] = jnp.zeros_like(rows_ref)
    for copy in copies:
        copy.wait()
    for index in range(4):
        table_ref[index : index + 1, :] = jnp.full((1, 128), values_ref[index])
    for i in range(2):
        own_ref[2 * i : 2 * i + 2, :] = conductance(region_ref[i] + 1, table_ref)
    for y in range(6):
        for x in range(6):
            row = y * 6 + x
            rows_ref[row : row + 1, :] = source_ref[x, y : y + 1, :]
            rows_ref[36 + row : 37 + row, :] = potential_ref[x, y : y + 1, :]
            rows_ref[72 + row : 73 + row, :] = map_ref[x, y : y + 1, :].astype(F32)
    for piece in range(3):
        turned_ref[128 * piece : 128 * piece + 128, :] = rows_ref[:, 128 * piece : 128 * piece + 128].T
    r_ref[...] = jnp.zeros_like(r_ref)
    ionic_ref[...] = jnp.zeros_like(ionic_ref)
    label_ref[...] = jnp.zeros_like(label_ref)
    for c in range(3):
        split = turned_ref[pl.ds(c, 128, stride=3), :].T
        for y in range(6):
            r_ref[c * 6 + y, 0:6, :] = split[6 * y : 6 * y + 6]
            tangent = jnp.tanh(split[36 + 6 * y : 42 + 6 * y])
            ionic_ref[c * 6 + y, 0:6, :] = 1.0 + 2.0 * (1.0 - tangent * tangent)
            label_ref[c * 6 + y, 0:6, :] = split[72 + 6 * y : 78 + 6 * y] + 1.0
    coarse_ref[...] = restrict(r_ref[...], label_ref[...])


def send(odd, both_ref, near_ref, far_ref):
    near_ref[...] = both_ref[odd]
    far_ref[...] = both_ref[1 - odd]


def receive(odd, near_ref, far_ref, both_ref):
    both_ref[odd] = near_ref[...]
    both_ref[1 - odd] = far_ref[...]


def diagonal_kernel(own_ref, corner_ref, below_ref, beside_ref, table_ref, matrix_ref, r_ref, ionic_ref, label_ref, coarse_ref,
                    sigma_ref, diagonal_ref, scaled_ref, message_ref, near_ref, far_ref,
                    total_ref, both_ref):
    sigma_ref[0:1, :] = conductance(corner_ref[3:4, :], table_ref)
    sigma_ref[1:3, :] = conductance(below_ref[...], table_ref)
    for i in range(2):
        sigma_ref[3 + 3 * i : 4 + 3 * i, :] = conductance(beside_ref[i : i + 1, :], table_ref)
        sigma_ref[4 + 3 * i : 6 + 3 * i, :] = own_ref[2 * i : 2 * i + 2, :]
    square = (64, 64)
    eye = lax.broadcasted_iota(jnp.int32, square, 0) == lax.broadcasted_iota(jnp.int32, square, 1)
    corner = jnp.sum(jnp.where(eye, matrix_ref[...], 0.0), axis=1, keepdims=True)
    assemble(lambda e: corner * sigma_ref[e : e + 1, :], 6, total_ref)
    labels = label_ref[...]
    diagonal = jnp.where(labels == 0.0, 1.0, total_ref[...] + ionic_ref[...])
    diagonal_ref[...] = diagonal
    even = lanes((8, 128)) % 2 == 0
    message = jnp.where(even, coarse_ref[...], SHARE * restrict(diagonal, labels))
    message_ref[...] = jnp.broadcast_to(message[None], message_ref.shape)
    scaled_ref[...] = r_ref[...] / diagonal
    both_ref[...] = jnp.zeros_like(both_ref)
    for n in range(18):
        both_ref[0, 3 * n : 3 * n + 3, :] = scaled_ref[n, 3:6, :]
        both_ref[0, 56 + 3 * n : 59 + 3 * n, :] = label_ref[n, 3:6, :]
        both_ref[1, 4 * n : 4 * n + 4, :] = scaled_ref[n, 0:4, :]
        both_ref[1, 72 + 4 * n : 76 + 4 * n, :] = label_ref[n, 0:4, :]
        both_ref[1, 144 + n : 145 + n, :] = ionic_ref[n, 0:1, :]
        both_ref[1, 162 + n : 163 + n, :] = diagonal_ref[n, 0:1, :]
    both_ref[1, 180:183, :] = sigma_ref[3:6, :]
    send(parity("slab"), both_ref, near_ref, far_ref)


def halved(coarse):
    return jnp.where(lanes((4, 128)) % 2 == 0, coarse[0:4], coarse[4:8])


def restored(tiles):
    return jnp.concatenate([even_part(tiles), odd_part(tiles)], tiles.ndim - 2)


def along(values):
    lane = lanes(values.shape)
    row = lax.broadcasted_iota(jnp.int32, values.shape, 1)
    after = pltpu.roll(values, 7, 1)
    carried = jnp.where(lane < 126, pltpu.roll(after, 126, 2), 0.0)
    after = jnp.where(row == 7, carried, after)
    before = pltpu.roll(values, 1, 1)
    carried = jnp.where(lane >= 2, pltpu.roll(before, 2, 2), 0.0)
    return after + jnp.where(row == 0, carried, before)


def smooth(start, valid):
    level = start
    for sweep in range(REACH):
        beside = level[2:] + level[:-2] + along(level[1:-1])
        here = slice(sweep + 1, 2 * NEAR - sweep)
        level = start[here] + (1.0 - DAMPING) * level[1:-1] + (DAMPING * COUPLING) * beside
        level = level * valid[here]
    return level


def around(count):
    rows, valid = [], []
    for step in range(-NEAR, NEAR + 1):
        row = lax.axis_index("slab") + step
        inside = jnp.logical_and(row >= 0, row < count)
        rows.append(jnp.clip(row, 0, count - 1))
        valid.append(jnp.where(inside, jnp.ones((1, 8, 128), F32), 0.0))
    return rows, jnp.concatenate(valid, 0)


def even_part(tiles):
    even = lanes(tiles.shape) % 2 == 0
    return jnp.where(even, tiles, pltpu.roll(tiles, 1, tiles.ndim - 1))


def odd_part(tiles):
    even = lanes(tiles.shape) % 2 == 0
    return jnp.where(even, pltpu.roll(tiles, 127, tiles.ndim - 1), tiles)


def widen(field_ref, both_ref, up_start, down_start, wide_ref):
    wide_ref[...] = jnp.zeros_like(wide_ref)
    for n in range(18):
        wide_ref[n, 0:3, :] = both_ref[1, up_start + 3 * n : up_start + 3 * n + 3, :]
        wide_ref[n, 3:9, :] = field_ref[n, 0:6, :]
        wide_ref[n, 9:13, :] = both_ref[0, down_start + 4 * n : down_start + 4 * n + 4, :]


def send_cross(odd, width, wide_ref, own_ref, near_ref, far_ref, both_ref):
    own_ref[...] = jnp.zeros_like(own_ref)
    for n in range(18):
        own_ref[n, 0:6, :] = wide_ref[n, 3:9, :]
    both_ref[...] = jnp.zeros_like(both_ref)
    for c in range(3):
        for y in range(3):
            row = (3 * c + y) * width
            both_ref[0, row : row + width, :] = wide_ref[6 * c + 3 + y, 0:width, :]
        both_ref[1, width * c : width * c + width, :] = wide_ref[6 * c, 0:width, :]
    send(odd, both_ref, near_ref, far_ref)


def first_solve_kernel(gathered_ref, scaled_ref, label_ref, left_ref, right_ref,
                       wide_ref, z_ref, near_ref, far_ref, scale_ref, wide_label_ref, edge_ref, slab_ref, cross_ref):
    receive(parity("slab"), right_ref, left_ref, slab_ref)
    rows, valid = around(gathered_ref.shape[0])
    tiles = jnp.concatenate([gathered_ref[pl.ds(row, 1)] for row in rows], 0)
    sums = jnp.sum(gathered_ref[...], axis=0)
    inverse = valid / jnp.sqrt(odd_part(tiles))
    share = 1.0 / odd_part(sums)
    scale_ref[0 : 2 * NEAR + 1] = inverse
    scale_ref[2 * NEAR + 1] = share
    level = smooth(DAMPING * even_part(tiles) * inverse, valid)
    coarse = level * inverse[REACH : REACH + 3] + (even_part(sums) * share)[None]
    edge_ref[...] = slab_ref[0, 144:184, :]
    widen(label_ref, slab_ref, 56, 72, wide_label_ref)
    widen(scaled_ref, slab_ref, 0, 0, wide_ref)
    wide_ref[...] += prolong(coarse, wide_label_ref[...])
    send_cross(parity("cross"), 13, wide_ref, z_ref, near_ref, far_ref, cross_ref)


def next_solve_kernel(gathered_ref, scaled_ref, wide_label_ref, low_ref, scale_ref,
                      wide_ref, w_ref, near_ref, far_ref, cross_ref):
    rows, valid = around(gathered_ref.shape[0])
    tiles = jnp.concatenate([gathered_ref[pl.ds(row, 1)] for row in rows], 0)
    tiles = restored(tiles)
    sums = restored(jnp.sum(gathered_ref[...], axis=0))
    inverse = scale_ref[0 : 2 * NEAR + 1]
    level = smooth(DAMPING * tiles * inverse, valid)
    coarse = level * inverse[REACH : REACH + 3] + (sums * scale_ref[2 * NEAR + 1])[None]
    wide_ref[...] = jnp.zeros_like(wide_ref)
    for n in range(18):
        wide_ref[n, 0:3, :] = low_ref[3 * n : 3 * n + 3, :]
        wide_ref[n, 3:10, :] = scaled_ref[n, 0:7, :]
    wide_ref[...] += prolong(coarse, wide_label_ref[...])
    send_cross(parity("cross"), 10, wide_ref, w_ref, near_ref, far_ref, cross_ref)


def operate(limit, wide_ref, near_ref, far_ref, sigma_ref, matrix_ref, ionic_ref,
            cross_ref, grid_ref, local_ref, product_ref, total_ref):
    columns = range(-1, (limit + 2) // 3)
    width = 3 * len(columns) + 1
    for n in range(18):
        grid_ref[n // 6 * 10 + 3 + n % 6, 0:width, :] = wide_ref[n, 0:width, :]
    receive(parity("cross"), near_ref, far_ref, cross_ref)
    for c in range(3):
        for y in range(3):
            row = (3 * c + y) * width
            grid_ref[10 * c + y, 0:width, :] = cross_ref[1, row : row + width, :]
        grid_ref[10 * c + 9, 0:width, :] = cross_ref[0, width * c : width * c + width, :]
    end = lanes((width, 128)) == 127
    for y in range(10):
        grid_ref[30 + y, 0:width, :] = jnp.where(end, 0.0, pltpu.roll(grid_ref[y, 0:width, :], 127, 1))
    for i in columns:
        for j in SPAN:
            left = ((i + 1) * 3 + j + 1) * 128
            for c in range(4):
                for b in range(4):
                    row = 16 * c + 4 * b
                    n = c * 10 + 3 * (j + 1) + b
                    local_ref[row : row + 4, left : left + 128] = grid_ref[n, 3 * i + 3 : 3 * i + 7, :]
    matrix = matrix_ref[...]
    matrix_high = matrix.astype(BF16)
    matrix_low = (matrix - matrix_high.astype(F32)).astype(BF16)
    local = local_ref[...]
    high = local.astype(BF16)
    low = (local - high.astype(F32)).astype(BF16)
    dot = functools.partial(jnp.dot, preferred_element_type=F32)
    product_ref[...] = dot(matrix_high, high) + (dot(matrix_high, low) + dot(matrix_low, high))
    assemble(lambda e: product_ref[:, 128 * e : 128 * e + 128] * sigma_ref[e : e + 1, :], limit, total_ref)
    for n in range(18):
        total_ref[n, 0:limit, :] += ionic_ref[n, 0:limit, :] * wide_ref[n, 3 : 3 + limit, :]


def first_image_kernel(wide_ref, far_ref, near_ref, sigma_ref, matrix_ref, ionic_ref, diagonal_ref, label_ref, edge_ref,
                       q_ref, scaled_ref, message_ref, up_ref,
                       all_sigma_ref, all_ionic_ref, all_diagonal_ref, *scratch):
    all_sigma_ref[0:9, :] = sigma_ref[...]
    all_sigma_ref[9:12, :] = edge_ref[36:39, :]
    all_ionic_ref[...] = ionic_ref[...]
    all_diagonal_ref[...] = diagonal_ref[...]
    for n in range(18):
        all_ionic_ref[n, 6:7, :] = edge_ref[n : n + 1, :]
        beyond = edge_ref[18 + n : 19 + n, :]
        all_diagonal_ref[n, 6:7, :] = jnp.where(beyond == 0.0, jnp.inf, beyond)
    operate(7, wide_ref, near_ref, far_ref, all_sigma_ref, matrix_ref, all_ionic_ref, *scratch)
    image = scratch[-1][...]
    q_ref[...] = image
    message_ref[...] = jnp.broadcast_to(halved(restrict(image, label_ref[...]))[None], message_ref.shape)
    scaled_ref[...] = image / all_diagonal_ref[...]
    up_ref[...] = jnp.zeros_like(up_ref)
    for n in range(18):
        up_ref[3 * n : 3 * n + 3, :] = scaled_ref[n, 3:6, :]


def next_image_kernel(wide_ref, far_ref, near_ref, sigma_ref, matrix_ref, ionic_ref,
                      w_ref, r_ref, z_ref, q_ref, t_ref, message_ref, *scratch):
    operate(6, wide_ref, near_ref, far_ref, sigma_ref, matrix_ref, ionic_ref, *scratch)
    image = scratch[-1][...]
    t_ref[...] = image
    r, z, q, w = r_ref[...], z_ref[...], q_ref[...], w_ref[...]
    row = jnp.zeros((1, 128), F32)
    for index, (left, right) in enumerate(((r, z), (z, q), (r, w), (q, w), (z, image), (w, image))):
        part = jnp.sum(jnp.sum(left * right, axis=0), axis=0, keepdims=True)
        row = jnp.where(lanes((1, 128)) == index, jnp.sum(part, axis=1, keepdims=True), row)
    message_ref[...] = jnp.broadcast_to(row[None], message_ref.shape)


def finish_kernel(dots_ref, r_ref, z_ref, q_ref, w_ref, t_ref, solution_ref, residual_ref, rows_ref, turned_ref):
    dots = jnp.sum(dots_ref[...], axis=0)
    rz, zq, rw, qw, zt, wt = [dots[:, index : index + 1] for index in range(6)]
    alpha = rz / zq
    rz_next = alpha * (alpha * qw - rw)
    beta = rz_next / rz
    more = 1.0 + beta
    second = rz_next / (more * more * zq - more * alpha * (zt + qw) + alpha * alpha * wt)
    from_z = alpha + second * more
    from_w = second * alpha
    rows_ref[...] = jnp.zeros_like(rows_ref)
    for c in range(3):
        for y in range(6):
            n = 6 * c + y
            answer = from_z * z_ref[n] - from_w * w_ref[n]
            left = r_ref[n] - from_z * q_ref[n] + from_w * t_ref[n]
            rows_ref[6 * y : 6 * y + 6, :] = answer[0:6]
            rows_ref[36 + 6 * y : 42 + 6 * y, :] = left[0:6]
        turned_ref[pl.ds(c, 128, stride=3), :] = rows_ref[...].T
    for piece in range(3):
        back = turned_ref[128 * piece : 128 * piece + 128, :].T
        for y in range(6):
            for x in range(6):
                row = y * 6 + x
                solution_ref[x, y : y + 1, 128 * piece : 128 * piece + 128] = back[row : row + 1]
                residual_ref[x, y : y + 1, 128 * piece : 128 * piece + 128] = back[36 + row : 37 + row]


def body(adjoint_source, potential, element_matrix, region_labels, conductivity, restriction_map):
    n_slab = lax.axis_size("slab")
    n_cross = lax.axis_size("cross")
    columns = [
        [slab * n_cross + cross for slab in (2 * pair, 2 * pair + 1) for cross in range(n_cross)]
        for pair in range(n_slab // 2)
    ]
    planes = [[2 * pair + low for pair in range(n_slab // 2)] for low in range(2)]
    def shifted(value, axis, step):
        count = lax.axis_size(axis)
        pairs = [(source, source + step) for source in range(count) if 0 <= source + step < count]
        return lax.ppermute(value, axis, pairs)

    def gather(copies):
        return lax.all_to_all(copies, "slab", 0, 0, tiled=True)

    field, wide = (18, 8, 128), (18, 16, 128)

    def space(columns, rows):
        return [(2, rows, 128), (40, 16, 128), (64, 384 * columns), (64, 384 * columns), field]

    regions = region_labels + 1
    pairs = [
        (here * n_cross + beside, (here + 1) * n_cross + beside + 1)
        for here in range(n_slab - 1)
        for beside in range(n_cross - 1)
    ]
    corner = lax.ppermute(regions.reshape(4, 128), ("slab", "cross"), pairs)
    below = shifted(regions[1], "slab", 1)
    beside = shifted(regions[:, 1], "cross", 1)
    r, ionic, labels, coarse, own, table = call(
        unpack_kernel, [field] * 3 + [(8, 128), (4, 128), (4, 128)],
        [(128, 384), (384, 128), (6, 6, 384), (6, 6, 384), pltpu.VMEM((6, 6, 384), jnp.int32),
         pltpu.VMEM((2, 2, 128), jnp.int32), pltpu.SMEM((4,), F32), pltpu.SemaphoreType.DMA((5,))],
        adjoint_source, potential, restriction_map, region_labels, conductivity, away=(0, 1, 2, 3, 4),
    )
    sigma, diagonal, scaled, message, near, far = call(
        diagonal_kernel, [(9, 128), field, field, (n_slab, 8, 128), (184, 128), (184, 128)],
        [field, (2, 184, 128)],
        own, corner, below, beside, table, element_matrix, r, ionic, labels, coarse,
    )

    def exchange(near, far, axis):
        count = lax.axis_size(axis)
        far_pairs = [(c, c + 1) for c in range(1, count - 1, 2)]
        far_pairs += [(above, c) for c, above in far_pairs]
        far = lax.ppermute(far, axis, far_pairs)
        return far, lax.ppermute(near, axis, [(c, c ^ 1) for c in range(count)])

    wide_z, z, near, far, scale, wide_labels, edge = call(
        first_solve_kernel, [wide, field, (120, 128), (120, 128), (10, 8, 128), wide, (40, 128)],
        [(2, 184, 128), (2, 120, 128)],
        gather(message), scaled, labels, *exchange(near, far, "slab"),
    )
    q, scaled, message, up = call(
        first_image_kernel, [field, field, (n_slab, 4, 128), (56, 128)],
        [(12, 128), field, field, *space(4, 120)],
        wide_z, *exchange(near, far, "cross"), sigma, element_matrix, ionic, diagonal, labels, edge,
    )
    wide_w, w, near, far = call(
        next_solve_kernel, [wide, field, (96, 128), (96, 128)], [(2, 96, 128)],
        gather(message), scaled, wide_labels, shifted(up, "slab", 1), scale,
    )
    t, message = call(
        next_image_kernel, [field, (2 * n_cross, 1, 128)], space(3, 96),
        wide_w, *exchange(near, far, "cross"), sigma, element_matrix, ionic, w, r, z, q,
    )
    parts = lax.all_to_all(message, ("slab", "cross"), 0, 0, axis_index_groups=columns, tiled=True)
    parts = jnp.broadcast_to(jnp.sum(parts, 0)[None], (n_slab // 2, 1, 128))
    dots = lax.all_to_all(parts, "slab", 0, 0, axis_index_groups=planes, tiled=True)
    return tuple(call(finish_kernel, [(6, 6, 384)] * 2, [(128, 128), (384, 128)], dots, r, z, q, w, t))


def solution(mesh):
    return jax.shard_map(
        body,
        mesh=mesh,
        in_specs=(
            P("slab", "cross", None),
            P("slab", "cross", None),
            P(),
            P("slab", "cross", None),
            P(),
            P("slab", "cross", None),
        ),
        out_specs=(P("slab", "cross", None), P("slab", "cross", None)),
        check_vma=False,
    )
```
